32 devices in a mesh: groups: 1, dp: 4 (over y, x), tensor: 8 (over z, core).
Axes of the slice: x: 2, y: 2, z: 4, core: 2. Of those that a mesh axis runs over, the one named last changes fastest.
Arguments:
- tokens: bfloat16 [512, 4096], P(('groups', 'dp', 'tensor')), may hold values from -6 to 6
- grad_out: bfloat16 [512, 4096], P(('groups', 'dp', 'tensor')), may hold values from -1.5 to 1.5
- gate_weight: bfloat16 [4096, 16384], P('dp', 'tensor'), may hold values from -0.09375 to 0.09375
- up_weight: bfloat16 [4096, 16384], P('dp', 'tensor'), may hold values from -0.09375 to 0.09375
- down_weight: bfloat16 [16384, 4096], P('tensor', 'dp'), may hold values from -0.09375 to 0.09375
- block_kind: int32 [160], P('tensor'), may hold values from 0 to 2
- block_ff: int32 [160], P('tensor'), may hold values from 0 to 15
- block_d: int32 [160], P('tensor'), may hold values from 0 to 31
- block_owner: int32 [160, 1], P('tensor'), may hold values from 0 to 3; in each aligned block of 20 rows (0 to 19, 20 to 39, ...) at most 5 rows name the same one
Outputs:
- grad_tokens: bfloat16 [512, 4096], P(('groups', 'dp', 'tensor'))
- delta_grads: float32 [160, 128, 128], P(('groups', 'dp', 'tensor'))
The draws below stay inside these ranges and needn't reach their ends.
Inputs may be any that keep to these rules, and one draw needn't show every extreme that they name: `block_owner`: among the 20 entries of one index of tensor no owner appears more than 5 times, and some owner appears exactly 5 times.
All inputs are finite; a program needn't handle non-finite values.
Results may differ from the reference program's by a relative error of at most 0.0095.
Values may be sent and summed in bfloat16 or wider, within the bound.
No kernel may reach another device: no remote copies, remote signals or barrier semaphores. Data moves between devices by JAX's collectives and lax.ppermute only.
A program may use at most 192 MiB of HBM per device.

```python
import math
import jax
import jax.numpy as jnp
import numpy as np
from jax import lax

D = 4096
FF = 16384
BLOCK = 128
KB = 20
CAP = 5
TOKENS = 512
LIST = 160
SLOTS = 160
N_DP = 4
N_TENSOR = 8


def plant(array, key, smallest, top_value):
    shape = array.shape
    spot = [jax.random.randint(jax.random.fold_in(key, axis), (), 0, shape[axis]) for axis in range(len(shape))]
    array = array.at[tuple(spot)].set(smallest)
    longest = shape.index(max(shape))
    spot[longest] = (spot[longest] + 1) % shape[longest]
    return array.at[tuple(spot)].set(top_value)


def block_levels(stream_key, extent, pieces, least, top_value):
    gain, own = 1.0, jax.random.fold_in(stream_key, 6)
    for dim, blocks in pieces:
        draws = jnp.exp(jax.random.uniform(jax.random.fold_in(own, dim), (blocks,), jnp.float32, least / len(pieces), top_value / len(pieces)))
        gain = gain * jnp.repeat(draws, extent[dim] // blocks).reshape([-1 if axis == dim else 1 for axis in range(len(extent))])
    return gain


def deal_out(key, own, number, rows, count, top, limit, lean):
    ranking = jax.random.permutation(key, count)
    heavy_load, common = load_shares(count, rows * top, limit, lean, True), load_shares(count, rows * top, limit, lean, False)
    places = jnp.arange(count)

    def named(sizes, turn):
        used = int((sizes > 0).sum())
        fixed = max(1, used // 4)
        passed = fixed + (places - fixed + turn * (used - fixed)) % max(1, count - fixed)
        return jnp.zeros((count,), jnp.int32).at[ranking[jnp.where(places < fixed, places, passed)]].set(jnp.asarray(sizes, jnp.int32))

    sizes = jnp.where(number % 4 == 0, named(heavy_load, number // 4), named(common, number - number // 4 - 1))
    mixed = jax.random.permutation(jax.random.fold_in(own, 3), count)
    donor, receiver = mixed[0:count // 2 * 2:2], mixed[1:count // 2 * 2:2]
    room = jnp.minimum(sizes[donor] - 1, limit - sizes[receiver]) // 2
    room = jnp.where((donor == ranking[0]) | (receiver == ranking[0]) | (sizes[receiver] == 0), 0, jnp.maximum(room, 0))
    passed = jax.random.randint(jax.random.fold_in(own, 4), (count // 2,), 0, 1 << 20) % (room + 1)
    sizes = sizes.at[donor].add(-passed).at[receiver].add(passed)
    items = jnp.searchsorted(jnp.cumsum(sizes), jnp.arange(rows * top), side="right").astype(jnp.int32)
    grid = items.reshape(top, rows).T
    grid = grid[jax.random.permutation(jax.random.fold_in(own, 1), rows)]
    turn = jax.random.randint(jax.random.fold_in(own, 2), (rows, 1), 0, top)
    return jnp.take_along_axis(grid, (jnp.arange(top)[None, :] + turn) % top, axis=1)


def load_shares(amount, total, reach, slope, full):
    loads = [(1 << 20) // math.isqrt(standing ** slope) + 1 for standing in range(1, amount + 1)]
    largest = reach if full else min(reach, max(-(-total // amount), total * loads[0] // sum(loads)))
    least = 1 if total - largest >= amount - 1 else 0
    given, surplus = [largest] + [least] * (amount - 1), total - largest - least * (amount - 1)
    while surplus > 0:
        movable = [i for i in range(1, amount) if given[i] < largest] or [i for i in range(1, amount) if given[i] < reach]
        pool, budget = sum([loads[i] for i in movable]), surplus
        for i in movable:
            more = min(reach - given[i], max(1, budget * loads[i] // pool), surplus)
            given[i] = given[i] + more
            surplus = surplus - more
    return np.array(given)


def noise(own_key, dims, width, reach, pieces=(), held_as=jnp.bfloat16):
    factor_of = block_levels(own_key, dims, pieces, -0.22, 0.18) if pieces else 1.0
    drawn = jax.random.normal(own_key, dims, jnp.float32) * width * factor_of
    return jnp.minimum(jnp.maximum(drawn, -reach), reach).astype(held_as)


def setup_inputs(seed: int = 0, part: int = 0) -> dict:
    arg_keys = jax.random.split(jax.random.key(seed), 10)
    part_keys = jax.random.split(jax.random.fold_in(arg_keys[9], part), 10)
    tokens = noise(part_keys[0], (TOKENS, D), 1.0, 6.0, ((0, 32),))
    grad_out = noise(part_keys[1], (TOKENS, D), 0.25, 1.5, ((0, 32),))
    gate_weight = noise(arg_keys[2], (D, FF), D ** -0.5, 0.09375, ((0, 4), (1, 8)))
    up_weight = noise(arg_keys[3], (D, FF), D ** -0.5, 0.09375, ((0, 4), (1, 8)))
    down_weight = noise(arg_keys[4], (FF, D), D ** -0.5, 0.09375, ((0, 8), (1, 4)))
    block_kind = plant(jax.random.randint(arg_keys[5], (LIST,), 0, 3), jax.random.fold_in(arg_keys[5], 1), 0, 2).astype(jnp.int32)
    block_ff = plant(jax.random.randint(arg_keys[6], (LIST,), 0, FF // (BLOCK * N_TENSOR)), jax.random.fold_in(arg_keys[6], 1), 0, (FF // (BLOCK * N_TENSOR)) - 1).astype(jnp.int32)
    block_d = plant(jax.random.randint(arg_keys[7], (LIST,), 0, D // BLOCK), jax.random.fold_in(arg_keys[7], 1), 0, (D // BLOCK) - 1).astype(jnp.int32)
    block_owner_keys = jax.random.split(jax.random.fold_in(arg_keys[8], 1), LIST // KB)
    block_owner_turns = jax.random.permutation(jax.random.fold_in(arg_keys[8], 3), LIST // KB)
    block_owner = jax.vmap(lambda own, number: deal_out(jax.random.fold_in(arg_keys[8], 2), own, number, KB, N_DP, 1, CAP, 2))(block_owner_keys, block_owner_turns).reshape((LIST, 1))
    return {"tokens": tokens, "grad_out": grad_out, "gate_weight": gate_weight, "up_weight": up_weight, "down_weight": down_weight, "block_kind": block_kind, "block_ff": block_ff, "block_d": block_d, "block_owner": block_owner}


def pick_blocks(source, indices):
    row_total = source.shape[0]
    return jnp.take(source.reshape(row_total, source.shape[1] // BLOCK, BLOCK), indices, axis=1)


def reference(tokens, grad_out, gate_weight, up_weight, down_weight, block_kind, block_ff, block_d, block_owner):
    contract = (((1,), (1,)), ((), ()))
    gate_proj = jnp.dot(tokens, gate_weight, preferred_element_type=jnp.float32)
    upward = jnp.dot(tokens, up_weight, preferred_element_type=jnp.float32)
    sigmoid_gate = jax.nn.sigmoid(gate_proj)
    silu_gate = gate_proj * sigmoid_gate
    hidden = (silu_gate * upward).astype(jnp.bfloat16)
    hidden_grad = lax.dot_general(grad_out, down_weight, contract, preferred_element_type=jnp.float32)
    gate_grad = (hidden_grad * upward * sigmoid_gate * (1.0 + gate_proj * (1.0 - sigmoid_gate))).astype(jnp.bfloat16)
    up_grad = (hidden_grad * silu_gate).astype(jnp.bfloat16)
    token_sum = lax.dot_general(gate_grad, gate_weight, contract, preferred_element_type=jnp.float32)
    token_sum = token_sum + lax.dot_general(up_grad, up_weight, contract, preferred_element_type=jnp.float32)
    grad_tokens = token_sum.astype(jnp.bfloat16)
    local_blocks = FF // (BLOCK * N_TENSOR)
    entries = jnp.arange(LIST, dtype=jnp.int32)
    tensor_rank = (entries // KB).astype(jnp.int32)
    global_ff = (tensor_rank * local_blocks + block_ff).astype(jnp.int32)
    kind_mask = block_kind[None, :, None]
    token_cols = pick_blocks(tokens, block_d)
    output_cols = pick_blocks(grad_out, block_d)
    hidden_cols = pick_blocks(hidden, global_ff)
    gate_cols = pick_blocks(gate_grad, global_ff)
    up_cols = pick_blocks(up_grad, global_ff)
    left_cols = jnp.where(kind_mask == 2, hidden_cols, token_cols).astype(jnp.float32)
    right_cols = jnp.where(kind_mask == 0, gate_cols, jnp.where(kind_mask == 1, up_cols, output_cols)).astype(jnp.float32)
    block_grad = jnp.einsum("tka,tkb->kab", left_cols, right_cols)
    owners = block_owner[:, 0]
    earlier_same = (owners[:, None] == owners[None, :]) & (tensor_rank[:, None] == tensor_rank[None, :]) & (entries[None, :] < entries[:, None])
    slot_index = jnp.sum(earlier_same.astype(jnp.int32), axis=1).astype(jnp.int32)
    target = ((owners * N_TENSOR + tensor_rank) * CAP + slot_index).astype(jnp.int32)
    delta_grads = jnp.zeros((SLOTS, BLOCK, BLOCK), jnp.float32).at[target].set(block_grad.astype(jnp.float32))
    return grad_tokens, delta_grads
```

```python
import jax
import jax.numpy as jnp
from jax import lax
from jax.sharding import PartitionSpec as P

BLOCK = 128
CAP = 5
CONTRACT_LAST = (((1,), (1,)), ((), ()))


def xor_perm(size, mask):
    return [(i, i ^ mask) for i in range(size)]


def ring_of(length):
    if length <= 4:
        return list(range(0, length, 2)) + list(range(1, length, 2))[::-1]
    return list(range(length))


def ring_perm(length, shift):
    ring = ring_of(length)
    pairs = []
    for place, z in enumerate(ring):
        target = ring[(place + shift) % length]
        pairs += [(2 * z + core, 2 * target + core) for core in range(2)]
    return pairs


def sum_over_dp(value, order, n_dp, lead=0):
    bits = len(order)
    left = list(range(bits - 1, -1, -1))
    for bit in order:
        axis = lead + left.index(bit)
        keep = lax.index_in_dim(value, 0, axis, keepdims=False)
        send = lax.index_in_dim(value, 1, axis, keepdims=False)
        got = lax.ppermute(send.astype(jnp.bfloat16), "dp", xor_perm(n_dp, 1 << bit))
        value = keep.astype(jnp.float32) + got.astype(jnp.float32)
        left.remove(bit)
    return value


def gather_over_dp(value, order, n_dp):
    have = []
    for bit in order:
        got = lax.ppermute(value, "dp", xor_perm(n_dp, 1 << bit))
        axis = sum(1 for other in have if other > bit)
        value = jnp.stack([value, got], axis=axis)
        have.append(bit)
    return value


def body(
    tokens,
    grad_out,
    gate_weight,
    up_weight,
    down_weight,
    block_kind,
    block_ff,
    block_d,
    block_owner,
):
    n_dp, n_tensor = lax.axis_size("dp"), lax.axis_size("tensor")
    n_z = n_tensor // 2
    bits = n_dp.bit_length() - 1
    rows, features = tokens.shape
    width, units = gate_weight.shape
    me, rank = lax.axis_index("dp"), lax.axis_index("tensor")
    bf16, f32 = jnp.bfloat16, jnp.float32

    both = jnp.stack([grad_out, tokens])
    pieces = []
    for mask in range(n_dp):
        piece = lax.dynamic_slice_in_dim(both, (me ^ mask) * width, width, axis=2)
        if mask:
            piece = lax.ppermute(piece, "dp", xor_perm(n_dp, mask))
        pieces.append(piece)
    mine = jnp.stack(pieces, axis=1)

    shards = {0: mine}
    for distance in range(1, n_z // 2 + 1):
        ahead, behind = shards[distance - 1], shards[-(distance - 1)]
        if 2 * distance == n_z:
            first = lax.ppermute(ahead[0], "tensor", ring_perm(n_z, 1))
            second = lax.ppermute(behind[1], "tensor", ring_perm(n_z, -1))
            shards[distance] = jnp.stack([first, second])
        else:
            shards[distance] = lax.ppermute(ahead, "tensor", ring_perm(n_z, 1))
            shards[-distance] = lax.ppermute(behind, "tensor", ring_perm(n_z, -1))

    window = lax.all_gather(both, "tensor", axis=0, tiled=False)

    parts = min(bits, 2)
    part = units // parts
    orders = [[(q + s) % bits for s in range(bits)] for q in range(parts)]
    kept = []
    total = None
    for distance, shard in shards.items():
        other = lax.ppermute(shard, "tensor", xor_perm(n_tensor, 1))
        chunk = jnp.stack([shard, other], axis=2).reshape(2, n_dp * 2 * rows, width)
        hidden_grad = lax.dot_general(
            chunk[0], down_weight, CONTRACT_LAST, preferred_element_type=f32
        ).astype(bf16)
        gate = jnp.dot(chunk[1], gate_weight, preferred_element_type=f32).astype(bf16)
        upward = jnp.dot(chunk[1], up_weight, preferred_element_type=f32).astype(bf16)
        gathered, hiddens, grads = [], [], []
        for q, order in enumerate(orders):
            cut = slice(q * part, (q + 1) * part)
            partial = jnp.stack([gate[:, cut], upward[:, cut], hidden_grad[:, cut]])
            partial = partial.reshape((3,) + (2,) * bits + (2 * rows, part))
            g, u, h = sum_over_dp(partial, order, n_dp, lead=1)
            sig = jax.nn.sigmoid(g)
            silu = g * sig
            hiddens.append((silu * u).astype(bf16))
            gate_grad = (h * u * sig * (1.0 + g * (1.0 - sig))).astype(bf16)
            up_grad = (h * silu).astype(bf16)
            own = jnp.stack([gate_grad, up_grad])
            grads.append(own)
            full = gather_over_dp(own, order[::-1], n_dp)
            full = full.reshape((n_dp, 2, 2 * rows, part))
            gathered.append(jnp.swapaxes(full, 0, 1).reshape(2, n_dp * 2 * rows, part))
        kept.append((jnp.concatenate(hiddens, axis=1), jnp.concatenate(grads, axis=2)))
        gathered = jnp.concatenate(gathered, axis=2)
        out = lax.dot_general(gathered[0], gate_weight, CONTRACT_LAST, preferred_element_type=f32)
        out = out + lax.dot_general(
            gathered[1], up_weight, CONTRACT_LAST, preferred_element_type=f32
        )
        out = out.reshape(n_dp, 2, rows, width)
        got = lax.ppermute(out[:, 1].astype(bf16), "tensor", xor_perm(n_tensor, 1))
        out = out[:, 0] + got.astype(f32)
        if distance:
            out = lax.ppermute(out.astype(bf16), "tensor", ring_perm(n_z, -distance)).astype(f32)
        total = out if total is None else total + out

    total = total.astype(bf16)
    pieces = [total[0]]
    for mask in range(1, n_dp):
        pieces.append(lax.ppermute(total[mask], "dp", xor_perm(n_dp, mask)))
    pieces = jnp.stack(pieces)
    slots = jnp.arange(n_dp, dtype=jnp.int32)
    grad_tokens = jnp.take(pieces, slots ^ me, axis=0)
    grad_tokens = jnp.swapaxes(grad_tokens, 0, 1).reshape(rows, features)

    ring = jnp.asarray(ring_of(n_z), jnp.int32)
    z, core = rank // 2, rank % 2
    place = jnp.argmax(ring == z).astype(jnp.int32)
    sources = []
    for distance in shards:
        from_z = ring[(place - distance + n_z) % n_z]
        sources += [2 * from_z + core, 2 * from_z + 1 - core]
    window = jnp.take(window, jnp.stack(sources), axis=0)
    window_grads = window[:, 0].reshape(n_tensor * rows, features // BLOCK, BLOCK)
    window_tokens = window[:, 1].reshape(n_tensor * rows, features // BLOCK, BLOCK)
    hidden = jnp.concatenate([item[0] for item in kept]).reshape(-1, units // BLOCK, BLOCK)
    gate_grad = jnp.concatenate([item[1][0] for item in kept]).reshape(-1, units // BLOCK, BLOCK)
    up_grad = jnp.concatenate([item[1][1] for item in kept]).reshape(-1, units // BLOCK, BLOCK)

    owners = block_owner[:, 0]
    entries = jnp.arange(owners.shape[0], dtype=jnp.int32)
    earlier_same = (owners[:, None] == owners[None, :]) & (entries[None, :] < entries[:, None])
    slot_index = jnp.sum(earlier_same.astype(jnp.int32), axis=1)
    target = (owners ^ me) * CAP + slot_index
    match = target[None, :] == jnp.arange(n_dp * CAP, dtype=jnp.int32)[:, None]
    filled = jnp.any(match, axis=1)

    def listed(values):
        return jnp.sum(jnp.where(match, values[None, :], 0), axis=1)

    kind, ff, col = listed(block_kind), listed(block_ff), listed(block_d)
    kind_mask = kind[None, :, None]
    left = jnp.where(
        kind_mask == 2, jnp.take(hidden, ff, axis=1), jnp.take(window_tokens, col, axis=1)
    )
    right = jnp.where(
        kind_mask == 0,
        jnp.take(gate_grad, ff, axis=1),
        jnp.where(
            kind_mask == 1, jnp.take(up_grad, ff, axis=1), jnp.take(window_grads, col, axis=1)
        ),
    )
    partial = jnp.einsum("tka,tkb->kab", left, right, preferred_element_type=f32)
    partial = jnp.where(filled[:, None, None], partial, 0.0)
    partial = partial.reshape((2,) * bits + (CAP, BLOCK, BLOCK))
    delta_grads = sum_over_dp(partial, orders[0], n_dp)
    return (grad_tokens, delta_grads)


def solution(mesh):
    placed = (
        P(("groups", "dp", "tensor"), None),
        P(("groups", "dp", "tensor"), None),
        P("dp", "tensor"),
        P("dp", "tensor"),
        P("tensor", "dp"),
        P("tensor"),
        P("tensor"),
        P("tensor"),
        P("tensor", None),
    )
    return jax.shard_map(
        body,
        mesh=mesh,
        in_specs=placed,
        out_specs=(P(("groups", "dp", "tensor"), None), P(("groups", "dp", "tensor"), None, None)),
        check_vma=False,
    )
```

```python
import functools

import jax
import jax.numpy as jnp
import numpy as np
from jax import lax
from jax.experimental import pallas as pl
from jax.experimental.pallas import tpu as pltpu
from jax.sharding import PartitionSpec as P

BLOCK = 128
CAP = 5
CONTRACT_LAST = (((1,), (1,)), ((), ()))


def xor_perm(size, mask):
    return [(i, i ^ mask) for i in range(size)]


def ring_of(length):
    if length <= 4:
        return list(range(0, length, 2)) + list(range(1, length, 2))[::-1]
    return list(range(length))


def ring_perm(length, shift):
    ring = ring_of(length)
    pairs = []
    for place, z in enumerate(ring):
        target = ring[(place + shift) % length]
        pairs += [(2 * z + core, 2 * target + core) for core in range(2)]
    return pairs


def sum_over_dp(value, order, n_dp, lead=0):
    bits = len(order)
    left = list(range(bits - 1, -1, -1))
    for bit in order:
        axis = lead + left.index(bit)
        keep = lax.index_in_dim(value, 0, axis, keepdims=False)
        send = lax.index_in_dim(value, 1, axis, keepdims=False)
        got = lax.ppermute(send.astype(jnp.bfloat16), "dp", xor_perm(n_dp, 1 << bit))
        value = keep.astype(jnp.float32) + got.astype(jnp.float32)
        left.remove(bit)
    return value


def gather_over_dp(value, order, n_dp):
    have = []
    for bit in order:
        got = lax.ppermute(value, "dp", xor_perm(n_dp, 1 << bit))
        axis = sum(1 for other in have if other > bit)
        value = jnp.stack([value, got], axis=axis)
        have.append(bit)
    return value


def after(value, *others):
    return lax.optimization_barrier((value,) + others)[0]


def chunk_distances(n_z):
    chunks = [(0,)]
    for distance in range(1, n_z // 2 + 1):
        chunks.append((distance,) if 2 * distance == n_z else (distance, -distance))
    return chunks


def source_table(n_z):
    ring = ring_of(n_z)
    table = np.zeros((2 * n_z, 2 * n_z), np.int32)
    for rank in range(2 * n_z):
        place, core = ring.index(rank // 2), rank % 2
        sources = []
        for chunk in chunk_distances(n_z):
            for distance in chunk:
                z = ring[(place - distance) % n_z]
                sources += [2 * z + core, 2 * z + 1 - core]
        table[rank] = sources
    return table


def delta_kernel(
    n_dp,
    me_ref,
    kind_ref,
    ff_ref,
    col_ref,
    owner_ref,
    grads_ref,
    tokens_ref,
    hidden_ref,
    gate_ref,
    up_ref,
    out_ref,
    used_ref,
):
    me = me_ref[0]
    out_ref[...] = jnp.zeros_like(out_ref)
    for owner in range(n_dp):
        used_ref[owner] = 0

    def step(entry, carry):
        owner = owner_ref[entry]
        slot = used_ref[owner]
        used_ref[owner] = slot + 1
        kind = kind_ref[entry]
        units = pl.ds(pl.multiple_of(ff_ref[entry] * BLOCK, BLOCK), BLOCK)
        columns = pl.ds(pl.multiple_of(col_ref[entry] * BLOCK, BLOCK), BLOCK)
        left = jnp.where(kind == 2, hidden_ref[:, units], tokens_ref[:, columns])
        right = jnp.where(
            kind == 0,
            gate_ref[:, units],
            jnp.where(kind == 1, up_ref[:, units], grads_ref[:, columns]),
        )
        out_ref[(owner ^ me) * CAP + slot] = lax.dot_general(
            left, right, (((0,), (0,)), ((), ())), preferred_element_type=jnp.float32
        )
        return carry

    lax.fori_loop(0, kind_ref.shape[0], step, 0)


def window_deltas(n_dp, me, kind, ff, col, owner, grads, tokens, hidden, gate_grad, up_grad):
    smem, vmem = pl.BlockSpec(memory_space=pltpu.SMEM), pl.BlockSpec(memory_space=pltpu.VMEM)
    return pl.pallas_call(
        functools.partial(delta_kernel, n_dp),
        out_shape=jax.ShapeDtypeStruct((n_dp * CAP, BLOCK, BLOCK), jnp.float32),
        in_specs=[smem] * 5 + [vmem] * 5,
        out_specs=vmem,
        scratch_shapes=[pltpu.SMEM((n_dp,), jnp.int32)],
        compiler_params=pltpu.CompilerParams(vmem_limit_bytes=24 << 20),
        cost_estimate=pl.CostEstimate(
            flops=2 * kind.shape[0] * BLOCK * BLOCK * grads.shape[0],
            bytes_accessed=16 << 20,
            transcendentals=0,
        ),
    )(me.reshape(1), kind, ff, col, owner, grads, tokens, hidden, gate_grad, up_grad)


def body(
    tokens,
    grad_out,
    gate_weight,
    up_weight,
    down_weight,
    block_kind,
    block_ff,
    block_d,
    block_owner,
):
    n_dp, n_tensor = lax.axis_size("dp"), lax.axis_size("tensor")
    n_z = n_tensor // 2
    bits = n_dp.bit_length() - 1
    rows, features = tokens.shape
    width, units = gate_weight.shape
    me, rank = lax.axis_index("dp"), lax.axis_index("tensor")
    bf16, f32 = jnp.bfloat16, jnp.float32
    parts = min(bits, 2)
    orders = [[(q + s) % bits for s in range(bits)] for q in range(parts)]

    both = jnp.stack([grad_out, tokens])
    pieces = []
    for mask in range(n_dp):
        piece = lax.dynamic_slice_in_dim(both, (me ^ mask) * width, width, axis=2)
        if mask:
            piece = lax.ppermute(piece, "dp", xor_perm(n_dp, mask))
        pieces.append(piece)
    mine = jnp.stack(pieces, axis=1)

    part = units // parts

    def first_partials(shards):
        other = lax.ppermute(shards, "tensor", xor_perm(n_tensor, 1))
        chunk = jnp.stack([shards, other], axis=3)
        chunk = jnp.swapaxes(chunk, 1, 2).reshape(2, -1, width)
        gate = jnp.dot(chunk[1], gate_weight, preferred_element_type=f32).astype(bf16)
        upward = jnp.dot(chunk[1], up_weight, preferred_element_type=f32).astype(bf16)
        hidden_grad = lax.dot_general(
            chunk[0], down_weight, CONTRACT_LAST, preferred_element_type=f32
        ).astype(bf16)
        partials = []
        for q in range(parts):
            cut = slice(q * part, (q + 1) * part)
            partial = jnp.stack([gate[:, cut], upward[:, cut], hidden_grad[:, cut]])
            partials.append(partial.reshape((3,) + (2,) * bits + (-1, part)))
        return partials

    distances = chunk_distances(n_z)
    held = {0: mine}
    partials = [first_partials(mine[:, None])]
    for chunk in distances[1:]:
        distance = chunk[0]
        ahead, behind = held[distance - 1], held[1 - distance]
        if distance > 1:
            ahead, behind = after(ahead, *partials[distance - 2]), after(behind, *partials[distance - 2])
        if len(chunk) == 1:
            first = lax.ppermute(ahead[0], "tensor", ring_perm(n_z, 1))
            second = lax.ppermute(behind[1], "tensor", ring_perm(n_z, -1))
            shards = jnp.stack([first, second])[:, None]
        else:
            held[distance] = lax.ppermute(ahead, "tensor", ring_perm(n_z, 1))
            held[-distance] = lax.ppermute(behind, "tensor", ring_perm(n_z, -1))
            shards = jnp.stack([held[distance], held[-distance]], axis=1)
        partials.append(first_partials(after(shards, *partials[distance - 1])))

    kept = []
    total = None
    window = None
    for chunk, chunk_partials in zip(distances, partials):
        gathered, hiddens, grads = [], [], []
        for partial, order in zip(chunk_partials, orders):
            g, u, h = sum_over_dp(partial, order, n_dp, lead=1)
            sig = jax.nn.sigmoid(g)
            silu = g * sig
            hiddens.append((silu * u).astype(bf16))
            gate_grad = (h * u * sig * (1.0 + g * (1.0 - sig))).astype(bf16)
            up_grad = (h * silu).astype(bf16)
            own = jnp.stack([gate_grad, up_grad])
            grads.append(own)
            full = gather_over_dp(own, order[::-1], n_dp)
            full = full.reshape((n_dp, 2) + own.shape[1:])
            gathered.append(jnp.swapaxes(full, 0, 1).reshape(2, -1, part))
        if window is None:
            late = after(both, *grads)
            window = lax.all_gather(late, "tensor", axis=0, tiled=False)
        kept.append((jnp.concatenate(hiddens, axis=1), jnp.concatenate(grads, axis=2)))
        gathered = jnp.concatenate(gathered, axis=2)
        out = lax.dot_general(gathered[0], gate_weight, CONTRACT_LAST, preferred_element_type=f32)
        out = out + lax.dot_general(
            gathered[1], up_weight, CONTRACT_LAST, preferred_element_type=f32
        )
        out = out.reshape(n_dp, len(chunk), 2, rows, width)
        got = lax.ppermute(out[:, :, 1].astype(bf16), "tensor", xor_perm(n_tensor, 1))
        out = out[:, :, 0] + got.astype(f32)
        for place, distance in enumerate(chunk):
            term = out[:, place]
            if distance:
                term = lax.ppermute(term.astype(bf16), "tensor", ring_perm(n_z, -distance))
                term = term.astype(f32)
            total = term if total is None else total + term

    total = total.astype(bf16)
    pieces = [total[0]]
    for mask in range(1, n_dp):
        pieces.append(lax.ppermute(total[mask], "dp", xor_perm(n_dp, mask)))
    pieces = jnp.stack(pieces)
    slots = jnp.arange(n_dp, dtype=jnp.int32)
    grad_tokens = jnp.take(pieces, slots ^ me, axis=0)
    grad_tokens = jnp.swapaxes(grad_tokens, 0, 1).reshape(rows, features)

    sources = jnp.asarray(source_table(n_z))[rank]
    window = jnp.take(window, sources, axis=0)
    hidden = jnp.concatenate([item[0] for item in kept])
    grads = jnp.concatenate([item[1] for item in kept], axis=1)
    deltas = window_deltas(
        n_dp,
        me,
        block_kind,
        block_ff,
        block_d,
        block_owner[:, 0],
        window[:, 0].reshape(n_tensor * rows, features),
        window[:, 1].reshape(n_tensor * rows, features),
        hidden,
        grads[0],
        grads[1],
    )
    deltas = after(deltas, gathered)
    deltas = deltas.reshape((2,) * bits + (CAP, BLOCK, BLOCK))
    cut = BLOCK // parts
    halves = [
        sum_over_dp(deltas[..., q * cut : (q + 1) * cut, :], order, n_dp)
        for q, order in enumerate(orders)
    ]
    return (grad_tokens, jnp.concatenate(halves, axis=1))


def solution(mesh):
    placed = (
        P(("groups", "dp", "tensor"), None),
        P(("groups", "dp", "tensor"), None),
        P("dp", "tensor"),
        P("dp", "tensor"),
        P("tensor", "dp"),
        P("tensor"),
        P("tensor"),
        P("tensor"),
        P("tensor", None),
    )
    return jax.shard_map(
        body,
        mesh=mesh,
        in_specs=placed,
        out_specs=(P(("groups", "dp", "tensor"), None), P(("groups", "dp", "tensor"), None, None)),
        check_vma=False,
    )
```

```python
import functools

import jax
import jax.numpy as jnp
from jax import lax
from jax.experimental import pallas as pl
from jax.experimental.pallas import tpu as pltpu
from jax.sharding import PartitionSpec as P

BLOCK = 128
CAP = 5
CONTRACT_LAST = (((1,), (1,)), ((), ()))


def xor_perm(size, mask):
    return [(i, i ^ mask) for i in range(size)]


def ring_of(length):
    if length <= 4:
        return list(range(0, length, 2)) + list(range(1, length, 2))[::-1]
    return list(range(length))


def ring_perm(length, shift):
    ring = ring_of(length)
    pairs = []
    for place, z in enumerate(ring):
        target = ring[(place + shift) % length]
        pairs += [(2 * z + core, 2 * target + core) for core in range(2)]
    return pairs


def chunk_distances(n_z):
    chunks = [(0,)]
    for distance in range(1, n_z // 2 + 1):
        chunks.append((distance,) if 2 * distance == n_z else (distance, -distance))
    return chunks


def delta_kernel(
    n_dp,
    me_ref,
    kind_ref,
    ff_ref,
    col_ref,
    owner_ref,
    grads_ref,
    tokens_ref,
    hidden_ref,
    gate_ref,
    up_ref,
    out_ref,
    used_ref,
):
    me = me_ref[0]
    out_ref[...] = jnp.zeros_like(out_ref)
    for owner in range(n_dp):
        used_ref[owner] = 0

    def step(entry, carry):
        owner = owner_ref[entry]
        slot = used_ref[owner]
        used_ref[owner] = slot + 1
        kind = kind_ref[entry]
        units = pl.ds(pl.multiple_of(ff_ref[entry] * BLOCK, BLOCK), BLOCK)
        columns = pl.ds(pl.multiple_of(col_ref[entry] * BLOCK, BLOCK), BLOCK)
        left = jnp.where(kind == 2, hidden_ref[:, units], tokens_ref[:, columns])
        right = jnp.where(
            kind == 0,
            gate_ref[:, units],
            jnp.where(kind == 1, up_ref[:, units], grads_ref[:, columns]),
        )
        out_ref[(owner ^ me) * CAP + slot] = lax.dot_general(
            left, right, (((0,), (0,)), ((), ())), preferred_element_type=jnp.float32
        )
        return carry

    lax.fori_loop(0, kind_ref.shape[0], step, 0)


def window_deltas(n_dp, me, kind, ff, col, owner, grads, tokens, hidden, gate_grad, up_grad):
    smem, vmem = pl.BlockSpec(memory_space=pltpu.SMEM), pl.BlockSpec(memory_space=pltpu.VMEM)
    return pl.pallas_call(
        functools.partial(delta_kernel, n_dp),
        out_shape=jax.ShapeDtypeStruct((n_dp * CAP, BLOCK, BLOCK), jnp.float32),
        in_specs=[smem] * 5 + [vmem] * 5,
        out_specs=vmem,
        scratch_shapes=[pltpu.SMEM((n_dp,), jnp.int32)],
        compiler_params=pltpu.CompilerParams(vmem_limit_bytes=24 << 20),
        cost_estimate=pl.CostEstimate(
            flops=2 * kind.shape[0] * BLOCK * BLOCK * grads.shape[0],
            bytes_accessed=16 << 20,
            transcendentals=0,
        ),
    )(me.reshape(1), kind, ff, col, owner, grads, tokens, hidden, gate_grad, up_grad)


def body(
    tokens,
    grad_out,
    gate_weight,
    up_weight,
    down_weight,
    block_kind,
    block_ff,
    block_d,
    block_owner,
):
    n_dp, n_tensor = lax.axis_size("dp"), lax.axis_size("tensor")
    n_z = n_tensor // 2
    bits = n_dp.bit_length() - 1
    rows, features = tokens.shape
    width, units = gate_weight.shape
    me = lax.axis_index("dp")
    bf16, f32 = jnp.bfloat16, jnp.float32
    parts = min(bits, 2)
    part = units // parts
    orders = [[(q + s) % bits for s in range(bits)] for q in range(parts)]
    distances = chunk_distances(n_z)
    last = len(distances) - 1
    stages = 2 * bits

    chain = []

    def ordered(*values):
        if not chain:
            return values
        return lax.optimization_barrier(values + tuple(chain))[: len(values)]

    def done(*results):
        chain[:] = results

    def over_dp(value, mask):
        return lax.ppermute(value, "dp", xor_perm(n_dp, mask))

    def over_core(value):
        return lax.ppermute(value, "tensor", xor_perm(n_tensor, 1))

    def over_z(value, shift):
        return lax.ppermute(value, "tensor", ring_perm(n_z, shift))

    def hop(held, distance, axis):
        ahead, behind = held[distance - 1], held[1 - distance]
        if 2 * distance == n_z:
            first = over_z(lax.index_in_dim(ahead, 0, axis, keepdims=False), 1)
            second = over_z(lax.index_in_dim(behind, 1, axis, keepdims=False), -1)
            held[distance] = (first, second)
        else:
            held[distance], held[-distance] = over_z(ahead, 1), over_z(behind, -1)

    pieces = []
    for mask in range(n_dp):
        start = (me ^ mask) * width
        piece = jnp.stack(
            [lax.dynamic_slice_in_dim(x, start, width, axis=1) for x in (grad_out, tokens)]
        )
        pieces.append(over_dp(piece, mask) if mask else piece)
    mine = jnp.stack(pieces, axis=1)

    held = {0: mine}
    window_held = {}
    shards, other = {0: mine[:, None]}, {}
    other[0] = over_core(shards[0])
    hop(held, 1, 0)
    flying, local, owns, out_flying, terms = {}, {}, {}, {}, {}

    def fetch(k):
        got = [x for distance in distances[k] for x in jax.tree.leaves(held[distance])]
        got = ordered(*got)
        if 2 * k == n_z:
            shards[k] = jnp.stack(got)[:, None]
        else:
            held[k], held[-k] = got
            shards[k] = jnp.stack(got, axis=1)
        other[k] = over_core(shards[k])
        if k < last:
            hop(held, k + 1, 0)
        done(shards[k])

    def forward(k):
        own, others = ordered(shards[k], other[k])
        chunk = jnp.swapaxes(jnp.stack([own, others], axis=3), 1, 2).reshape(2, -1, width)
        gate = jnp.dot(chunk[1], gate_weight, preferred_element_type=f32).astype(bf16)
        upward = jnp.dot(chunk[1], up_weight, preferred_element_type=f32).astype(bf16)
        hidden_grad = lax.dot_general(
            chunk[0], down_weight, CONTRACT_LAST, preferred_element_type=f32
        ).astype(bf16)
        values = []
        for q in range(parts):
            cut = slice(q * part, (q + 1) * part)
            value = jnp.stack([gate[:, cut], upward[:, cut], hidden_grad[:, cut]])
            values.append(value.reshape((3,) + (2,) * bits + (-1, part)))
        return values

    def send_halves(values, orders, s, lead):
        keep, fly = [], []
        for value, order in zip(values, orders):
            left = sorted(order[s:], reverse=True)
            axis = lead + left.index(order[s])
            keep.append(lax.index_in_dim(value, 0, axis, keepdims=False))
            fly.append(lax.index_in_dim(value, 1, axis, keepdims=False).astype(bf16))
        fly = [over_dp(x, 1 << order[s]) for x, order in zip(fly, orders)]
        return keep, fly

    def add_halves(keep, fly):
        got = ordered(*fly)
        return [x.astype(f32) + y.astype(f32) for x, y in zip(keep, got)]

    def gradients(sums):
        hiddens, values = [], []
        for g, u, h in sums:
            sig = jax.nn.sigmoid(g)
            silu = g * sig
            hiddens.append((silu * u).astype(bf16))
            gate_grad = (h * u * sig * (1.0 + g * (1.0 - sig))).astype(bf16)
            up_grad = (h * silu).astype(bf16)
            values.append(jnp.stack([gate_grad, up_grad]))
        return hiddens, values

    def join(values, got, s):
        joined = []
        for value, more, order in zip(values, got, orders):
            order = order[::-1]
            axis = sum(1 for bit in order[:s] if bit > order[s])
            joined.append(jnp.stack([value, more], axis=axis))
        return joined

    def step(k, s):
        if s < bits:
            values = forward(k) if s == 0 else add_halves(local[k], flying[k])
            local[k], flying[k] = send_halves(values, orders, s, 1)
            done(*values)
            return
        if s == bits:
            hiddens, values = gradients(add_halves(local[k], flying[k]))
            owns[k] = (hiddens, values)
            done(*hiddens, *values)
        else:
            if k == 0 and s == stages - 1:
                got = ordered(*flying[last], *flying[0])
                flying[last] = got[:parts]
                values = join(local[k], got[parts:], s - 1 - bits)
            else:
                values = join(local[k], ordered(*flying[k]), s - 1 - bits)
            done(*values)
        local[k] = values
        flying[k] = [
            over_dp(value, 1 << order[::-1][s - bits]) for value, order in zip(values, orders)
        ]

    def finish(k):
        values = join(local[k], ordered(*flying[k]), bits - 1)
        gathered = []
        for value in values:
            value = value.reshape((n_dp, 2, -1, part))
            gathered.append(jnp.swapaxes(value, 0, 1).reshape(2, -1, part))
        gathered = jnp.concatenate(gathered, axis=2)
        out = lax.dot_general(gathered[0], gate_weight, CONTRACT_LAST, preferred_element_type=f32)
        out = out + lax.dot_general(
            gathered[1], up_weight, CONTRACT_LAST, preferred_element_type=f32
        )
        out = out.reshape(n_dp, len(distances[k]), 2, rows, width)
        send = out[:, :, 1].astype(bf16)
        out_flying[k] = (out[:, :, 0], over_core(send))
        done(send)

    def send_home(k):
        own, got = out_flying[k]
        (got,) = ordered(got)
        out = own + got.astype(f32)
        for place, distance in enumerate(distances[k]):
            term = out[:, place]
            if distance:
                term = term.astype(bf16)
                terms[distance] = over_z(term, -distance)
            else:
                terms[distance] = term
            done(term)

    def window_hop(distance):
        if distance == 1:
            window_held[0] = jnp.stack(ordered(grad_out, tokens))
        elif distance <= last:
            window_held[distance - 1], window_held[1 - distance] = ordered(
                window_held[distance - 1], window_held[1 - distance]
            )
        if distance <= last:
            hop(window_held, distance, 0)
            return
        order = [d for chunk in distances for d in chunk]
        got = ordered(*[x for d in order for x in jax.tree.leaves(window_held[d])])
        got = list(got)
        if 2 * last == n_z:
            got[-2:] = [jnp.stack(got[-2:])]
        window_held["own"] = jnp.stack(got, axis=1)
        window_held["other"] = over_core(window_held["own"])
        done(window_held["own"])

    def delta_terms():
        both, other_core = ordered(window_held["own"], window_held["other"])
        window = jnp.stack([both, other_core], axis=2).reshape(2, -1, features)
        chunks = range(last + 1)
        hidden = jnp.concatenate([jnp.concatenate(owns[k][0], axis=1) for k in chunks])
        grads = jnp.concatenate([jnp.concatenate(owns[k][1], axis=2) for k in chunks], axis=1)
        deltas = window_deltas(
            n_dp,
            me,
            block_kind,
            block_ff,
            block_d,
            block_owner[:, 0],
            window[0],
            window[1],
            hidden,
            grads[0],
            grads[1],
        )
        done(deltas)
        deltas = deltas.reshape((2,) * bits + (CAP, BLOCK, BLOCK))
        cut = BLOCK // parts
        halves = [deltas[..., q * cut : (q + 1) * cut, :] for q in range(parts)]
        local["delta"], flying["delta"] = send_halves(halves, orders, 0, 0)

    def delta_sums(s):
        halves = add_halves(local["delta"], flying["delta"])
        if s < bits:
            local["delta"], flying["delta"] = send_halves(halves, orders, s, 0)
        done(*halves)
        return halves

    events = []
    for k in range(last + 1):
        for s in range(stages):
            if k or s < stages - 1:
                events.append((k + s, -k, functools.partial(step, k, s)))
        if k:
            events.append((k - 1, 0.5 - (k - 1), functools.partial(fetch, k)))
            events.append((k + stages, -k, functools.partial(finish, k)))
            events.append((k + stages, 0.5 - k, functools.partial(send_home, k)))
        events.append((1 + k, 50, functools.partial(window_hop, k + 1)))
    events.append((last + bits, 0.5 - last, delta_terms))
    events.append((last + stages, -last - 1, functools.partial(step, 0, stages - 1)))
    for s in range(1, bits):
        events.append((last + stages, 50 + s, functools.partial(delta_sums, s)))
    for _, _, run in sorted(events, key=lambda event: event[:2]):
        run()
    finish(0)
    send_home(0)

    total = terms[0]
    for distance in ordered(*[terms[d] for d in terms if d]):
        total = total + distance.astype(f32)
    total = total.astype(bf16)
    pieces = [total[0]] + [over_dp(total[mask], mask) for mask in range(1, n_dp)]
    done(total)
    halves = delta_sums(bits)
    pieces = jnp.stack(pieces)
    slots = jnp.arange(n_dp, dtype=jnp.int32)
    grad_tokens = pieces.at[slots ^ me].get(mode="promise_in_bounds")
    grad_tokens = jnp.swapaxes(grad_tokens, 0, 1).reshape(rows, features)
    return (grad_tokens, jnp.concatenate(halves, axis=1))


def solution(mesh):
    placed = (
        P(("groups", "dp", "tensor"), None),
        P(("groups", "dp", "tensor"), None),
        P("dp", "tensor"),
        P("dp", "tensor"),
        P("tensor", "dp"),
        P("tensor"),
        P("tensor"),
        P("tensor"),
        P("tensor", None),
    )
    return jax.shard_map(
        body,
        mesh=mesh,
        in_specs=placed,
        out_specs=(P(("groups", "dp", "tensor"), None), P(("groups", "dp", "tensor"), None, None)),
        check_vma=False,
    )
```

```python
import functools

import jax
import jax.numpy as jnp
from jax import lax
from jax.experimental import pallas as pl
from jax.experimental.pallas import tpu as pltpu
from jax.sharding import PartitionSpec as P

BLOCK = 128
CAP = 5
CONTRACT_LAST = (((1,), (1,)), ((), ()))
SMALL = pl.CostEstimate(flops=1, bytes_accessed=1, transcendentals=0)


def xor_perm(size, mask):
    return [(i, i ^ mask) for i in range(size)]


def ring_of(length):
    if length <= 4:
        return list(range(0, length, 2)) + list(range(1, length, 2))[::-1]
    return list(range(length))


def ring_perm(length, shift):
    ring = ring_of(length)
    pairs = []
    for place, z in enumerate(ring):
        target = ring[(place + shift) % length]
        pairs += [(2 * z + core, 2 * target + core) for core in range(2)]
    return pairs


def chunk_distances(n_z):
    chunks = [(0,)]
    for distance in range(1, n_z // 2 + 1):
        chunks.append((distance,) if 2 * distance == n_z else (distance, -distance))
    return chunks


def delta_kernel(n_dp, n_pieces, me_ref, kind_ref, ff_ref, col_ref, owner_ref, *refs):
    window_refs, refs = refs[:2], refs[2:]
    hidden_refs, grad_refs, refs = refs[:n_pieces], refs[n_pieces : 2 * n_pieces], refs[2 * n_pieces :]
    out_ref, grads_ref, tokens_ref, hidden_ref, gate_ref, up_ref, used_ref = refs
    me = me_ref[0]
    out_ref[...] = jnp.zeros_like(out_ref)
    for owner in range(n_dp):
        used_ref[owner] = 0

    start = 0
    _, chips, rows, _ = window_refs[0].shape
    for chip in range(chips):
        for window_ref in window_refs:
            grads_ref[start : start + rows] = window_ref[0, chip]
            tokens_ref[start : start + rows] = window_ref[1, chip]
            start += rows
    start, column = 0, 0
    for hidden_piece, grad_piece in zip(hidden_refs, grad_refs):
        rows, units = hidden_piece.shape
        place = (slice(start, start + rows), slice(column, column + units))
        hidden_ref[place] = hidden_piece[...]
        gate_ref[place] = grad_piece[0]
        up_ref[place] = grad_piece[1]
        column += units
        if column == hidden_ref.shape[1]:
            start, column = start + rows, 0

    def step(entry, carry):
        owner = owner_ref[entry]
        slot = used_ref[owner]
        used_ref[owner] = slot + 1
        kind = kind_ref[entry]
        units = pl.ds(pl.multiple_of(ff_ref[entry] * BLOCK, BLOCK), BLOCK)
        columns = pl.ds(pl.multiple_of(col_ref[entry] * BLOCK, BLOCK), BLOCK)
        left = jnp.where(kind == 2, hidden_ref[:, units], tokens_ref[:, columns])
        right = jnp.where(
            kind == 0,
            gate_ref[:, units],
            jnp.where(kind == 1, up_ref[:, units], grads_ref[:, columns]),
        )
        out_ref[(owner ^ me) * CAP + slot] = lax.dot_general(
            left, right, (((0,), (0,)), ((), ())), preferred_element_type=jnp.float32
        )
        return carry

    lax.fori_loop(0, kind_ref.shape[0], step, 0)


def window_deltas(n_dp, units, me, kind, ff, col, owner, windows, hiddens, grads):
    _, chips, rows, features = windows[0].shape
    total = 2 * chips * rows
    if rows % 16:
        joined = jnp.stack(windows, axis=2).reshape(2, 1, total, features)
        windows = [joined[:, :, : total // 2], joined[:, :, total // 2 :]]
        across = units // hiddens[0].shape[1]
        groups = range(0, len(hiddens), across)
        hiddens = [
            jnp.concatenate([jnp.concatenate(hiddens[i : i + across], axis=1) for i in groups])
        ]
        grads = [
            jnp.concatenate([jnp.concatenate(grads[i : i + across], axis=2) for i in groups], axis=1)
        ]
    smem, vmem = pl.BlockSpec(memory_space=pltpu.SMEM), pl.BlockSpec(memory_space=pltpu.VMEM)
    bf16 = jnp.bfloat16
    return pl.pallas_call(
        functools.partial(delta_kernel, n_dp, len(hiddens)),
        out_shape=jax.ShapeDtypeStruct((n_dp * CAP, BLOCK, BLOCK), jnp.float32),
        in_specs=[smem] * 5 + [vmem] * (2 + 2 * len(hiddens)),
        out_specs=vmem,
        scratch_shapes=[
            pltpu.VMEM((total, features), bf16),
            pltpu.VMEM((total, features), bf16),
            pltpu.VMEM((total, units), bf16),
            pltpu.VMEM((total, units), bf16),
            pltpu.VMEM((total, units), bf16),
            pltpu.SMEM((n_dp,), jnp.int32),
        ],
        compiler_params=pltpu.CompilerParams(vmem_limit_bytes=24 << 20),
        cost_estimate=SMALL,
    )(me.reshape(1), kind, ff, col, owner, *windows, *hiddens, *grads)


def forward_kernel(chunk_ref, gate_ref, up_ref, down_ref, out_ref):
    f32 = jnp.float32
    rows = chunk_ref[1]
    gate = jnp.dot(rows, gate_ref[...], preferred_element_type=f32)
    out_ref[0] = gate.astype(out_ref.dtype)
    upward = jnp.dot(rows, up_ref[...], preferred_element_type=f32)
    out_ref[1] = upward.astype(out_ref.dtype)
    hidden_grad = lax.dot_general(
        chunk_ref[0], down_ref[...], CONTRACT_LAST, preferred_element_type=f32
    )
    out_ref[2] = hidden_grad.astype(out_ref.dtype)


def forward_partials(chunk, gate_weight, up_weight, down_weight):
    _, rows, width = chunk.shape
    units = gate_weight.shape[1]
    block = min(units, 512)
    return pl.pallas_call(
        forward_kernel,
        grid=(units // block,),
        out_shape=jax.ShapeDtypeStruct((3, rows, units), jnp.bfloat16),
        in_specs=[
            pl.BlockSpec((2, rows, width), lambda j: (0, 0, 0)),
            pl.BlockSpec((width, block), lambda j: (0, j)),
            pl.BlockSpec((width, block), lambda j: (0, j)),
            pl.BlockSpec((block, width), lambda j: (j, 0)),
        ],
        out_specs=pl.BlockSpec((3, rows, block), lambda j: (0, 0, j)),
        compiler_params=pltpu.CompilerParams(vmem_limit_bytes=24 << 20),
        cost_estimate=SMALL,
    )(chunk, gate_weight, up_weight, down_weight)


def backward_kernel(grads_ref, gate_ref, up_ref, out_ref):
    f32 = jnp.float32
    first = lax.dot_general(grads_ref[0], gate_ref[...], CONTRACT_LAST, preferred_element_type=f32)
    second = lax.dot_general(grads_ref[1], up_ref[...], CONTRACT_LAST, preferred_element_type=f32)
    out_ref[...] = first + second


def backward_partials(grads, gate_weight, up_weight):
    _, rows, units = grads.shape
    width = gate_weight.shape[0]
    block = min(width, 256)
    return pl.pallas_call(
        backward_kernel,
        grid=(width // block,),
        out_shape=jax.ShapeDtypeStruct((rows, width), jnp.float32),
        in_specs=[
            pl.BlockSpec((2, rows, units), lambda j: (0, 0, 0)),
            pl.BlockSpec((block, units), lambda j: (j, 0)),
            pl.BlockSpec((block, units), lambda j: (j, 0)),
        ],
        out_specs=pl.BlockSpec((rows, block), lambda j: (0, j)),
        compiler_params=pltpu.CompilerParams(vmem_limit_bytes=24 << 20),
        cost_estimate=SMALL,
    )(grads, gate_weight, up_weight)


def body(
    tokens,
    grad_out,
    gate_weight,
    up_weight,
    down_weight,
    block_kind,
    block_ff,
    block_d,
    block_owner,
):
    n_dp, n_tensor = lax.axis_size("dp"), lax.axis_size("tensor")
    n_z = n_tensor // 2
    bits = n_dp.bit_length() - 1
    rows, features = tokens.shape
    width, units = gate_weight.shape
    me = lax.axis_index("dp")
    bf16, f32 = jnp.bfloat16, jnp.float32
    parts = min(bits, 2)
    part = units // parts
    orders = [[(q + s) % bits for s in range(bits)] for q in range(parts)]
    distances = chunk_distances(n_z)
    last = len(distances) - 1
    stages = 2 * bits

    chain = []

    def ordered(*values):
        if not chain:
            return values
        return lax.optimization_barrier(values + tuple(chain))[: len(values)]

    def done(*results):
        chain[:] = results

    def over_dp(value, mask):
        return lax.ppermute(value, "dp", xor_perm(n_dp, mask))

    def over_core(value):
        return lax.ppermute(value, "tensor", xor_perm(n_tensor, 1))

    def over_z(value, shift):
        return lax.ppermute(value, "tensor", ring_perm(n_z, shift))

    def hop(distance):
        held[distance] = over_z(held[distance - 1], 1)
        if 2 * distance < n_z:
            held[-distance] = over_z(held[1 - distance], -1)

    pieces = []
    for mask in range(n_dp):
        start = (me ^ mask) * width
        piece = jnp.stack(
            [lax.dynamic_slice_in_dim(x, start, width, axis=1) for x in (grad_out, tokens)]
        )
        pieces.append(over_dp(piece, mask) if mask else piece)
    mine = jnp.stack(pieces, axis=1)

    held = {0: mine}
    window_held = {}
    shards, other = {0: mine[:, None]}, {}
    other[0] = over_core(shards[0])
    hop(1)
    flying, local, owns, out_flying, terms = {}, {}, {}, {}, {}

    def fetch(k):
        got = ordered(*[held[distance] for distance in distances[k]])
        for distance, rows_there in zip(distances[k], got):
            held[distance] = rows_there
        shards[k] = jnp.stack(got, axis=1)
        other[k] = over_core(shards[k])
        if k < last:
            hop(k + 1)
        done(shards[k])

    def forward(k):
        own, others = ordered(shards[k], other[k])
        chunk = jnp.swapaxes(jnp.stack([own, others], axis=3), 1, 2).reshape(2, -1, width)
        sums = forward_partials(chunk, gate_weight, up_weight, down_weight)
        values = []
        for q in range(parts):
            value = sums[:, :, q * part : (q + 1) * part]
            values.append(value.reshape((3,) + (2,) * bits + (-1, part)))
        return values

    def send_halves(values, orders, s, lead):
        keep, fly = [], []
        for value, order in zip(values, orders):
            left = sorted(order[s:], reverse=True)
            axis = lead + left.index(order[s])
            keep.append(lax.index_in_dim(value, 0, axis, keepdims=False))
            fly.append(lax.index_in_dim(value, 1, axis, keepdims=False).astype(bf16))
        fly = [over_dp(x, 1 << order[s]) for x, order in zip(fly, orders)]
        return keep, fly

    def add_halves(keep, fly):
        got = ordered(*fly)
        return [x.astype(f32) + y.astype(f32) for x, y in zip(keep, got)]

    def gradients(sums):
        hiddens, values = [], []
        for g, u, h in sums:
            sig = jax.nn.sigmoid(g)
            silu = g * sig
            hiddens.append((silu * u).astype(bf16))
            gate_grad = (h * u * sig * (1.0 + g * (1.0 - sig))).astype(bf16)
            up_grad = (h * silu).astype(bf16)
            values.append(jnp.stack([gate_grad, up_grad]))
        return hiddens, values

    def join(values, got, s):
        joined = []
        for value, more, order in zip(values, got, orders):
            order = order[::-1]
            axis = sum(1 for bit in order[:s] if bit > order[s])
            joined.append(jnp.stack([value, more], axis=axis))
        return joined

    def step(k, s):
        if s < bits:
            values = forward(k) if s == 0 else add_halves(local[k], flying[k])
            local[k], flying[k] = send_halves(values, orders, s, 1)
            done(*values)
            return
        if s == bits:
            hiddens, values = gradients(add_halves(local[k], flying[k]))
            owns[k] = (hiddens, values)
            done(*hiddens, *values)
        else:
            values = join(local[k], ordered(*flying[k]), s - 1 - bits)
            done(*values)
        local[k] = values
        if k or s < stages - 1:
            gather_step(k, s)

    def gather_step(k, s):
        values = local[k]
        if k == 0 and s == stages - 1:
            local[k] = values = list(ordered(*values))
        flying[k] = [
            over_dp(value, 1 << order[::-1][s - bits]) for value, order in zip(values, orders)
        ]

    def finish(k):
        values = join(local[k], ordered(*flying[k]), bits - 1)
        gathered = []
        for value in values:
            value = value.reshape((n_dp, 2, -1, part))
            gathered.append(jnp.swapaxes(value, 0, 1).reshape(2, -1, part))
        gathered = jnp.concatenate(gathered, axis=2)
        out = backward_partials(gathered, gate_weight, up_weight)
        out = out.reshape(n_dp, len(distances[k]), 2, rows, width)
        send = out[:, :, 1].astype(bf16)
        out_flying[k] = (out[:, :, 0], over_core(send))
        done(send)

    def send_home(k):
        own, got = out_flying[k]
        (got,) = ordered(got)
        out = own + got.astype(f32)
        for place, distance in enumerate(distances[k]):
            term = out[:, place]
            if distance:
                term = term.astype(bf16)
                terms[distance] = over_z(term, -distance)
            else:
                terms[distance] = term
            done(term)

    def window_hop(distance):
        if distance == 1:
            window_held[0] = jnp.stack(ordered(grad_out, tokens))
        else:
            (window_held[distance - 1],) = ordered(window_held[distance - 1])
        if distance < n_z:
            window_held[distance] = over_z(window_held[distance - 1], 1)
            return
        places = [distance % n_z for chunk in distances for distance in chunk]
        window_held["own"] = jnp.stack([window_held[place] for place in places], axis=1)
        window_held["other"] = over_core(window_held["own"])
        done(window_held["own"])

    def delta_terms():
        windows = ordered(window_held["own"], window_held["other"])
        chunks = range(last + 1)
        deltas = window_deltas(
            n_dp,
            units,
            me,
            block_kind,
            block_ff,
            block_d,
            block_owner[:, 0],
            list(windows),
            [piece for k in chunks for piece in owns[k][0]],
            [piece for k in chunks for piece in owns[k][1]],
        )
        done(deltas)
        deltas = deltas.reshape((n_dp, CAP, BLOCK, BLOCK))
        delta_send(deltas)

    def delta_send(values):
        half = values.shape[0] // 2
        local["delta"] = values[:half]
        flying["delta"] = over_dp(values[half:].astype(bf16), half)

    def delta_add():
        (got,) = ordered(flying["delta"])
        return local["delta"] + got.astype(f32)

    def delta_step():
        values = delta_add()
        done(values)
        delta_send(values)

    events = {}
    for k in range(last + 1):
        for s in range(stages):
            events["step", k, s] = (k + s, 0 if s == 0 else 2 + k, functools.partial(step, k, s))
        if k:
            events["fetch", k] = (k - 1, 1, functools.partial(fetch, k))
            events["finish", k] = (k + stages, -k, functools.partial(finish, k))
            events["home", k] = (k + stages, 0.5 - k, functools.partial(send_home, k))
    for distance in range(n_z):
        events["window", distance] = (
            1 + distance * (last + bits - 1) // n_z,
            50 + distance,
            functools.partial(window_hop, distance + 1),
        )
    events["delta"] = (last + bits, 99, delta_terms)
    for s in range(1, bits):
        events["delta", s] = (last + stages, 50 + s, delta_step)
    events["late"] = (last + stages, -last - 1, functools.partial(gather_step, 0, stages - 1))
    if (n_z, bits) == (4, 2):
        listed = [("step", 0, 0), ("fetch", 1), ("step", 0, 1), ("step", 1, 0), ("fetch", 2)]
        listed += [("step", 0, 2), ("window", 0), ("step", 0, 3), ("step", 2, 0), ("window", 1)]
        listed += [("step", 1, 1), ("step", 2, 1), ("window", 2), ("step", 1, 2), ("step", 2, 2)]
        listed += [("window", 3), ("step", 1, 3), ("step", 2, 3), "delta", ("finish", 1), "late"]
        listed += [("finish", 2), ("delta", 1), ("home", 1), ("home", 2)]
    else:
        listed = sorted(events, key=lambda name: events[name][:2])
    for name in listed:
        events[name][2]()
    finish(0)
    send_home(0)

    total = terms[0]
    for distance in ordered(*[terms[d] for d in terms if d]):
        total = total + distance.astype(f32)
    total = total.astype(bf16)
    pieces = [total[0]] + [over_dp(total[mask], mask) for mask in range(1, n_dp)]
    done(total)
    deltas = delta_add()[0]
    pieces = jnp.stack(pieces)
    slots = jnp.arange(n_dp, dtype=jnp.int32)
    grad_tokens = pieces.at[slots ^ me].get(mode="promise_in_bounds")
    grad_tokens = jnp.swapaxes(grad_tokens, 0, 1).reshape(rows, features)
    return (grad_tokens, deltas)


def solution(mesh):
    placed = (
        P(("groups", "dp", "tensor"), None),
        P(("groups", "dp", "tensor"), None),
        P("dp", "tensor"),
        P("dp", "tensor"),
        P("tensor", "dp"),
        P("tensor"),
        P("tensor"),
        P("tensor"),
        P("tensor", None),
    )
    return jax.shard_map(
        body,
        mesh=mesh,
        in_specs=placed,
        out_specs=(P(("groups", "dp", "tensor"), None), P(("groups", "dp", "tensor"), None, None)),
        check_vma=False,
    )
```

```python
import functools

import jax
import jax.numpy as jnp
import numpy as np
from jax import lax
from jax.experimental import pallas as pl
from jax.experimental.pallas import tpu as pltpu
from jax.sharding import PartitionSpec as P

BLOCK = 128
CAP = 5
CONTRACT_LAST = (((1,), (1,)), ((), ()))
SMALL = pl.CostEstimate(flops=1, bytes_accessed=1, transcendentals=0)


def xor_perm(size, mask):
    return [(i, i ^ mask) for i in range(size)]


def ring_of(length):
    if length <= 4:
        return list(range(0, length, 2)) + list(range(1, length, 2))[::-1]
    return list(range(length))


def ring_perm(length, shift):
    ring = ring_of(length)
    pairs = []
    for place, z in enumerate(ring):
        target = ring[(place + shift) % length]
        pairs += [(2 * z + core, 2 * target + core) for core in range(2)]
    return pairs


def in_hbm(value):
    return pltpu.with_memory_space_constraint(value, pltpu.HBM)


def chunk_distances(n_z):
    chunks = [(0,)]
    for distance in range(1, n_z // 2 + 1):
        chunks.append((distance,) if 2 * distance == n_z else (distance, -distance))
    return chunks


def delta_kernel(n_dp, n_pieces, me_ref, kind_ref, ff_ref, col_ref, owner_ref, *refs):
    window_refs, refs = refs[:2], refs[2:]
    hidden_refs, grad_refs, refs = refs[:n_pieces], refs[n_pieces : 2 * n_pieces], refs[2 * n_pieces :]
    out_ref, grads_ref, tokens_ref, hidden_ref, gate_ref, up_ref, used_ref = refs
    me = me_ref[0]
    out_ref[...] = jnp.zeros_like(out_ref)
    for owner in range(n_dp):
        used_ref[owner] = 0

    start = 0
    _, chips, rows, _ = window_refs[0].shape
    for chip in range(chips):
        for window_ref in window_refs:
            grads_ref[start : start + rows] = window_ref[0, chip]
            tokens_ref[start : start + rows] = window_ref[1, chip]
            start += rows
    start, column = 0, 0
    for hidden_piece, grad_piece in zip(hidden_refs, grad_refs):
        rows, units = hidden_piece.shape
        place = (slice(start, start + rows), slice(column, column + units))
        hidden_ref[place] = hidden_piece[...]
        gate_ref[place] = grad_piece[0]
        up_ref[place] = grad_piece[1]
        column += units
        if column == hidden_ref.shape[1]:
            start, column = start + rows, 0

    def step(entry, carry):
        owner = owner_ref[entry]
        slot = used_ref[owner]
        used_ref[owner] = slot + 1
        kind = kind_ref[entry]
        units = pl.ds(pl.multiple_of(ff_ref[entry] * BLOCK, BLOCK), BLOCK)
        columns = pl.ds(pl.multiple_of(col_ref[entry] * BLOCK, BLOCK), BLOCK)
        left = jnp.where(kind == 2, hidden_ref[:, units], tokens_ref[:, columns])
        right = jnp.where(
            kind == 0,
            gate_ref[:, units],
            jnp.where(kind == 1, up_ref[:, units], grads_ref[:, columns]),
        )
        out_ref[(owner ^ me) * CAP + slot] = lax.dot_general(
            left, right, (((0,), (0,)), ((), ())), preferred_element_type=jnp.float32
        )
        return carry

    lax.fori_loop(0, kind_ref.shape[0], step, 0)


def window_deltas(n_dp, units, me, kind, ff, col, owner, windows, hiddens, grads):
    _, chips, rows, features = windows[0].shape
    total = 2 * chips * rows
    if rows % 16:
        joined = jnp.stack(windows, axis=2).reshape(2, 1, total, features)
        windows = [joined[:, :, : total // 2], joined[:, :, total // 2 :]]
        across = units // hiddens[0].shape[1]
        groups = range(0, len(hiddens), across)
        hiddens = [
            jnp.concatenate([jnp.concatenate(hiddens[i : i + across], axis=1) for i in groups])
        ]
        grads = [
            jnp.concatenate([jnp.concatenate(grads[i : i + across], axis=2) for i in groups], axis=1)
        ]
    smem, vmem = pl.BlockSpec(memory_space=pltpu.SMEM), pl.BlockSpec(memory_space=pltpu.VMEM)
    bf16 = jnp.bfloat16
    return pl.pallas_call(
        functools.partial(delta_kernel, n_dp, len(hiddens)),
        out_shape=jax.ShapeDtypeStruct((n_dp * CAP, BLOCK, BLOCK), jnp.float32),
        in_specs=[smem] * 5 + [vmem] * (2 + 2 * len(hiddens)),
        out_specs=vmem,
        scratch_shapes=[
            pltpu.VMEM((total, features), bf16),
            pltpu.VMEM((total, features), bf16),
            pltpu.VMEM((total, units), bf16),
            pltpu.VMEM((total, units), bf16),
            pltpu.VMEM((total, units), bf16),
            pltpu.SMEM((n_dp,), jnp.int32),
        ],
        compiler_params=pltpu.CompilerParams(vmem_limit_bytes=24 << 20),
        cost_estimate=SMALL,
    )(me.reshape(1), kind, ff, col, owner, *windows, *hiddens, *grads)


def forward_kernel(own_ref, other_ref, gate_ref, up_ref, down_ref, out_ref, chunk_ref):
    f32 = jnp.float32

    @pl.when(pl.program_id(0) == 0)
    def _():
        start = 0
        chips, _, windows, rows, _ = own_ref.shape
        for window in range(windows):
            for chip in range(chips):
                for ref in (own_ref, other_ref):
                    chunk_ref[:, start : start + rows] = ref[chip, :, window]
                    start += rows

    tokens = chunk_ref[1]
    gate = jnp.dot(tokens, gate_ref[...], preferred_element_type=f32)
    out_ref[0] = gate.astype(out_ref.dtype)
    upward = jnp.dot(tokens, up_ref[...], preferred_element_type=f32)
    out_ref[1] = upward.astype(out_ref.dtype)
    hidden_grad = lax.dot_general(
        chunk_ref[0], down_ref[...], CONTRACT_LAST, preferred_element_type=f32
    )
    out_ref[2] = hidden_grad.astype(out_ref.dtype)


def forward_partials(own, other, gate_weight, up_weight, down_weight):
    chips, _, windows, rows, width = own.shape
    units = gate_weight.shape[1]
    total = 2 * chips * windows * rows
    if rows % 16:
        joined = jnp.stack([own, other], axis=3).transpose(1, 2, 0, 3, 4, 5)
        joined = joined.reshape(1, 2, 1, total, width)
        own, other = joined[..., : total // 2, :], joined[..., total // 2 :, :]
    block = min(units, 512)
    whole = pl.BlockSpec(own.shape, lambda j: (0, 0, 0, 0, 0))
    weights = [in_hbm(w) for w in (gate_weight, up_weight, down_weight)]
    return pl.pallas_call(
        forward_kernel,
        grid=(units // block,),
        out_shape=jax.ShapeDtypeStruct((3, total, units), jnp.bfloat16),
        in_specs=[
            whole,
            whole,
            pl.BlockSpec((width, block), lambda j: (0, j)),
            pl.BlockSpec((width, block), lambda j: (0, j)),
            pl.BlockSpec((block, width), lambda j: (j, 0)),
        ],
        out_specs=pl.BlockSpec((3, total, block), lambda j: (0, 0, j)),
        scratch_shapes=[pltpu.VMEM((2, total, width), jnp.bfloat16)],
        compiler_params=pltpu.CompilerParams(vmem_limit_bytes=24 << 20),
        cost_estimate=SMALL,
    )(own, other, *weights)


def backward_kernel(places, *refs):
    f32 = jnp.float32
    n = len(places)
    piece_refs, (gate_ref, up_ref, out_ref, grads_ref) = refs[:n], refs[n:]

    @pl.when(pl.program_id(0) == 0)
    def _():
        for piece_ref, (starts, column) in zip(piece_refs, places):
            _, _, rows, columns = piece_ref.shape
            for index, start in enumerate(starts):
                place = (slice(None), slice(start, start + rows), slice(column, column + columns))
                grads_ref[place] = piece_ref[index]

    first = lax.dot_general(grads_ref[0], gate_ref[...], CONTRACT_LAST, preferred_element_type=f32)
    second = lax.dot_general(grads_ref[1], up_ref[...], CONTRACT_LAST, preferred_element_type=f32)
    out_ref[...] = first + second


def backward_partials(pieces, places, gate_weight, up_weight):
    width, units = gate_weight.shape
    total = max(start for starts, _ in places for start in starts) + pieces[0].shape[2]
    if pieces[0].shape[2] % 16:
        grads = jnp.zeros((2, total, units), pieces[0].dtype)
        for piece, (starts, column) in zip(pieces, places):
            for index, start in enumerate(starts):
                grads = grads.at[
                    :, start : start + piece.shape[2], column : column + piece.shape[3]
                ].set(piece[index])
        pieces, places = [grads[None]], [((0,), 0)]
    block = min(width, 256)
    weights = [in_hbm(w) for w in (gate_weight, up_weight)]
    return pl.pallas_call(
        functools.partial(backward_kernel, places),
        grid=(width // block,),
        out_shape=jax.ShapeDtypeStruct((total, width), jnp.float32),
        in_specs=[pl.BlockSpec(piece.shape, lambda j: (0, 0, 0, 0)) for piece in pieces]
        + [pl.BlockSpec((block, units), lambda j: (j, 0))] * 2,
        out_specs=pl.BlockSpec((total, block), lambda j: (0, j)),
        scratch_shapes=[pltpu.VMEM((2, total, units), jnp.bfloat16)],
        compiler_params=pltpu.CompilerParams(vmem_limit_bytes=24 << 20),
        cost_estimate=SMALL,
    )(*pieces, *weights)


def body(
    tokens,
    grad_out,
    gate_weight,
    up_weight,
    down_weight,
    block_kind,
    block_ff,
    block_d,
    block_owner,
):
    n_dp, n_tensor = lax.axis_size("dp"), lax.axis_size("tensor")
    n_z = n_tensor // 2
    bits = n_dp.bit_length() - 1
    rows, features = tokens.shape
    width, units = gate_weight.shape
    me = lax.axis_index("dp")
    bf16, f32 = jnp.bfloat16, jnp.float32
    parts = min(bits, 2)
    part = units // parts
    orders = [[(q + s) % bits for s in range(bits)] for q in range(parts)]
    distances = chunk_distances(n_z)
    last = len(distances) - 1
    stages = 2 * bits

    chain = []

    def ordered(*values):
        if not chain:
            return values
        return lax.optimization_barrier(values + tuple(chain))[: len(values)]

    def done(*results):
        chain[:] = results

    def over_dp(value, mask):
        return lax.ppermute(value, "dp", xor_perm(n_dp, mask))

    def over_core(value):
        return lax.ppermute(value, "tensor", xor_perm(n_tensor, 1))

    def over_z(value, shift):
        return lax.ppermute(value, "tensor", ring_perm(n_z, shift))

    held, shards, other, own_raw = {}, {}, {}, {}
    flying, local, owns, out_flying, terms = {}, {}, {}, {}, {}

    def hop(distance):
        held[distance] = over_z(held[distance - 1], 1)
        if 2 * distance < n_z:
            held[-distance] = over_z(held[1 - distance], -1)

    def exchange(k, rows_there):
        pieces = []
        for mask in range(n_dp):
            piece = lax.dynamic_slice_in_dim(rows_there, (me ^ mask) * width, width, axis=3)
            pieces.append(over_dp(piece, mask) if mask else piece)
        shards[k] = pieces

    def swap(k):
        pieces = ordered(*shards[k])
        shards[k] = jnp.stack(pieces, axis=2)
        other[k] = over_core(shards[k])
        done(shards[k])

    def fetch(k):
        got = ordered(*[held[distance] for distance in distances[k]])
        for distance, rows_there in zip(distances[k], got):
            held[distance] = rows_there
        if k < last:
            hop(k + 1)
        got = jnp.stack(got)
        done(got)
        exchange(k, got)

    held[0] = jnp.stack([grad_out, tokens])
    hop(1)
    exchange(0, held[0][None])

    def forward(k):
        own, others = ordered(shards[k], other[k])
        sums = forward_partials(own, others, gate_weight, up_weight, down_weight)
        values = []
        for q in range(parts):
            value = sums[:, :, q * part : (q + 1) * part]
            values.append(value.reshape((3,) + (2,) * bits + (-1, part)))
        return values

    def send_halves(values, orders, s, lead):
        keep, fly = [], []
        for value, order in zip(values, orders):
            left = sorted(order[s:], reverse=True)
            axis = lead + left.index(order[s])
            keep.append(lax.index_in_dim(value, 0, axis, keepdims=False))
            fly.append(lax.index_in_dim(value, 1, axis, keepdims=False).astype(bf16))
        fly = [over_dp(x, 1 << order[s]) for x, order in zip(fly, orders)]
        return keep, fly

    def add_halves(keep, fly):
        got = ordered(*fly)
        return [x.astype(f32) + y.astype(f32) for x, y in zip(keep, got)]

    def gradients(sums):
        hiddens, values = [], []
        for g, u, h in sums:
            sig = jax.nn.sigmoid(g)
            silu = g * sig
            hiddens.append((silu * u).astype(bf16))
            gate_grad = (h * u * sig * (1.0 + g * (1.0 - sig))).astype(bf16)
            up_grad = (h * silu).astype(bf16)
            values.append(jnp.stack([gate_grad, up_grad]))
        return hiddens, values

    def join(values, got, s):
        joined = []
        for value, more, order in zip(values, got, orders):
            order = order[::-1]
            axis = sum(1 for bit in order[:s] if bit > order[s])
            joined.append(jnp.stack([value, more], axis=axis))
        return joined

    def step(k, s):
        if s < bits:
            values = forward(k) if s == 0 else add_halves(local[k], flying[k])
            local[k], flying[k] = send_halves(values, orders, s, 1)
            done(*values)
            return
        if s == bits:
            hiddens, values = gradients(add_halves(local[k], flying[k]))
            owns[k] = (hiddens, values)
            done(*hiddens, *values)
        else:
            values = join(local[k], ordered(*flying[k]), s - 1 - bits)
            done(*values)
        local[k] = values
        flying[k] = [
            over_dp(value, 1 << order[::-1][s - bits]) for value, order in zip(values, orders)
        ]

    def finish(k):
        got = ordered(*flying[k])
        count = 2 * len(distances[k]) * rows
        pieces, places = [], []
        for q in range(parts):
            order = orders[q][::-1]
            known = sorted(order[:-1], reverse=True)
            windows = [
                sum(bit << at for bit, at in zip(index, known)) for index in np.ndindex((2,) * (bits - 1))
            ]
            for here, arrived in enumerate((local[k][q], got[q])):
                pieces.append(arrived.reshape(-1, 2, count, part))
                starts = [(window | here << order[-1]) * count for window in windows]
                places.append((tuple(starts), q * part))
        out = backward_partials(pieces, tuple(places), gate_weight, up_weight)
        out = out.reshape(n_dp, len(distances[k]), 2, rows, width)
        send = out[:, :, 1].astype(bf16)
        out_flying[k] = (out[:, :, 0], over_core(send))
        done(send)

    def send_home(k):
        own, got = out_flying[k]
        (got,) = ordered(got)
        out = own + got.astype(f32)
        for place, distance in enumerate(distances[k]):
            term = out[:, place]
            if distance:
                term = term.astype(bf16)
                terms[distance] = over_z(term, -distance)
            else:
                terms[distance] = term
            done(term)

    def window_swap():
        places = [distance for chunk in distances for distance in chunk]
        own_raw["own"] = jnp.stack(ordered(*[held[place] for place in places]), axis=1)
        own_raw["other"] = over_core(own_raw["own"])
        done(own_raw["own"])

    def delta_terms():
        windows = ordered(own_raw["own"], own_raw["other"])
        chunks = range(last + 1)
        deltas = window_deltas(
            n_dp,
            units,
            me,
            block_kind,
            block_ff,
            block_d,
            block_owner[:, 0],
            list(windows),
            [piece for k in chunks for piece in owns[k][0]],
            [piece for k in chunks for piece in owns[k][1]],
        )
        done(deltas)
        deltas = deltas.reshape((n_dp, CAP, BLOCK, BLOCK))
        delta_send(deltas)

    def delta_send(values):
        half = values.shape[0] // 2
        local["delta"] = values[:half]
        flying["delta"] = over_dp(values[half:].astype(bf16), half)

    def delta_add():
        (got,) = ordered(flying["delta"])
        return local["delta"] + got.astype(f32)

    def delta_step():
        values = delta_add()
        done(values)
        delta_send(values)

    events = {}
    for k in range(last + 1):
        for s in range(stages):
            events["step", k, s] = (k + s, -k, functools.partial(step, k, s))
        events["swap", k] = (k - 1, 0.6 - k, functools.partial(swap, k))
        events["finish", k] = (k + stages, -k, functools.partial(finish, k))
        events["home", k] = (k + stages, 0.5 - k, functools.partial(send_home, k))
        if k:
            events["fetch", k] = (k - 2, 0.5 - k, functools.partial(fetch, k))
    events["window"] = (last + bits - 1, 99, window_swap)
    events["delta"] = (last + bits, 99, delta_terms)
    for s in range(1, bits):
        events["delta", s] = (last + stages, 50 + s, delta_step)
    if (n_z, bits) == (4, 2):
        listed = [("swap", 0), ("fetch", 1), ("step", 0, 0), ("swap", 1), ("fetch", 2)]
        listed += [("step", 1, 0), ("step", 0, 1), ("swap", 2), ("step", 2, 0), ("step", 1, 1)]
        listed += [("step", 0, 2), ("step", 2, 1), ("step", 1, 2), ("step", 0, 3), ("step", 2, 2)]
        listed += ["window", ("step", 1, 3), ("finish", 0), ("step", 2, 3), "delta", ("home", 0)]
        listed += [("finish", 1), ("finish", 2), ("home", 1), ("delta", 1), ("home", 2)]
    else:
        listed = sorted(events, key=lambda name: events[name][:2])
    for name in listed:
        events[name][2]()

    total = terms[0]
    for distance in ordered(*[terms[d] for d in terms if d]):
        total = total + distance.astype(f32)
    total = total.astype(bf16)
    pieces = [total[0]] + [over_dp(total[mask], mask) for mask in range(1, n_dp)]
    done(total)
    deltas = delta_add()[0]
    pieces = jnp.stack(pieces)
    slots = jnp.arange(n_dp, dtype=jnp.int32)
    grad_tokens = pieces.at[slots ^ me].get(mode="promise_in_bounds")
    grad_tokens = jnp.swapaxes(grad_tokens, 0, 1).reshape(rows, features)
    return (grad_tokens, deltas)


def solution(mesh):
    placed = (
        P(("groups", "dp", "tensor"), None),
        P(("groups", "dp", "tensor"), None),
        P("dp", "tensor"),
        P("dp", "tensor"),
        P("tensor", "dp"),
        P("tensor"),
        P("tensor"),
        P("tensor"),
        P("tensor", None),
    )
    return jax.shard_map(
        body,
        mesh=mesh,
        in_specs=placed,
        out_specs=(P(("groups", "dp", "tensor"), None), P(("groups", "dp", "tensor"), None, None)),
        check_vma=False,
    )
```

```python
import functools

import jax
import jax.numpy as jnp
from jax import lax
from jax.experimental import pallas as pl
from jax.experimental.pallas import tpu as pltpu
from jax.sharding import PartitionSpec as P

BLOCK = 128
CAP = 5
CONTRACT_LAST = (((1,), (1,)), ((), ()))
SMALL = pl.CostEstimate(flops=1, bytes_accessed=1, transcendentals=0)


def xor_perm(size, mask):
    return [(i, i ^ mask) for i in range(size)]


def z_perm(n_tensor, mask):
    return [(rank, rank ^ 2 * mask) for rank in range(n_tensor)]


def chunk_masks(n_z):
    chunks, size = [(0,)], 1
    while size < n_z:
        chunks.append(tuple(range(size, 2 * size)))
        size *= 2
    return chunks


def delta_kernel(n_dp, n_pieces, me_ref, kind_ref, ff_ref, col_ref, owner_ref, *refs):
    window_refs, refs = refs[:2], refs[2:]
    hidden_refs, grad_refs, refs = refs[:n_pieces], refs[n_pieces : 2 * n_pieces], refs[2 * n_pieces :]
    out_ref, grads_ref, tokens_ref, hidden_ref, gate_ref, up_ref, used_ref = refs
    me = me_ref[0]
    out_ref[...] = jnp.zeros_like(out_ref)
    for owner in range(n_dp):
        used_ref[owner] = 0

    start = 0
    _, chips, rows, _ = window_refs[0].shape
    for chip in range(chips):
        for window_ref in window_refs:
            grads_ref[start : start + rows] = window_ref[0, chip]
            tokens_ref[start : start + rows] = window_ref[1, chip]
            start += rows
    start, column = 0, 0
    for hidden_piece, grad_piece in zip(hidden_refs, grad_refs):
        rows, units = hidden_piece.shape
        place = (slice(start, start + rows), slice(column, column + units))
        hidden_ref[place] = hidden_piece[...]
        gate_ref[place] = grad_piece[0]
        up_ref[place] = grad_piece[1]
        column += units
        if column == hidden_ref.shape[1]:
            start, column = start + rows, 0

    def step(entry, carry):
        owner = owner_ref[entry]
        slot = used_ref[owner]
        used_ref[owner] = slot + 1
        kind = kind_ref[entry]
        units = pl.ds(pl.multiple_of(ff_ref[entry] * BLOCK, BLOCK), BLOCK)
        columns = pl.ds(pl.multiple_of(col_ref[entry] * BLOCK, BLOCK), BLOCK)
        left = jnp.where(kind == 2, hidden_ref[:, units], tokens_ref[:, columns])
        right = jnp.where(
            kind == 0,
            gate_ref[:, units],
            jnp.where(kind == 1, up_ref[:, units], grads_ref[:, columns]),
        )
        out_ref[(owner ^ me) * CAP + slot] = lax.dot_general(
            left, right, (((0,), (0,)), ((), ())), preferred_element_type=jnp.float32
        )
        return carry

    lax.fori_loop(0, kind_ref.shape[0], step, 0)


def window_deltas(n_dp, units, me, kind, ff, col, owner, windows, hiddens, grads):
    _, chips, rows, features = windows[0].shape
    total = 2 * chips * rows
    if rows % 16:
        joined = jnp.stack(windows, axis=2).reshape(2, 1, total, features)
        windows = [joined[:, :, : total // 2], joined[:, :, total // 2 :]]
        across = units // hiddens[0].shape[1]
        groups = range(0, len(hiddens), across)
        hiddens = [
            jnp.concatenate([jnp.concatenate(hiddens[i : i + across], axis=1) for i in groups])
        ]
        grads = [
            jnp.concatenate([jnp.concatenate(grads[i : i + across], axis=2) for i in groups], axis=1)
        ]
    smem, vmem = pl.BlockSpec(memory_space=pltpu.SMEM), pl.BlockSpec(memory_space=pltpu.VMEM)
    bf16 = jnp.bfloat16
    return pl.pallas_call(
        functools.partial(delta_kernel, n_dp, len(hiddens)),
        out_shape=jax.ShapeDtypeStruct((n_dp * CAP, BLOCK, BLOCK), jnp.float32),
        in_specs=[smem] * 5 + [vmem] * (2 + 2 * len(hiddens)),
        out_specs=vmem,
        scratch_shapes=[
            pltpu.VMEM((total, features), bf16),
            pltpu.VMEM((total, features), bf16),
            pltpu.VMEM((total, units), bf16),
            pltpu.VMEM((total, units), bf16),
            pltpu.VMEM((total, units), bf16),
            pltpu.SMEM((n_dp,), jnp.int32),
        ],
        compiler_params=pltpu.CompilerParams(vmem_limit_bytes=24 << 20),
        cost_estimate=SMALL,
    )(me.reshape(1), kind, ff, col, owner, *windows, *hiddens, *grads)


def body(
    tokens,
    grad_out,
    gate_weight,
    up_weight,
    down_weight,
    block_kind,
    block_ff,
    block_d,
    block_owner,
):
    n_dp, n_tensor = lax.axis_size("dp"), lax.axis_size("tensor")
    n_z = n_tensor // 2
    bits = n_dp.bit_length() - 1
    rows, features = tokens.shape
    width, units = gate_weight.shape
    me = lax.axis_index("dp")
    bf16, f32 = jnp.bfloat16, jnp.float32
    parts = min(bits, 2)
    part = units // parts
    orders = [[(q + s) % bits for s in range(bits)] for q in range(parts)]
    masks = chunk_masks(n_z)
    last = len(masks) - 1
    stages = 2 * bits

    chain = []

    def ordered(*values):
        if not chain:
            return values
        return lax.optimization_barrier(values + tuple(chain))[: len(values)]

    def done(*results):
        chain[:] = results

    def over_dp(value, mask):
        return lax.ppermute(value, "dp", xor_perm(n_dp, mask))

    def over_core(value):
        return lax.ppermute(value, "tensor", xor_perm(n_tensor, 1))

    def over_z(value, mask):
        return lax.ppermute(value, "tensor", z_perm(n_tensor, mask))

    held, shards, other, own_raw = {}, {}, {}, {}
    ready, flying, local, owns, out_flying, terms = {}, {}, {}, {}, {}, {}

    def hop(mask):
        low = mask & -mask
        held[mask] = over_z(held[mask ^ low], low)

    def relay(k):
        first = masks[k][0]
        (held[first],) = ordered(held[first])
        for mask in masks[k][1:]:
            hop(mask)
        done(held[first])
        if k < last:
            hop(masks[k + 1][0])

    def exchange(k, rows_there):
        pieces = []
        for mask in range(n_dp):
            piece = lax.dynamic_slice_in_dim(rows_there, (me ^ mask) * width, width, axis=3)
            pieces.append(over_dp(piece, mask) if mask else piece)
        shards[k] = pieces

    def swap(k):
        pieces = ordered(*shards[k])
        shards[k] = jnp.stack(pieces, axis=2)
        other[k] = over_core(shards[k])
        done(shards[k])

    def fetch(k):
        got = ordered(*[held[mask] for mask in masks[k]])
        for mask, rows_there in zip(masks[k], got):
            held[mask] = rows_there
        got = jnp.stack(got)
        done(got)
        exchange(k, got)

    held[0] = jnp.stack([grad_out, tokens])
    exchange(0, held[0][None])
    for mask in masks[1] + masks[2][:1]:
        hop(mask)

    def forward(k):
        own, others = ordered(shards[k], other[k])
        chunk = jnp.stack([own, others], axis=3).transpose(1, 2, 0, 3, 4, 5)
        chunk = chunk.reshape(2, -1, width)
        gate = jnp.dot(chunk[1], gate_weight, preferred_element_type=f32).astype(bf16)
        upward = jnp.dot(chunk[1], up_weight, preferred_element_type=f32).astype(bf16)
        hidden_grad = lax.dot_general(
            chunk[0], down_weight, CONTRACT_LAST, preferred_element_type=f32
        ).astype(bf16)
        values = []
        for q in range(parts):
            cut = slice(q * part, (q + 1) * part)
            value = jnp.stack([gate[:, cut], upward[:, cut], hidden_grad[:, cut]])
            values.append(value.reshape((3,) + (2,) * bits + (-1, part)))
        ready[k] = values
        done(*values)

    def add_halves(keep, fly):
        got = ordered(*fly)
        return [x.astype(f32) + y.astype(f32) for x, y in zip(keep, got)]

    def gradients(sums):
        hiddens, values = [], []
        for g, u, h in sums:
            sig = jax.nn.sigmoid(g)
            silu = g * sig
            hiddens.append((silu * u).astype(bf16))
            gate_grad = (h * u * sig * (1.0 + g * (1.0 - sig))).astype(bf16)
            up_grad = (h * silu).astype(bf16)
            values.append(jnp.stack([gate_grad, up_grad]))
        return hiddens, values

    def join(values, got, s):
        joined = []
        for value, more, order in zip(values, got, orders):
            order = order[::-1]
            axis = sum(1 for bit in order[:s] if bit > order[s])
            joined.append(jnp.stack([value, more], axis=axis))
        return joined

    def send(k, s):
        values = ordered(*ready[k])
        if s >= bits:
            local[k] = values
            flying[k] = [
                over_dp(value, 1 << order[::-1][s - bits]) for value, order in zip(values, orders)
            ]
            return
        local[k], fly = [], []
        for value, order in zip(values, orders):
            axis = (k != "delta") + sorted(order[s:], reverse=True).index(order[s])
            local[k].append(lax.index_in_dim(value, 0, axis, keepdims=False))
            fly.append(lax.index_in_dim(value, 1, axis, keepdims=False).astype(bf16))
        flying[k] = [over_dp(x, 1 << order[s]) for x, order in zip(fly, orders)]

    def take(k, s):
        if s < bits:
            values = add_halves(local[k], flying[k])
            if k == "delta":
                ready[k] = values
                done(*values)
                return
        else:
            values = join(local[k], ordered(*flying[k]), s - bits)
        if s == bits - 1:
            hiddens, values = gradients(values)
            owns[k] = (hiddens, values)
            done(*hiddens, *values)
        else:
            done(*values)
        ready[k] = values

    def merge(*chunks):
        ready[chunks] = [
            jnp.concatenate(values, axis=-2) for values in zip(*[ready[k] for k in chunks])
        ]

    def split(*chunks):
        start = 0
        for k in chunks:
            count = 2 * len(masks[k]) * rows
            ready[k] = [
                lax.slice_in_dim(x, start, start + count, axis=x.ndim - 2) for x in ready[chunks]
            ]
            start += count

    def finish(k):
        values = join(local[k], ordered(*flying[k]), bits - 1)
        gathered = []
        for value in values:
            value = value.reshape((n_dp, 2, -1, part))
            gathered.append(jnp.swapaxes(value, 0, 1).reshape(2, -1, part))
        gathered = jnp.concatenate(gathered, axis=2)
        out = lax.dot_general(gathered[0], gate_weight, CONTRACT_LAST, preferred_element_type=f32)
        out = out + lax.dot_general(
            gathered[1], up_weight, CONTRACT_LAST, preferred_element_type=f32
        )
        out = out.reshape(n_dp, len(masks[k]), 2, rows, width)
        send = out[:, :, 1].astype(bf16)
        out_flying[k] = (out[:, :, 0], over_core(send))
        done(send)

    def send_home(k):
        own, got = out_flying[k]
        (got,) = ordered(got)
        out = own + got.astype(f32)
        for place, mask in enumerate(masks[k]):
            term = out[:, place]
            if mask:
                term = term.astype(bf16)
                terms[mask] = over_z(term, mask)
            else:
                terms[mask] = term
            done(term)

    def window_swap():
        rows_there = [held[mask] for chunk in masks for mask in chunk]
        own_raw["own"] = jnp.stack(ordered(*rows_there), axis=1)
        own_raw["other"] = over_core(own_raw["own"])
        done(own_raw["own"])

    def delta_terms():
        windows = ordered(own_raw["own"], own_raw["other"])
        chunks = range(last + 1)
        deltas = window_deltas(
            n_dp,
            units,
            me,
            block_kind,
            block_ff,
            block_d,
            block_owner[:, 0],
            list(windows),
            [piece for k in chunks for piece in owns[k][0]],
            [piece for k in chunks for piece in owns[k][1]],
        )
        done(deltas)
        deltas = deltas.reshape((2,) * bits + (CAP, BLOCK, BLOCK))
        cut = BLOCK // parts
        ready["delta"] = [deltas[..., q * cut : (q + 1) * cut, :] for q in range(parts)]

    def run(*steps):
        for name, *args in steps:
            plan[name](*args)

    plan = {
        "swap": swap, "fetch": fetch, "relay": relay, "forward": forward,
        "send": send, "take": take, "merge": merge, "split": split,
        "finish": finish, "home": send_home, "window": window_swap, "delta": delta_terms,
    }
    if (n_z, bits) == (4, 2):
        run(("swap", 0), ("fetch", 1), ("forward", 0), ("send", 0, 0), ("relay", 2))
        run(("swap", 1), ("forward", 1), ("send", 1, 0), ("fetch", 2))
        run(("take", 0, 0), ("send", 0, 1), ("swap", 2))
        run(("take", 1, 0), ("send", 1, 1))
        run(("forward", 2), ("send", 2, 0))
        run(("take", 0, 1), ("take", 1, 1), ("merge", 0, 1), ("send", (0, 1), 2))
        run(("take", 2, 0), ("send", 2, 1), ("window",))
        run(("take", (0, 1), 2), ("split", 0, 1), ("send", 1, 3))
        run(("take", 2, 1), ("send", 2, 2), ("delta",))
        run(("finish", 1), ("send", "delta", 0))
        run(("take", 2, 2), ("send", 2, 3), ("home", 1))
        run(("take", "delta", 0), ("send", 0, 3))
        run(("finish", 2), ("send", "delta", 1), ("home", 2), ("finish", 0), ("home", 0))
    else:
        for k in range(2, last + 1):
            run(("relay", k))
        sends = [(k + s, -k, s) for k in range(last + 1) for s in range(stages)]
        for _, k, s in sorted(sends):
            k = -k
            if s:
                run(("take", k, s - 1))
            elif k:
                run(("fetch", k), ("swap", k), ("forward", k))
            else:
                run(("swap", k), ("forward", k))
            run(("send", k, s))
        run(("window",), ("delta",), ("send", "delta", 0))
        for s in range(1, bits):
            run(("take", "delta", s - 1), ("send", "delta", s))
        for k in range(last, -1, -1):
            run(("finish", k), ("home", k))

    total = terms[0]
    for term in ordered(*[terms[mask] for mask in terms if mask]):
        total = total + term.astype(f32)
    total = total.astype(bf16)
    pieces = [total[0]] + [over_dp(total[mask], mask) for mask in range(1, n_dp)]
    done(total)
    take("delta", bits - 1)
    deltas = jnp.concatenate(ready["delta"], axis=1)
    pieces = jnp.stack(pieces)
    slots = jnp.arange(n_dp, dtype=jnp.int32)
    grad_tokens = pieces.at[slots ^ me].get(mode="promise_in_bounds")
    grad_tokens = jnp.swapaxes(grad_tokens, 0, 1).reshape(rows, features)
    return (grad_tokens, deltas)


def solution(mesh):
    placed = (
        P(("groups", "dp", "tensor"), None),
        P(("groups", "dp", "tensor"), None),
        P("dp", "tensor"),
        P("dp", "tensor"),
        P("tensor", "dp"),
        P("tensor"),
        P("tensor"),
        P("tensor"),
        P("tensor", None),
    )
    return jax.shard_map(
        body,
        mesh=mesh,
        in_specs=placed,
        out_specs=(P(("groups", "dp", "tensor"), None), P(("groups", "dp", "tensor"), None, None)),
        check_vma=False,
    )
```

```python
import functools

import jax
import jax.numpy as jnp
from jax import lax
from jax.experimental import pallas as pl
from jax.experimental.pallas import tpu as pltpu
from jax.sharding import PartitionSpec as P

BLOCK = 128
CAP = 5
CONTRACT_LAST = (((1,), (1,)), ((), ()))
SMALL = pl.CostEstimate(flops=1, bytes_accessed=1, transcendentals=0)


def xor_perm(size, mask):
    return [(i, i ^ mask) for i in range(size)]


def z_perm(n_tensor, mask):
    return [(rank, rank ^ 2 * mask) for rank in range(n_tensor)]


def chunk_masks(n_z):
    return [tuple(range(n_z // 2)), tuple(range(n_z // 2, n_z))]


def delta_kernel(n_dp, n_pieces, me_ref, kind_ref, ff_ref, col_ref, owner_ref, *refs):
    window_refs, refs = refs[:2], refs[2:]
    hidden_refs, grad_refs, refs = refs[:n_pieces], refs[n_pieces : 2 * n_pieces], refs[2 * n_pieces :]
    out_ref, grads_ref, tokens_ref, hidden_ref, gate_ref, up_ref, used_ref = refs
    me = me_ref[0]
    out_ref[...] = jnp.zeros_like(out_ref)
    for owner in range(n_dp):
        used_ref[owner] = 0

    start = 0
    _, chips, rows, _ = window_refs[0].shape
    for chip in range(chips):
        for window_ref in window_refs:
            grads_ref[start : start + rows] = window_ref[0, chip]
            tokens_ref[start : start + rows] = window_ref[1, chip]
            start += rows
    start, column = 0, 0
    for hidden_piece, grad_piece in zip(hidden_refs, grad_refs):
        rows, units = hidden_piece.shape
        place = (slice(start, start + rows), slice(column, column + units))
        hidden_ref[place] = hidden_piece[...]
        gate_ref[place] = grad_piece[0]
        up_ref[place] = grad_piece[1]
        column += units
        if column == hidden_ref.shape[1]:
            start, column = start + rows, 0

    def step(entry, carry):
        owner = owner_ref[entry]
        slot = used_ref[owner]
        used_ref[owner] = slot + 1
        kind = kind_ref[entry]
        units = pl.ds(pl.multiple_of(ff_ref[entry] * BLOCK, BLOCK), BLOCK)
        columns = pl.ds(pl.multiple_of(col_ref[entry] * BLOCK, BLOCK), BLOCK)
        left = jnp.where(kind == 2, hidden_ref[:, units], tokens_ref[:, columns])
        right = jnp.where(
            kind == 0,
            gate_ref[:, units],
            jnp.where(kind == 1, up_ref[:, units], grads_ref[:, columns]),
        )
        out_ref[(owner ^ me) * CAP + slot] = lax.dot_general(
            left, right, (((0,), (0,)), ((), ())), preferred_element_type=jnp.float32
        )
        return carry

    lax.fori_loop(0, kind_ref.shape[0], step, 0)


def window_deltas(n_dp, units, me, kind, ff, col, owner, windows, hiddens, grads):
    _, chips, rows, features = windows[0].shape
    total = 2 * chips * rows
    if rows % 16:
        joined = jnp.stack(windows, axis=2).reshape(2, 1, total, features)
        windows = [joined[:, :, : total // 2], joined[:, :, total // 2 :]]
        across = units // hiddens[0].shape[1]
        groups = range(0, len(hiddens), across)
        hiddens = [
            jnp.concatenate([jnp.concatenate(hiddens[i : i + across], axis=1) for i in groups])
        ]
        grads = [
            jnp.concatenate([jnp.concatenate(grads[i : i + across], axis=2) for i in groups], axis=1)
        ]
    smem, vmem = pl.BlockSpec(memory_space=pltpu.SMEM), pl.BlockSpec(memory_space=pltpu.VMEM)
    bf16 = jnp.bfloat16
    return pl.pallas_call(
        functools.partial(delta_kernel, n_dp, len(hiddens)),
        out_shape=jax.ShapeDtypeStruct((n_dp * CAP, BLOCK, BLOCK), jnp.float32),
        in_specs=[smem] * 5 + [vmem] * (2 + 2 * len(hiddens)),
        out_specs=vmem,
        scratch_shapes=[
            pltpu.VMEM((total, features), bf16),
            pltpu.VMEM((total, features), bf16),
            pltpu.VMEM((total, units), bf16),
            pltpu.VMEM((total, units), bf16),
            pltpu.VMEM((total, units), bf16),
            pltpu.SMEM((n_dp,), jnp.int32),
        ],
        compiler_params=pltpu.CompilerParams(vmem_limit_bytes=24 << 20),
        cost_estimate=SMALL,
    )(me.reshape(1), kind, ff, col, owner, *windows, *hiddens, *grads)


def body(
    tokens,
    grad_out,
    gate_weight,
    up_weight,
    down_weight,
    block_kind,
    block_ff,
    block_d,
    block_owner,
):
    n_dp, n_tensor = lax.axis_size("dp"), lax.axis_size("tensor")
    n_z = n_tensor // 2
    bits = n_dp.bit_length() - 1
    rows, features = tokens.shape
    width, units = gate_weight.shape
    me = lax.axis_index("dp")
    bf16, f32 = jnp.bfloat16, jnp.float32
    parts = min(bits, 2)
    part = units // parts
    orders = [[(q + s) % bits for s in range(bits)] for q in range(parts)]
    masks = chunk_masks(n_z)
    last = len(masks) - 1
    stages = 2 * bits

    chain = []

    def ordered(*values):
        if not chain:
            return values
        return lax.optimization_barrier(values + tuple(chain))[: len(values)]

    def done(*results):
        chain[:] = results

    def over_dp(value, mask):
        return lax.ppermute(value, "dp", xor_perm(n_dp, mask))

    def over_core(value):
        return lax.ppermute(value, "tensor", xor_perm(n_tensor, 1))

    def over_z(value, mask):
        return lax.ppermute(value, "tensor", z_perm(n_tensor, mask))

    held, window_held, shards, other = {}, {}, {}, {}
    ready, flying, local, owns, out_flying, terms = {}, {}, {}, {}, {}, {}

    def hop(held, mask):
        low = mask & -mask
        held[mask] = over_z(held[mask ^ low], low)

    def relay(held, mask):
        (held[mask],) = ordered(held[mask])
        low = mask & -mask if mask else n_z
        for step in range(low.bit_length() - 1):
            hop(held, mask | 1 << step)

    def swap(k):
        got = ordered(*[held[mask] for mask in masks[k]])
        shards[k] = jnp.stack(got)
        other[k] = over_core(shards[k])
        done(shards[k])

    pieces = []
    for mask in range(n_dp):
        start = (me ^ mask) * width
        piece = jnp.stack(
            [lax.dynamic_slice_in_dim(x, start, width, axis=1) for x in (grad_out, tokens)]
        )
        pieces.append(over_dp(piece, mask) if mask else piece)
    held[0] = jnp.stack(pieces, axis=1)
    relay(held, 0)

    def forward(k):
        own, others = ordered(shards[k], other[k])
        chunk = jnp.stack([own, others], axis=3).transpose(1, 2, 0, 3, 4, 5)
        chunk = chunk.reshape(2, -1, width)
        gate = jnp.dot(chunk[1], gate_weight, preferred_element_type=f32).astype(bf16)
        upward = jnp.dot(chunk[1], up_weight, preferred_element_type=f32).astype(bf16)
        hidden_grad = lax.dot_general(
            chunk[0], down_weight, CONTRACT_LAST, preferred_element_type=f32
        ).astype(bf16)
        values = []
        for q in range(parts):
            cut = slice(q * part, (q + 1) * part)
            value = jnp.stack([gate[:, cut], upward[:, cut], hidden_grad[:, cut]])
            values.append(value.reshape((3,) + (2,) * bits + (-1, part)))
        ready[k] = values
        done(*values)

    def add_halves(keep, fly):
        got = ordered(*fly)
        return [x.astype(f32) + y.astype(f32) for x, y in zip(keep, got)]

    def gradients(sums):
        hiddens, values = [], []
        for g, u, h in sums:
            sig = jax.nn.sigmoid(g)
            silu = g * sig
            hiddens.append((silu * u).astype(bf16))
            gate_grad = (h * u * sig * (1.0 + g * (1.0 - sig))).astype(bf16)
            up_grad = (h * silu).astype(bf16)
            values.append(jnp.stack([gate_grad, up_grad]))
        return hiddens, values

    def join(values, got, s):
        joined = []
        for value, more, order in zip(values, got, orders):
            order = order[::-1]
            axis = sum(1 for bit in order[:s] if bit > order[s])
            joined.append(jnp.stack([value, more], axis=axis))
        return joined

    def send(k, s):
        values = ordered(*ready[k])
        if s >= bits:
            local[k] = values
            flying[k] = [
                over_dp(value, 1 << order[::-1][s - bits]) for value, order in zip(values, orders)
            ]
            return
        local[k], fly = [], []
        for value, order in zip(values, orders):
            axis = (k != "delta") + sorted(order[s:], reverse=True).index(order[s])
            local[k].append(lax.index_in_dim(value, 0, axis, keepdims=False))
            fly.append(lax.index_in_dim(value, 1, axis, keepdims=False).astype(bf16))
        flying[k] = [over_dp(x, 1 << order[s]) for x, order in zip(fly, orders)]

    def take(k, s):
        if s < bits:
            values = add_halves(local[k], flying[k])
            if k == "delta":
                ready[k] = values
                done(*values)
                return
        else:
            values = join(local[k], ordered(*flying[k]), s - bits)
        if s == bits - 1:
            hiddens, values = gradients(values)
            owns[k] = (hiddens, values)
            done(*hiddens, *values)
        else:
            done(*values)
        ready[k] = values

    def finish(k):
        values = join(local[k], ordered(*flying[k]), bits - 1)
        gathered = []
        for value in values:
            value = value.reshape((n_dp, 2, -1, part))
            gathered.append(jnp.swapaxes(value, 0, 1).reshape(2, -1, part))
        gathered = jnp.concatenate(gathered, axis=2)
        out = lax.dot_general(gathered[0], gate_weight, CONTRACT_LAST, preferred_element_type=f32)
        out = out + lax.dot_general(
            gathered[1], up_weight, CONTRACT_LAST, preferred_element_type=f32
        )
        out = out.reshape(n_dp, len(masks[k]), 2, rows, width)
        send = out[:, :, 1].astype(bf16)
        out_flying[k] = (out[:, :, 0], over_core(send))
        done(send)

    def send_home(k):
        own, got = out_flying[k]
        (got,) = ordered(got)
        out = own + got.astype(f32)
        for place, mask in enumerate(masks[k]):
            term = out[:, place]
            if mask:
                term = term.astype(bf16)
                terms[mask] = over_z(term, mask)
            else:
                terms[mask] = term
            done(term)

    def window_rows(mask):
        if mask == 0:
            window_held[0] = jnp.stack([grad_out, tokens])
        if mask < n_z:
            relay(window_held, mask)
            return
        rows_there = [window_held[mask] for chunk in masks for mask in chunk]
        window_held["own"] = jnp.stack(ordered(*rows_there), axis=1)
        window_held["other"] = over_core(window_held["own"])
        done(window_held["own"])

    def delta_terms():
        windows = ordered(window_held["own"], window_held["other"])
        chunks = range(last + 1)
        deltas = window_deltas(
            n_dp,
            units,
            me,
            block_kind,
            block_ff,
            block_d,
            block_owner[:, 0],
            list(windows),
            [piece for k in chunks for piece in owns[k][0]],
            [piece for k in chunks for piece in owns[k][1]],
        )
        done(deltas)
        deltas = deltas.reshape((2,) * bits + (CAP, BLOCK, BLOCK))
        cut = BLOCK // parts
        ready["delta"] = [deltas[..., q * cut : (q + 1) * cut, :] for q in range(parts)]

    for mask in range(1, n_z // 2):
        relay(held, mask)
    swap(0)
    forward(0)
    send(0, 0)
    for mask in range(n_z // 2, n_z):
        relay(held, mask)
    swap(1)
    take(0, 0)
    send(0, 1)
    forward(1)
    send(1, 0)
    hops = iter(range(n_z))
    for s in range(2, stages - 1):
        window_rows(next(hops))
        take(0, s - 1)
        send(0, s)
        window_rows(next(hops))
        take(1, s - 2)
        send(1, s - 1)
    for mask in hops:
        window_rows(mask)
    take(0, stages - 2)
    window_rows(n_z)
    take(1, stages - 3)
    send(1, stages - 2)
    delta_terms()
    send("delta", 0)
    take(1, stages - 2)
    send(1, stages - 1)
    for s in range(1, bits):
        take("delta", s - 1)
        if s == 1:
            send(0, stages - 1)
            finish(1)
            send_home(1)
        send("delta", s)
    finish(0)
    send_home(0)

    total = terms[0]
    for term in ordered(*[terms[mask] for mask in terms if mask]):
        total = total + term.astype(f32)
    total = total.astype(bf16)
    pieces = [total[0]] + [over_dp(total[mask], mask) for mask in range(1, n_dp)]
    done(total)
    take("delta", bits - 1)
    deltas = jnp.concatenate(ready["delta"], axis=1)
    pieces = jnp.stack(pieces)
    slots = jnp.arange(n_dp, dtype=jnp.int32)
    grad_tokens = pieces.at[slots ^ me].get(mode="promise_in_bounds")
    grad_tokens = jnp.swapaxes(grad_tokens, 0, 1).reshape(rows, features)
    return (grad_tokens, deltas)


def solution(mesh):
    placed = (
        P(("groups", "dp", "tensor"), None),
        P(("groups", "dp", "tensor"), None),
        P("dp", "tensor"),
        P("dp", "tensor"),
        P("tensor", "dp"),
        P("tensor"),
        P("tensor"),
        P("tensor"),
        P("tensor", None),
    )
    return jax.shard_map(
        body,
        mesh=mesh,
        in_specs=placed,
        out_specs=(P(("groups", "dp", "tensor"), None), P(("groups", "dp", "tensor"), None, None)),
        check_vma=False,
    )
```

```python
import functools

import jax
import jax.numpy as jnp
from jax import lax
from jax.experimental import pallas as pl
from jax.experimental.pallas import tpu as pltpu
from jax.sharding import PartitionSpec as P

BLOCK = 128
CAP = 5
CONTRACT_LAST = (((1,), (1,)), ((), ()))
SMALL = pl.CostEstimate(flops=1, bytes_accessed=1, transcendentals=0)


def xor_perm(size, mask):
    return [(i, i ^ mask) for i in range(size)]


def z_perm(n_tensor, mask):
    return [(rank, rank ^ 2 * mask) for rank in range(n_tensor)]


def chunk_masks(n_z):
    low, high = tuple(range(n_z // 2)), tuple(range(n_z // 2, n_z))
    return {"own": low[:1], "near": low[1:], 0: low, 1: high}


def delta_kernel(n_dp, n_pieces, me_ref, kind_ref, ff_ref, col_ref, owner_ref, *refs):
    window_refs, refs = refs[:2], refs[2:]
    hidden_refs, grad_refs, refs = refs[:n_pieces], refs[n_pieces : 2 * n_pieces], refs[2 * n_pieces :]
    out_ref, grads_ref, tokens_ref, hidden_ref, gate_ref, up_ref, used_ref = refs
    me = me_ref[0]
    out_ref[...] = jnp.zeros_like(out_ref)
    for owner in range(n_dp):
        used_ref[owner] = 0

    start = 0
    _, chips, rows, _ = window_refs[0].shape
    for chip in range(chips):
        for window_ref in window_refs:
            grads_ref[start : start + rows] = window_ref[0, chip]
            tokens_ref[start : start + rows] = window_ref[1, chip]
            start += rows
    start, column = 0, 0
    for hidden_piece, grad_piece in zip(hidden_refs, grad_refs):
        rows, units = hidden_piece.shape
        place = (slice(start, start + rows), slice(column, column + units))
        hidden_ref[place] = hidden_piece[...]
        gate_ref[place] = grad_piece[0]
        up_ref[place] = grad_piece[1]
        column += units
        if column == hidden_ref.shape[1]:
            start, column = start + rows, 0

    def step(entry, carry):
        owner = owner_ref[entry]
        slot = used_ref[owner]
        used_ref[owner] = slot + 1
        kind = kind_ref[entry]
        units = pl.ds(pl.multiple_of(ff_ref[entry] * BLOCK, BLOCK), BLOCK)
        columns = pl.ds(pl.multiple_of(col_ref[entry] * BLOCK, BLOCK), BLOCK)
        left = jnp.where(kind == 2, hidden_ref[:, units], tokens_ref[:, columns])
        right = jnp.where(
            kind == 0,
            gate_ref[:, units],
            jnp.where(kind == 1, up_ref[:, units], grads_ref[:, columns]),
        )
        out_ref[(owner ^ me) * CAP + slot] = lax.dot_general(
            left, right, (((0,), (0,)), ((), ())), preferred_element_type=jnp.float32
        )
        return carry

    lax.fori_loop(0, kind_ref.shape[0], step, 0)


def window_deltas(n_dp, units, me, kind, ff, col, owner, windows, hiddens, grads):
    _, chips, rows, features = windows[0].shape
    total = 2 * chips * rows
    if rows % 16:
        joined = jnp.stack(windows, axis=2).reshape(2, 1, total, features)
        windows = [joined[:, :, : total // 2], joined[:, :, total // 2 :]]
        across = units // hiddens[0].shape[1]
        groups = range(0, len(hiddens), across)
        hiddens = [
            jnp.concatenate([jnp.concatenate(hiddens[i : i + across], axis=1) for i in groups])
        ]
        grads = [
            jnp.concatenate([jnp.concatenate(grads[i : i + across], axis=2) for i in groups], axis=1)
        ]
    smem, vmem = pl.BlockSpec(memory_space=pltpu.SMEM), pl.BlockSpec(memory_space=pltpu.VMEM)
    bf16 = jnp.bfloat16
    return pl.pallas_call(
        functools.partial(delta_kernel, n_dp, len(hiddens)),
        out_shape=jax.ShapeDtypeStruct((n_dp * CAP, BLOCK, BLOCK), jnp.float32),
        in_specs=[smem] * 5 + [vmem] * (2 + 2 * len(hiddens)),
        out_specs=vmem,
        scratch_shapes=[
            pltpu.VMEM((total, features), bf16),
            pltpu.VMEM((total, features), bf16),
            pltpu.VMEM((total, units), bf16),
            pltpu.VMEM((total, units), bf16),
            pltpu.VMEM((total, units), bf16),
            pltpu.SMEM((n_dp,), jnp.int32),
        ],
        compiler_params=pltpu.CompilerParams(vmem_limit_bytes=24 << 20),
        cost_estimate=SMALL,
    )(me.reshape(1), kind, ff, col, owner, *windows, *hiddens, *grads)


def forward_kernel(own_ref, other_ref, gate_ref, up_ref, down_ref, out_ref, chunk_ref):
    f32 = jnp.float32

    @pl.when(pl.program_id(0) == 0)
    def _():
        start = 0
        chips, _, windows, rows, _ = own_ref.shape
        for window in range(windows):
            for chip in range(chips):
                for ref in (own_ref, other_ref):
                    chunk_ref[:, start : start + rows] = ref[chip, :, window]
                    start += rows

    tokens = chunk_ref[1]
    gate = jnp.dot(tokens, gate_ref[...], preferred_element_type=f32)
    out_ref[0] = gate.astype(out_ref.dtype)
    upward = jnp.dot(tokens, up_ref[...], preferred_element_type=f32)
    out_ref[1] = upward.astype(out_ref.dtype)
    hidden_grad = lax.dot_general(
        chunk_ref[0], down_ref[...], CONTRACT_LAST, preferred_element_type=f32
    )
    out_ref[2] = hidden_grad.astype(out_ref.dtype)


def forward_partials(own, other, gate_weight, up_weight, down_weight):
    chips, _, windows, rows, width = own.shape
    units = gate_weight.shape[1]
    total = 2 * chips * windows * rows
    if rows % 16:
        joined = jnp.stack([own, other], axis=3).transpose(1, 2, 0, 3, 4, 5)
        joined = joined.reshape(1, 2, 1, total, width)
        own, other = joined[..., : total // 2, :], joined[..., total // 2 :, :]
    block = min(units, 512)
    whole = pl.BlockSpec(own.shape, lambda j: (0, 0, 0, 0, 0))
    return pl.pallas_call(
        forward_kernel,
        grid=(units // block,),
        out_shape=jax.ShapeDtypeStruct((3, total, units), jnp.bfloat16),
        in_specs=[
            whole,
            whole,
            pl.BlockSpec((width, block), lambda j: (0, j)),
            pl.BlockSpec((width, block), lambda j: (0, j)),
            pl.BlockSpec((block, width), lambda j: (j, 0)),
        ],
        out_specs=pl.BlockSpec((3, total, block), lambda j: (0, 0, j)),
        scratch_shapes=[pltpu.VMEM((2, total, width), jnp.bfloat16)],
        compiler_params=pltpu.CompilerParams(vmem_limit_bytes=24 << 20),
        cost_estimate=SMALL,
    )(own, other, gate_weight, up_weight, down_weight)


def body(
    tokens,
    grad_out,
    gate_weight,
    up_weight,
    down_weight,
    block_kind,
    block_ff,
    block_d,
    block_owner,
):
    n_dp, n_tensor = lax.axis_size("dp"), lax.axis_size("tensor")
    n_z = n_tensor // 2
    bits = n_dp.bit_length() - 1
    rows, features = tokens.shape
    width, units = gate_weight.shape
    me = lax.axis_index("dp")
    bf16, f32 = jnp.bfloat16, jnp.float32
    parts = min(bits, 2)
    part = units // parts
    orders = [[(q + s) % bits for s in range(bits)] for q in range(parts)]
    masks = chunk_masks(n_z)
    stages = 2 * bits

    chain = []

    def ordered(*values):
        if not chain:
            return values
        return lax.optimization_barrier(values + tuple(chain))[: len(values)]

    def done(*results):
        chain[:] = results

    def over_dp(value, mask):
        return lax.ppermute(value, "dp", xor_perm(n_dp, mask))

    def over_core(value):
        return lax.ppermute(value, "tensor", xor_perm(n_tensor, 1))

    def over_z(value, mask):
        return lax.ppermute(value, "tensor", z_perm(n_tensor, mask))

    held, window_held, shards, other = {}, {}, {}, {}
    ready, flying, local, owns, out_flying, terms = {}, {}, {}, {}, {}, {}

    def hop(held, mask):
        low = mask & -mask
        held[mask] = over_z(held[mask ^ low], low)

    def relay(held, mask):
        (held[mask],) = ordered(held[mask])
        low = mask & -mask if mask else n_z
        for step in range(low.bit_length() - 1):
            hop(held, mask | 1 << step)

    def swap(k):
        got = ordered(*[held[mask] for mask in masks[k]])
        shards[k] = jnp.stack(got)
        other[k] = over_core(shards[k])
        done(shards[k])

    pieces = []
    for mask in range(n_dp):
        start = (me ^ mask) * width
        piece = jnp.stack(
            [lax.dynamic_slice_in_dim(x, start, width, axis=1) for x in (grad_out, tokens)]
        )
        pieces.append(over_dp(piece, mask) if mask else piece)
    held[0] = jnp.stack(pieces, axis=1)
    relay(held, 0)

    def forward(k):
        own, others = ordered(shards[k], other[k])
        if k == 1:
            sums = forward_partials(own, others, gate_weight, up_weight, down_weight)
        else:
            chunk = jnp.stack([own, others], axis=3).transpose(1, 2, 0, 3, 4, 5)
            chunk = chunk.reshape(2, -1, width)
            gate = jnp.dot(chunk[1], gate_weight, preferred_element_type=f32).astype(bf16)
            upward = jnp.dot(chunk[1], up_weight, preferred_element_type=f32).astype(bf16)
            hidden_grad = lax.dot_general(
                chunk[0], down_weight, CONTRACT_LAST, preferred_element_type=f32
            ).astype(bf16)
            sums = jnp.stack([gate, upward, hidden_grad])
        values = []
        for q in range(parts):
            value = sums[:, :, q * part : (q + 1) * part]
            values.append(value.reshape((3,) + (2,) * bits + (-1, part)))
        ready[k] = values
        done(*values)

    def add_halves(keep, fly):
        got = ordered(*fly)
        return [x.astype(f32) + y.astype(f32) for x, y in zip(keep, got)]

    def gradients(sums):
        hiddens, values = [], []
        for g, u, h in sums:
            sig = jax.nn.sigmoid(g)
            silu = g * sig
            hiddens.append((silu * u).astype(bf16))
            gate_grad = (h * u * sig * (1.0 + g * (1.0 - sig))).astype(bf16)
            up_grad = (h * silu).astype(bf16)
            values.append(jnp.stack([gate_grad, up_grad]))
        return hiddens, values

    def join(values, got, s):
        joined = []
        for value, more, order in zip(values, got, orders):
            order = order[::-1]
            axis = sum(1 for bit in order[:s] if bit > order[s])
            joined.append(jnp.stack([value, more], axis=axis))
        return joined

    def send(k, s):
        values = ordered(*ready[k])
        if s >= bits:
            local[k] = values
            flying[k] = [
                over_dp(value, 1 << order[::-1][s - bits]) for value, order in zip(values, orders)
            ]
            return
        local[k], fly = [], []
        for value, order in zip(values, orders):
            axis = (k != "delta") + sorted(order[s:], reverse=True).index(order[s])
            local[k].append(lax.index_in_dim(value, 0, axis, keepdims=False))
            fly.append(lax.index_in_dim(value, 1, axis, keepdims=False).astype(bf16))
        flying[k] = [over_dp(x, 1 << order[s]) for x, order in zip(fly, orders)]

    def take(k, s):
        if s < bits:
            values = add_halves(local[k], flying[k])
            if k == "delta":
                ready[k] = values
                done(*values)
                return
        else:
            values = join(local[k], ordered(*flying[k]), s - bits)
        if s == bits - 1:
            hiddens, values = gradients(values)
            owns[k] = (hiddens, values)
            done(*hiddens, *values)
        else:
            done(*values)
        ready[k] = values

    def merge():
        ready[0] = [
            jnp.concatenate(values, axis=-2) for values in zip(ready["own"], ready["near"])
        ]
        done(*ready[0])

    def finish(k):
        values = join(local[k], ordered(*flying[k]), bits - 1)
        gathered = []
        for value in values:
            value = value.reshape((n_dp, 2, -1, part))
            gathered.append(jnp.swapaxes(value, 0, 1).reshape(2, -1, part))
        gathered = jnp.concatenate(gathered, axis=2)
        out = lax.dot_general(gathered[0], gate_weight, CONTRACT_LAST, preferred_element_type=f32)
        out = out + lax.dot_general(
            gathered[1], up_weight, CONTRACT_LAST, preferred_element_type=f32
        )
        out = out.reshape(n_dp, len(masks[k]), 2, rows, width)
        send = out[:, :, 1].astype(bf16)
        out_flying[k] = (out[:, :, 0], over_core(send))
        done(send)

    def send_home(k):
        own, got = out_flying[k]
        (got,) = ordered(got)
        out = own + got.astype(f32)
        for place, mask in enumerate(masks[k]):
            term = out[:, place]
            if mask:
                term = term.astype(bf16)
                terms[mask] = over_z(term, mask)
            else:
                terms[mask] = term
            done(term)

    def collect(sources):
        total = 0.0
        for term in ordered(*[terms[mask] for mask in sources]):
            total = total + term.astype(f32)
        done(total)
        return total

    def window_rows(mask):
        if mask == 0:
            window_held[0] = jnp.stack(ordered(grad_out, tokens))
        else:
            places = list(window_held)
            values = ordered(*[window_held[place] for place in places])
            window_held.update(zip(places, values))
        if mask + 1 < n_z:
            hop(window_held, mask + 1)
            return
        rows_there = [window_held[mask] for k in range(2) for mask in masks[k]]
        window_held["own"] = jnp.stack(rows_there, axis=1)
        window_held["other"] = over_core(window_held["own"])
        done(window_held["own"])

    def delta_terms():
        windows = ordered(window_held["own"], window_held["other"])
        chunks = range(2)
        deltas = window_deltas(
            n_dp,
            units,
            me,
            block_kind,
            block_ff,
            block_d,
            block_owner[:, 0],
            list(windows),
            [piece for k in chunks for piece in owns[k][0]],
            [piece for k in chunks for piece in owns[k][1]],
        )
        done(deltas)
        deltas = deltas.reshape((2,) * bits + (CAP, BLOCK, BLOCK))
        cut = BLOCK // parts
        ready["delta"] = [deltas[..., q * cut : (q + 1) * cut, :] for q in range(parts)]

    swap("own")
    forward("own")
    send("own", 0)
    for mask in masks["near"]:
        relay(held, mask)
    swap("near")
    forward("near")
    send("near", 0)
    for mask in masks[1]:
        relay(held, mask)
    take("own", 0)
    swap(1)
    take("near", 0)
    merge()
    send(0, 1)
    forward(1)
    send(1, 0)
    window_rows(0)
    hops = iter(range(1, n_z))
    for s in range(2, stages - 1):
        take(0, s - 1)
        send(0, s)
        window_rows(next(hops))
        take(1, s - 2)
        send(1, s - 1)
    for mask in hops:
        window_rows(mask)
    take(1, stages - 3)
    take(0, stages - 2)
    send(1, stages - 2)
    delta_terms()
    take(1, stages - 2)
    send(1, stages - 1)
    send("delta", 0)
    finish(1)
    send(0, stages - 1)
    for s in range(1, bits):
        take("delta", s - 1)
        if s == 1:
            send_home(1)
            total = collect(masks[1])
        send("delta", s)
    finish(0)
    send_home(0)

    total = (total + terms[0] + collect(masks["near"])).astype(bf16)
    pieces = [total[0]] + [over_dp(total[mask], mask) for mask in range(1, n_dp)]
    done(total)
    take("delta", bits - 1)
    deltas = jnp.concatenate(ready["delta"], axis=1)
    pieces = jnp.stack(pieces)
    slots = jnp.arange(n_dp, dtype=jnp.int32)
    grad_tokens = pieces.at[slots ^ me].get(mode="promise_in_bounds")
    grad_tokens = jnp.swapaxes(grad_tokens, 0, 1).reshape(rows, features)
    return (grad_tokens, deltas)


def solution(mesh):
    placed = (
        P(("groups", "dp", "tensor"), None),
        P(("groups", "dp", "tensor"), None),
        P("dp", "tensor"),
        P("dp", "tensor"),
        P("tensor", "dp"),
        P("tensor"),
        P("tensor"),
        P("tensor"),
        P("tensor", None),
    )
    return jax.shard_map(
        body,
        mesh=mesh,
        in_specs=placed,
        out_specs=(P(("groups", "dp", "tensor"), None), P(("groups", "dp", "tensor"), None, None)),
        check_vma=False,
    )
```

```python
import functools

import jax
import jax.numpy as jnp
from jax import lax
from jax.experimental import pallas as pl
from jax.experimental.pallas import tpu as pltpu
from jax.sharding import PartitionSpec as P

BLOCK = 128
CAP = 5
CONTRACT_LAST = (((1,), (1,)), ((), ()))
SMALL = pl.CostEstimate(flops=1, bytes_accessed=1, transcendentals=0)


def xor_perm(size, mask):
    return [(i, i ^ mask) for i in range(size)]


def z_perm(n_tensor, mask):
    return [(rank, rank ^ 2 * mask) for rank in range(n_tensor)]


def chunk_masks(n_z):
    low, high = tuple(range(n_z // 2)), tuple(range(n_z // 2, n_z))
    return {"own": low[:1], "near": low[1:], 0: low, 1: high}


def delta_kernel(n_dp, n_pieces, me_ref, kind_ref, ff_ref, col_ref, owner_ref, *refs):
    window_refs, refs = refs[:2], refs[2:]
    hidden_refs, grad_refs, refs = refs[:n_pieces], refs[n_pieces : 2 * n_pieces], refs[2 * n_pieces :]
    out_ref, grads_ref, tokens_ref, hidden_ref, gate_ref, up_ref, used_ref = refs
    me = me_ref[0]
    out_ref[...] = jnp.zeros_like(out_ref)
    for owner in range(n_dp):
        used_ref[owner] = 0

    start = 0
    _, chips, rows, _ = window_refs[0].shape
    for chip in range(chips):
        for window_ref in window_refs:
            grads_ref[start : start + rows] = window_ref[0, chip]
            tokens_ref[start : start + rows] = window_ref[1, chip]
            start += rows
    start, column = 0, 0
    for hidden_piece, grad_piece in zip(hidden_refs, grad_refs):
        rows, units = hidden_piece.shape
        place = (slice(start, start + rows), slice(column, column + units))
        hidden_ref[place] = hidden_piece[...]
        gate_ref[place] = grad_piece[0]
        up_ref[place] = grad_piece[1]
        column += units
        if column == hidden_ref.shape[1]:
            start, column = start + rows, 0

    def step(entry, carry):
        owner = owner_ref[entry]
        slot = used_ref[owner]
        used_ref[owner] = slot + 1
        kind = kind_ref[entry]
        units = pl.ds(pl.multiple_of(ff_ref[entry] * BLOCK, BLOCK), BLOCK)
        columns = pl.ds(pl.multiple_of(col_ref[entry] * BLOCK, BLOCK), BLOCK)
        left = jnp.where(kind == 2, hidden_ref[:, units], tokens_ref[:, columns])
        right = jnp.where(
            kind == 0,
            gate_ref[:, units],
            jnp.where(kind == 1, up_ref[:, units], grads_ref[:, columns]),
        )
        out_ref[(owner ^ me) * CAP + slot] = lax.dot_general(
            left, right, (((0,), (0,)), ((), ())), preferred_element_type=jnp.float32
        )
        return carry

    lax.fori_loop(0, kind_ref.shape[0], step, 0)


def window_deltas(n_dp, units, me, kind, ff, col, owner, windows, hiddens, grads):
    _, chips, rows, features = windows[0].shape
    total = 2 * chips * rows
    if rows % 16:
        joined = jnp.stack(windows, axis=2).reshape(2, 1, total, features)
        windows = [joined[:, :, : total // 2], joined[:, :, total // 2 :]]
        across = units // hiddens[0].shape[1]
        groups = range(0, len(hiddens), across)
        hiddens = [
            jnp.concatenate([jnp.concatenate(hiddens[i : i + across], axis=1) for i in groups])
        ]
        grads = [
            jnp.concatenate([jnp.concatenate(grads[i : i + across], axis=2) for i in groups], axis=1)
        ]
    smem, vmem = pl.BlockSpec(memory_space=pltpu.SMEM), pl.BlockSpec(memory_space=pltpu.VMEM)
    bf16 = jnp.bfloat16
    return pl.pallas_call(
        functools.partial(delta_kernel, n_dp, len(hiddens)),
        out_shape=jax.ShapeDtypeStruct((n_dp * CAP, BLOCK, BLOCK), jnp.float32),
        in_specs=[smem] * 5 + [vmem] * (2 + 2 * len(hiddens)),
        out_specs=vmem,
        scratch_shapes=[
            pltpu.VMEM((total, features), bf16),
            pltpu.VMEM((total, features), bf16),
            pltpu.VMEM((total, units), bf16),
            pltpu.VMEM((total, units), bf16),
            pltpu.VMEM((total, units), bf16),
            pltpu.SMEM((n_dp,), jnp.int32),
        ],
        compiler_params=pltpu.CompilerParams(vmem_limit_bytes=24 << 20),
        cost_estimate=SMALL,
    )(me.reshape(1), kind, ff, col, owner, *windows, *hiddens, *grads)


def load_kernel(*refs):
    n = (len(refs) - 1) // 2
    copies = [
        pltpu.make_async_copy(source, target, refs[-1].at[i])
        for i, (source, target) in enumerate(zip(refs[:n], refs[n : 2 * n]))
    ]
    for copy in copies:
        copy.start()
    for copy in copies:
        copy.wait()


def in_vmem(*weights):
    return pl.pallas_call(
        load_kernel,
        out_shape=[pltpu.VMEM(w.shape, w.dtype) for w in weights],
        in_specs=[pl.BlockSpec(memory_space=pl.ANY)] * len(weights),
        out_specs=[pl.BlockSpec(memory_space=pltpu.VMEM)] * len(weights),
        scratch_shapes=[pltpu.SemaphoreType.DMA((len(weights),))],
        compiler_params=pltpu.CompilerParams(vmem_limit_bytes=1 << 20),
        cost_estimate=SMALL,
    )(*[pltpu.with_memory_space_constraint(w, pltpu.HBM) for w in weights])


def forward_kernel(bits, own_ref, other_ref, gate_ref, up_ref, down_ref, *refs):
    out_refs, chunk_ref = refs[:-1], refs[-1]
    f32 = jnp.float32
    chips, _, windows, rows, _ = own_ref.shape
    start = 0
    for window in range(windows):
        for chip in range(chips):
            for ref in (own_ref, other_ref):
                chunk_ref[:, start : start + rows] = ref[chip, :, window]
                start += rows
    count = start // windows
    grads, tokens = chunk_ref[0], chunk_ref[1]
    part = out_refs[0].shape[3]
    block = min(part, 512)
    for q, bit in enumerate(bits):
        for column in range(0, part, block):
            units = slice(q * part + column, q * part + column + block)
            products = (
                jnp.dot(tokens, gate_ref[:, units], preferred_element_type=f32),
                jnp.dot(tokens, up_ref[:, units], preferred_element_type=f32),
                lax.dot_general(
                    grads, down_ref[units, :], CONTRACT_LAST, preferred_element_type=f32
                ),
            )
            for i, product in enumerate(products):
                product = product.astype(chunk_ref.dtype)
                places = [0, 0]
                for window in range(windows):
                    sent = window >> bit & 1
                    out_refs[2 * q + sent][i, places[sent], :, column : column + block] = product[
                        window * count : (window + 1) * count
                    ]
                    places[sent] += 1


def forward_partials(bits, own, other, gate_weight, up_weight, down_weight):
    chips, _, windows, rows, width = own.shape
    count = 2 * chips * rows
    part = gate_weight.shape[1] // len(bits)
    vmem = pl.BlockSpec(memory_space=pltpu.VMEM)
    outs = pl.pallas_call(
        functools.partial(forward_kernel, bits),
        out_shape=[jax.ShapeDtypeStruct((3, windows // 2, count, part), own.dtype)] * 2 * len(bits),
        in_specs=[vmem] * 5,
        out_specs=[vmem] * 2 * len(bits),
        scratch_shapes=[pltpu.VMEM((2, windows * count, width), own.dtype)],
        compiler_params=pltpu.CompilerParams(vmem_limit_bytes=16 << 20),
        cost_estimate=SMALL,
    )(own, other, gate_weight, up_weight, down_weight)
    return outs[::2], outs[1::2]


def place_kernel(me_ref, *refs):
    piece_refs, out_ref = refs[:-1], refs[-1]
    width = piece_refs[0].shape[1]
    for mask, piece_ref in enumerate(piece_refs):
        start = pl.multiple_of((me_ref[0] ^ mask) * width, BLOCK)
        out_ref[:, pl.ds(start, width)] = piece_ref[...]


def place_slices(me, pieces):
    smem, vmem = pl.BlockSpec(memory_space=pltpu.SMEM), pl.BlockSpec(memory_space=pltpu.VMEM)
    rows, width = pieces[0].shape
    return pl.pallas_call(
        place_kernel,
        out_shape=jax.ShapeDtypeStruct((rows, width * len(pieces)), pieces[0].dtype),
        in_specs=[smem] + [vmem] * len(pieces),
        out_specs=vmem,
        compiler_params=pltpu.CompilerParams(vmem_limit_bytes=4 << 20),
        cost_estimate=SMALL,
    )(me.reshape(1), *pieces)


def body(
    tokens,
    grad_out,
    gate_weight,
    up_weight,
    down_weight,
    block_kind,
    block_ff,
    block_d,
    block_owner,
):
    n_dp, n_tensor = lax.axis_size("dp"), lax.axis_size("tensor")
    n_z = n_tensor // 2
    bits = n_dp.bit_length() - 1
    rows, features = tokens.shape
    width, units = gate_weight.shape
    me = lax.axis_index("dp")
    bf16, f32 = jnp.bfloat16, jnp.float32
    parts = min(bits, 2)
    part = units // parts
    orders = [[(q + s) % bits for s in range(bits)] for q in range(parts)]
    masks = chunk_masks(n_z)
    stages = 2 * bits

    chain = []

    def ordered(*values):
        if not chain:
            return values
        return lax.optimization_barrier(values + tuple(chain))[: len(values)]

    def done(*results):
        chain[:] = results

    def over_dp(value, mask):
        return lax.ppermute(value, "dp", xor_perm(n_dp, mask))

    def over_core(value):
        return lax.ppermute(value, "tensor", xor_perm(n_tensor, 1))

    def over_z(value, mask):
        return lax.ppermute(value, "tensor", z_perm(n_tensor, mask))

    held, window_held, shards, other = {}, {}, {}, {}
    ready, flying, local, owns, out_flying, terms = {}, {}, {}, {}, {}, {}

    def hop(held, mask):
        low = mask & -mask
        held[mask] = over_z(held[mask ^ low], low)

    def relay(held, mask):
        (held[mask],) = ordered(held[mask])
        low = mask & -mask if mask else n_z
        for step in range(low.bit_length() - 1):
            hop(held, mask | 1 << step)

    def swap(k):
        got = ordered(*[held[mask] for mask in masks[k]])
        shards[k] = jnp.stack(got)
        other[k] = over_core(shards[k])
        done(shards[k])

    pieces = []
    for mask in range(n_dp):
        start = (me ^ mask) * width
        piece = jnp.stack(
            [lax.dynamic_slice_in_dim(x, start, width, axis=1) for x in (grad_out, tokens)]
        )
        pieces.append(over_dp(piece, mask) if mask else piece)
    if rows % 16 == 0:
        gate_weight, up_weight, down_weight = in_vmem(gate_weight, up_weight, down_weight)
        done(gate_weight, up_weight, down_weight)
    held[0] = jnp.stack(ordered(*pieces), axis=1)
    hop(held, 1)

    def forward(k):
        own, others = ordered(shards[k], other[k])
        weights = (gate_weight, up_weight, down_weight)
        if rows % 16 == 0:
            first = [order[0] for order in orders]
            keep, fly = forward_partials(first, own, others, *weights)
            shape = (3,) + (2,) * (bits - 1) + (-1, part)
            local[k] = [x.reshape(shape) for x in keep]
            ready[k] = [x.reshape(shape) for x in fly]
            done(*local[k], *ready[k])
            return
        chunk = jnp.stack([own, others], axis=3).transpose(1, 2, 0, 3, 4, 5)
        chunk = chunk.reshape(2, -1, width)
        gate = jnp.dot(chunk[1], gate_weight, preferred_element_type=f32).astype(bf16)
        upward = jnp.dot(chunk[1], up_weight, preferred_element_type=f32).astype(bf16)
        hidden_grad = lax.dot_general(
            chunk[0], down_weight, CONTRACT_LAST, preferred_element_type=f32
        ).astype(bf16)
        sums = jnp.stack([gate, upward, hidden_grad])
        values = []
        for q in range(parts):
            value = sums[:, :, q * part : (q + 1) * part]
            values.append(value.reshape((3,) + (2,) * bits + (-1, part)))
        ready[k] = values
        done(*values)

    def add_halves(keep, fly):
        got = ordered(*fly)
        return [x.astype(f32) + y.astype(f32) for x, y in zip(keep, got)]

    def gradients(sums):
        hiddens, values = [], []
        for g, u, h in sums:
            sig = jax.nn.sigmoid(g)
            silu = g * sig
            hiddens.append((silu * u).astype(bf16))
            gate_grad = (h * u * sig * (1.0 + g * (1.0 - sig))).astype(bf16)
            up_grad = (h * silu).astype(bf16)
            values.append(jnp.stack([gate_grad, up_grad]))
        return hiddens, values

    def join(values, got, s):
        joined = []
        for value, more, order in zip(values, got, orders):
            order = order[::-1]
            axis = sum(1 for bit in order[:s] if bit > order[s])
            joined.append(jnp.stack([value, more], axis=axis))
        return joined

    def send(k, s):
        values = ordered(*ready[k])
        if s >= bits:
            local[k] = values
            flying[k] = [
                over_dp(value, 1 << order[::-1][s - bits]) for value, order in zip(values, orders)
            ]
            return
        if k != "delta" and s == 0 and rows % 16 == 0:
            flying[k] = [over_dp(x, 1 << order[s]) for x, order in zip(values, orders)]
            return
        local[k], fly = [], []
        for value, order in zip(values, orders):
            axis = (k != "delta") + sorted(order[s:], reverse=True).index(order[s])
            local[k].append(lax.index_in_dim(value, 0, axis, keepdims=False))
            fly.append(lax.index_in_dim(value, 1, axis, keepdims=False).astype(bf16))
        flying[k] = [over_dp(x, 1 << order[s]) for x, order in zip(fly, orders)]

    def take(k, s):
        if s < bits:
            values = add_halves(local[k], flying[k])
            if k == "delta":
                ready[k] = values
                done(*values)
                return
        else:
            values = join(local[k], ordered(*flying[k]), s - bits)
        if s == bits - 1:
            hiddens, values = gradients(values)
            owns[k] = (hiddens, values)
            done(*hiddens, *values)
        else:
            done(*values)
        ready[k] = values

    def merge():
        ready[0] = [
            jnp.concatenate(values, axis=-2) for values in zip(ready["own"], ready["near"])
        ]
        done(*ready[0])

    def finish(k):
        values = join(local[k], ordered(*flying[k]), bits - 1)
        gathered = []
        for value in values:
            value = value.reshape((n_dp, 2, -1, part))
            gathered.append(jnp.swapaxes(value, 0, 1).reshape(2, -1, part))
        gathered = jnp.concatenate(gathered, axis=2)
        out = lax.dot_general(gathered[0], gate_weight, CONTRACT_LAST, preferred_element_type=f32)
        out = out + lax.dot_general(
            gathered[1], up_weight, CONTRACT_LAST, preferred_element_type=f32
        )
        out = out.reshape(n_dp, len(masks[k]), 2, rows, width)
        send = out[:, :, 1].astype(bf16)
        out_flying[k] = (out[:, :, 0], over_core(send))
        done(send)

    def send_home(k):
        own, got = out_flying[k]
        (got,) = ordered(got)
        out = own + got.astype(f32)
        for place, mask in enumerate(masks[k]):
            term = out[:, place]
            if mask:
                term = term.astype(bf16)
                terms[mask] = over_z(term, mask)
            else:
                terms[mask] = term
            done(term)

    def collect(sources):
        total = 0.0
        for term in ordered(*[terms[mask] for mask in sources]):
            total = total + term.astype(f32)
        done(total)
        return total

    def window_rows(mask):
        if mask == 0:
            window_held[0] = jnp.stack(ordered(grad_out, tokens))
        else:
            places = list(window_held)
            values = ordered(*[window_held[place] for place in places])
            window_held.update(zip(places, values))
        if mask + 1 < n_z:
            hop(window_held, mask + 1)
            return
        rows_there = [window_held[mask] for k in range(2) for mask in masks[k]]
        window_held["own"] = jnp.stack(rows_there, axis=1)
        window_held["other"] = over_core(window_held["own"])
        done(window_held["own"])

    def delta_terms():
        windows = ordered(window_held["own"], window_held["other"])
        chunks = range(2)
        deltas = window_deltas(
            n_dp,
            units,
            me,
            block_kind,
            block_ff,
            block_d,
            block_owner[:, 0],
            list(windows),
            [piece for k in chunks for piece in owns[k][0]],
            [piece for k in chunks for piece in owns[k][1]],
        )
        done(deltas)
        deltas = deltas.reshape((2,) * bits + (CAP, BLOCK, BLOCK))
        cut = BLOCK // parts
        ready["delta"] = [deltas[..., q * cut : (q + 1) * cut, :] for q in range(parts)]

    swap("own")
    forward("own")
    send("own", 0)
    for step in range(1, n_z.bit_length() - 1):
        (held[0],) = ordered(held[0])
        hop(held, 1 << step)
    for mask in masks["near"]:
        relay(held, mask)
    swap("near")
    forward("near")
    send("near", 0)
    for mask in masks[1]:
        relay(held, mask)
    take("own", 0)
    swap(1)
    take("near", 0)
    merge()
    send(0, 1)
    forward(1)
    send(1, 0)
    window_rows(0)
    hops = iter(range(1, n_z))
    for s in range(2, stages - 1):
        take(0, s - 1)
        send(0, s)
        window_rows(next(hops))
        take(1, s - 2)
        send(1, s - 1)
    for mask in hops:
        window_rows(mask)
    take(1, stages - 3)
    take(0, stages - 2)
    send(1, stages - 2)
    delta_terms()
    take(1, stages - 2)
    send(1, stages - 1)
    send("delta", 0)
    finish(1)
    send(0, stages - 1)
    for s in range(1, bits):
        take("delta", s - 1)
        send("delta", s)
    send_home(1)
    total = collect(masks[1])
    *flying[0], total = lax.optimization_barrier((*flying[0], total))
    finish(0)
    send_home(0)

    total = (total + terms[0] + collect(masks["near"])).astype(bf16)
    pieces = [total[0]] + [over_dp(total[mask], mask) for mask in range(1, n_dp)]
    done(total)
    take("delta", bits - 1)
    deltas = jnp.concatenate(ready["delta"], axis=1)
    grad_tokens = place_slices(me, pieces)
    return (grad_tokens, deltas)


def solution(mesh):
    placed = (
        P(("groups", "dp", "tensor"), None),
        P(("groups", "dp", "tensor"), None),
        P("dp", "tensor"),
        P("dp", "tensor"),
        P("tensor", "dp"),
        P("tensor"),
        P("tensor"),
        P("tensor"),
        P("tensor", None),
    )
    return jax.shard_map(
        body,
        mesh=mesh,
        in_specs=placed,
        out_specs=(P(("groups", "dp", "tensor"), None), P(("groups", "dp", "tensor"), None, None)),
        check_vma=False,
    )
```

```python
import functools

import jax
import jax.numpy as jnp
import numpy as np
from jax import lax
from jax.experimental import pallas as pl
from jax.experimental.pallas import tpu as pltpu
from jax.sharding import PartitionSpec as P

BLOCK = 128
CAP = 5
CONTRACT_LAST = (((1,), (1,)), ((), ()))
SMALL = pl.CostEstimate(flops=1, bytes_accessed=1, transcendentals=0)


def xor_perm(size, mask):
    return [(i, i ^ mask) for i in range(size)]


def z_perm(n_tensor, mask):
    return [(rank, rank ^ 2 * mask) for rank in range(n_tensor)]


def chunk_masks(n_z):
    low, high = tuple(range(n_z // 2)), tuple(range(n_z // 2, n_z))
    return {"own": low[:1], "near": low[1:], 0: low, 1: high}


def delta_kernel(n_dp, n_pieces, me_ref, kind_ref, ff_ref, col_ref, owner_ref, *refs):
    window_refs, refs = refs[:2], refs[2:]
    hidden_refs, grad_refs, refs = refs[:n_pieces], refs[n_pieces : 2 * n_pieces], refs[2 * n_pieces :]
    out_ref, grads_ref, tokens_ref, hidden_ref, gate_ref, up_ref, used_ref = refs
    me = me_ref[0]
    out_ref[...] = jnp.zeros_like(out_ref)
    for owner in range(n_dp):
        used_ref[owner] = 0

    start = 0
    _, chips, rows, _ = window_refs[0].shape
    for chip in range(chips):
        for window_ref in window_refs:
            grads_ref[start : start + rows] = window_ref[0, chip]
            tokens_ref[start : start + rows] = window_ref[1, chip]
            start += rows
    start, column = 0, 0
    for hidden_piece, grad_piece in zip(hidden_refs, grad_refs):
        rows, units = hidden_piece.shape
        place = (slice(start, start + rows), slice(column, column + units))
        hidden_ref[place] = hidden_piece[...]
        gate_ref[place] = grad_piece[0]
        up_ref[place] = grad_piece[1]
        column += units
        if column == hidden_ref.shape[1]:
            start, column = start + rows, 0

    def step(entry, carry):
        owner = owner_ref[entry]
        slot = used_ref[owner]
        used_ref[owner] = slot + 1
        kind = kind_ref[entry]
        units = pl.ds(pl.multiple_of(ff_ref[entry] * BLOCK, BLOCK), BLOCK)
        columns = pl.ds(pl.multiple_of(col_ref[entry] * BLOCK, BLOCK), BLOCK)
        left = jnp.where(kind == 2, hidden_ref[:, units], tokens_ref[:, columns])
        right = jnp.where(
            kind == 0,
            gate_ref[:, units],
            jnp.where(kind == 1, up_ref[:, units], grads_ref[:, columns]),
        )
        out_ref[(owner ^ me) * CAP + slot] = lax.dot_general(
            left, right, (((0,), (0,)), ((), ())), preferred_element_type=jnp.float32
        )
        return carry

    lax.fori_loop(0, kind_ref.shape[0], step, 0)


def window_deltas(n_dp, units, me, kind, ff, col, owner, windows, hiddens, grads):
    _, chips, rows, features = windows[0].shape
    total = 2 * chips * rows
    if rows % 16:
        joined = jnp.stack(windows, axis=2).reshape(2, 1, total, features)
        windows = [joined[:, :, : total // 2], joined[:, :, total // 2 :]]
        across = units // hiddens[0].shape[1]
        groups = range(0, len(hiddens), across)
        hiddens = [
            jnp.concatenate([jnp.concatenate(hiddens[i : i + across], axis=1) for i in groups])
        ]
        grads = [
            jnp.concatenate([jnp.concatenate(grads[i : i + across], axis=2) for i in groups], axis=1)
        ]
    smem, vmem = pl.BlockSpec(memory_space=pltpu.SMEM), pl.BlockSpec(memory_space=pltpu.VMEM)
    bf16 = jnp.bfloat16
    return pl.pallas_call(
        functools.partial(delta_kernel, n_dp, len(hiddens)),
        out_shape=jax.ShapeDtypeStruct((n_dp * CAP, BLOCK, BLOCK), jnp.float32),
        in_specs=[smem] * 5 + [vmem] * (2 + 2 * len(hiddens)),
        out_specs=vmem,
        scratch_shapes=[
            pltpu.VMEM((total, features), bf16),
            pltpu.VMEM((total, features), bf16),
            pltpu.VMEM((total, units), bf16),
            pltpu.VMEM((total, units), bf16),
            pltpu.VMEM((total, units), bf16),
            pltpu.SMEM((n_dp,), jnp.int32),
        ],
        compiler_params=pltpu.CompilerParams(vmem_limit_bytes=24 << 20),
        cost_estimate=SMALL,
    )(me.reshape(1), kind, ff, col, owner, *windows, *hiddens, *grads)


def load_kernel(*refs):
    n = (len(refs) - 1) // 2
    copies = [
        pltpu.make_async_copy(source, target, refs[-1].at[i])
        for i, (source, target) in enumerate(zip(refs[:n], refs[n : 2 * n]))
    ]
    for copy in copies:
        copy.start()
    for copy in copies:
        copy.wait()


def in_vmem(*weights):
    return pl.pallas_call(
        load_kernel,
        out_shape=[pltpu.VMEM(w.shape, w.dtype) for w in weights],
        in_specs=[pl.BlockSpec(memory_space=pl.ANY)] * len(weights),
        out_specs=[pl.BlockSpec(memory_space=pltpu.VMEM)] * len(weights),
        scratch_shapes=[pltpu.SemaphoreType.DMA((len(weights),))],
        compiler_params=pltpu.CompilerParams(vmem_limit_bytes=1 << 20),
        cost_estimate=SMALL,
    )(*[pltpu.with_memory_space_constraint(w, pltpu.HBM) for w in weights])


def forward_kernel(bits, own_ref, other_ref, gate_ref, up_ref, down_ref, *refs):
    out_refs, chunk_ref = refs[:-1], refs[-1]
    f32 = jnp.float32
    chips, _, windows, rows, _ = own_ref.shape
    start = 0
    for window in range(windows):
        for chip in range(chips):
            for ref in (own_ref, other_ref):
                chunk_ref[:, start : start + rows] = ref[chip, :, window]
                start += rows
    count = start // windows
    grads, tokens = chunk_ref[0], chunk_ref[1]
    part = out_refs[0].shape[3]
    block = min(part, 512)
    for q, bit in enumerate(bits):
        for column in range(0, part, block):
            units = slice(q * part + column, q * part + column + block)
            products = (
                jnp.dot(tokens, gate_ref[:, units], preferred_element_type=f32),
                jnp.dot(tokens, up_ref[:, units], preferred_element_type=f32),
                lax.dot_general(
                    grads, down_ref[units, :], CONTRACT_LAST, preferred_element_type=f32
                ),
            )
            for i, product in enumerate(products):
                product = product.astype(chunk_ref.dtype)
                places = [0, 0]
                for window in range(windows):
                    sent = window >> bit & 1
                    out_refs[2 * q + sent][i, places[sent], :, column : column + block] = product[
                        window * count : (window + 1) * count
                    ]
                    places[sent] += 1


def forward_partials(bits, own, other, gate_weight, up_weight, down_weight):
    chips, _, windows, rows, width = own.shape
    count = 2 * chips * rows
    part = gate_weight.shape[1] // len(bits)
    vmem = pl.BlockSpec(memory_space=pltpu.VMEM)
    outs = pl.pallas_call(
        functools.partial(forward_kernel, bits),
        out_shape=[jax.ShapeDtypeStruct((3, windows // 2, count, part), own.dtype)] * 2 * len(bits),
        in_specs=[vmem] * 5,
        out_specs=[vmem] * 2 * len(bits),
        scratch_shapes=[pltpu.VMEM((2, windows * count, width), own.dtype)],
        compiler_params=pltpu.CompilerParams(vmem_limit_bytes=16 << 20),
        cost_estimate=SMALL,
    )(own, other, gate_weight, up_weight, down_weight)
    return outs[::2], outs[1::2]


def backward_kernel(places, *refs):
    f32 = jnp.float32
    n = len(places)
    piece_refs, (gate_ref, up_ref, out_ref, grads_ref) = refs[:n], refs[n:]
    for piece_ref, (starts, column) in zip(piece_refs, places):
        _, _, rows, columns = piece_ref.shape
        for index, start in enumerate(starts):
            place = (slice(None), slice(start, start + rows), slice(column, column + columns))
            grads_ref[place] = piece_ref[index]
    width = out_ref.shape[1]
    block = min(width, 256)
    for column in range(0, width, block):
        cut = slice(column, column + block)
        first = lax.dot_general(
            grads_ref[0], gate_ref[cut, :], CONTRACT_LAST, preferred_element_type=f32
        )
        second = lax.dot_general(
            grads_ref[1], up_ref[cut, :], CONTRACT_LAST, preferred_element_type=f32
        )
        out_ref[:, cut] = first + second


def backward_partials(pieces, places, gate_weight, up_weight):
    width, units = gate_weight.shape
    total = max(start for starts, _ in places for start in starts) + pieces[0].shape[2]
    vmem = pl.BlockSpec(memory_space=pltpu.VMEM)
    return pl.pallas_call(
        functools.partial(backward_kernel, places),
        out_shape=jax.ShapeDtypeStruct((total, width), jnp.float32),
        in_specs=[vmem] * (len(pieces) + 2),
        out_specs=vmem,
        scratch_shapes=[pltpu.VMEM((2, total, units), jnp.bfloat16)],
        compiler_params=pltpu.CompilerParams(vmem_limit_bytes=16 << 20),
        cost_estimate=SMALL,
    )(*pieces, gate_weight, up_weight)


def place_kernel(me_ref, *refs):
    piece_refs, out_ref = refs[:-1], refs[-1]
    width = piece_refs[0].shape[1]
    for mask, piece_ref in enumerate(piece_refs):
        start = pl.multiple_of((me_ref[0] ^ mask) * width, BLOCK)
        out_ref[:, pl.ds(start, width)] = piece_ref[...]


def place_slices(me, pieces):
    smem, vmem = pl.BlockSpec(memory_space=pltpu.SMEM), pl.BlockSpec(memory_space=pltpu.VMEM)
    rows, width = pieces[0].shape
    return pl.pallas_call(
        place_kernel,
        out_shape=jax.ShapeDtypeStruct((rows, width * len(pieces)), pieces[0].dtype),
        in_specs=[smem] + [vmem] * len(pieces),
        out_specs=vmem,
        compiler_params=pltpu.CompilerParams(vmem_limit_bytes=4 << 20),
        cost_estimate=SMALL,
    )(me.reshape(1), *pieces)


def body(
    tokens,
    grad_out,
    gate_weight,
    up_weight,
    down_weight,
    block_kind,
    block_ff,
    block_d,
    block_owner,
):
    n_dp, n_tensor = lax.axis_size("dp"), lax.axis_size("tensor")
    n_z = n_tensor // 2
    bits = n_dp.bit_length() - 1
    rows, features = tokens.shape
    width, units = gate_weight.shape
    me = lax.axis_index("dp")
    bf16, f32 = jnp.bfloat16, jnp.float32
    parts = min(bits, 2)
    part = units // parts
    orders = [[(q + s) % bits for s in range(bits)] for q in range(parts)]
    masks = chunk_masks(n_z)
    stages = 2 * bits

    chain = []

    def ordered(*values):
        if not chain:
            return values
        return lax.optimization_barrier(values + tuple(chain))[: len(values)]

    def done(*results):
        chain[:] = results

    def over_dp(value, mask):
        return lax.ppermute(value, "dp", xor_perm(n_dp, mask))

    def over_core(value):
        return lax.ppermute(value, "tensor", xor_perm(n_tensor, 1))

    def over_z(value, mask):
        return lax.ppermute(value, "tensor", z_perm(n_tensor, mask))

    held, window_held, shards, other = {}, {}, {}, {}
    ready, flying, local, owns, out_flying, terms = {}, {}, {}, {}, {}, {}

    def hop(held, mask):
        low = mask & -mask
        held[mask] = over_z(held[mask ^ low], low)

    def relay(held, mask):
        (held[mask],) = ordered(held[mask])
        low = mask & -mask if mask else n_z
        for step in range(low.bit_length() - 1):
            hop(held, mask | 1 << step)

    def swap(k):
        got = ordered(*[held[mask] for mask in masks[k]])
        shards[k] = jnp.stack(got)
        other[k] = over_core(shards[k])
        done(shards[k])

    pieces = []
    for mask in range(n_dp):
        start = (me ^ mask) * width
        piece = jnp.stack(
            [lax.dynamic_slice_in_dim(x, start, width, axis=1) for x in (grad_out, tokens)]
        )
        pieces.append(over_dp(piece, mask) if mask else piece)
    if rows % 16 == 0:
        gate_weight, up_weight, down_weight = in_vmem(gate_weight, up_weight, down_weight)
        done(gate_weight, up_weight, down_weight)
    held[0] = jnp.stack(ordered(*pieces), axis=1)
    for step in range(n_z.bit_length() - 1):
        hop(held, 1 << step)

    def forward(k):
        own, others = ordered(shards[k], other[k])
        weights = (gate_weight, up_weight, down_weight)
        if rows % 16 == 0:
            first = [order[0] for order in orders]
            keep, fly = forward_partials(first, own, others, *weights)
            shape = (3,) + (2,) * (bits - 1) + (-1, part)
            local[k] = [x.reshape(shape) for x in keep]
            ready[k] = [x.reshape(shape) for x in fly]
            done(*local[k], *ready[k])
            return
        chunk = jnp.stack([own, others], axis=3).transpose(1, 2, 0, 3, 4, 5)
        chunk = chunk.reshape(2, -1, width)
        gate = jnp.dot(chunk[1], gate_weight, preferred_element_type=f32).astype(bf16)
        upward = jnp.dot(chunk[1], up_weight, preferred_element_type=f32).astype(bf16)
        hidden_grad = lax.dot_general(
            chunk[0], down_weight, CONTRACT_LAST, preferred_element_type=f32
        ).astype(bf16)
        sums = jnp.stack([gate, upward, hidden_grad])
        values = []
        for q in range(parts):
            value = sums[:, :, q * part : (q + 1) * part]
            values.append(value.reshape((3,) + (2,) * bits + (-1, part)))
        ready[k] = values
        done(*values)

    def add_halves(keep, fly):
        got = ordered(*fly)
        return [x.astype(f32) + y.astype(f32) for x, y in zip(keep, got)]

    def gradients(sums):
        hiddens, values = [], []
        for g, u, h in sums:
            sig = jax.nn.sigmoid(g)
            silu = g * sig
            hiddens.append((silu * u).astype(bf16))
            gate_grad = (h * u * sig * (1.0 + g * (1.0 - sig))).astype(bf16)
            up_grad = (h * silu).astype(bf16)
            values.append(jnp.stack([gate_grad, up_grad]))
        return hiddens, values

    def join(values, got, s):
        joined = []
        for value, more, order in zip(values, got, orders):
            order = order[::-1]
            axis = sum(1 for bit in order[:s] if bit > order[s])
            joined.append(jnp.stack([value, more], axis=axis))
        return joined

    def send(k, s):
        values = ordered(*ready[k])
        if s >= bits:
            local[k] = values
            flying[k] = [
                over_dp(value, 1 << order[::-1][s - bits]) for value, order in zip(values, orders)
            ]
            return
        if k != "delta" and s == 0 and rows % 16 == 0:
            flying[k] = [over_dp(x, 1 << order[s]) for x, order in zip(values, orders)]
            return
        local[k], fly = [], []
        for value, order in zip(values, orders):
            axis = (k != "delta") + sorted(order[s:], reverse=True).index(order[s])
            local[k].append(lax.index_in_dim(value, 0, axis, keepdims=False))
            fly.append(lax.index_in_dim(value, 1, axis, keepdims=False).astype(bf16))
        flying[k] = [over_dp(x, 1 << order[s]) for x, order in zip(fly, orders)]

    def take(k, s):
        if s < bits:
            values = add_halves(local[k], flying[k])
            if k == "delta":
                ready[k] = values
                done(*values)
                return
        else:
            values = join(local[k], ordered(*flying[k]), s - bits)
        if s == bits - 1:
            hiddens, values = gradients(values)
            owns[k] = (hiddens, values)
            done(*hiddens, *values)
        else:
            done(*values)
        ready[k] = values

    def merge():
        ready[0] = [
            jnp.concatenate(values, axis=-2) for values in zip(ready["own"], ready["near"])
        ]
        done(*ready[0])

    def part_again():
        count = 2 * rows
        ready["own"] = [x[..., :count, :] for x in ready[0]]
        ready["near"] = [x[..., count:, :] for x in ready[0]]
        done(*ready["own"], *ready["near"])

    def finish(k):
        got = ordered(*flying[k])
        if rows % 16 == 0:
            count = 2 * len(masks[k]) * rows
            pieces, places = [], []
            for q in range(parts):
                order = orders[q][::-1]
                known = sorted(order[:-1], reverse=True)
                windows = [
                    sum(bit << at for bit, at in zip(index, known))
                    for index in np.ndindex((2,) * (bits - 1))
                ]
                for here, piece in enumerate((local[k][q], got[q])):
                    pieces.append(piece.reshape(-1, 2, count, part))
                    starts = [(window | here << order[-1]) * count for window in windows]
                    places.append((tuple(starts), q * part))
            out = backward_partials(pieces, tuple(places), gate_weight, up_weight)
        else:
            gathered = []
            for value in join(local[k], got, bits - 1):
                value = value.reshape((n_dp, 2, -1, part))
                gathered.append(jnp.swapaxes(value, 0, 1).reshape(2, -1, part))
            gathered = jnp.concatenate(gathered, axis=2)
            out = sum(
                lax.dot_general(x, w, CONTRACT_LAST, preferred_element_type=f32)
                for x, w in zip(gathered, (gate_weight, up_weight))
            )
        out = out.reshape(n_dp, len(masks[k]), 2, rows, width)
        send = out[:, :, 1].astype(bf16)
        out_flying[k] = (out[:, :, 0], over_core(send))
        done(send)

    def send_home(k):
        own, got = out_flying[k]
        (got,) = ordered(got)
        out = own + got.astype(f32)
        for place, mask in enumerate(masks[k]):
            term = out[:, place]
            if mask:
                term = term.astype(bf16)
                terms[mask] = over_z(term, mask)
            else:
                terms[mask] = term
            done(term)

    def collect(sources):
        total = 0.0
        for term in ordered(*[terms[mask] for mask in sources]):
            total = total + term.astype(f32)
        done(total)
        return total

    def window_rows(mask):
        if mask == 0:
            window_held[0] = jnp.stack(ordered(grad_out, tokens))
        else:
            places = list(window_held)
            values = ordered(*[window_held[place] for place in places])
            window_held.update(zip(places, values))
        if mask + 1 < n_z:
            hop(window_held, mask + 1)
            return
        rows_there = [window_held[mask] for k in range(2) for mask in masks[k]]
        window_held["own"] = jnp.stack(rows_there, axis=1)
        window_held["other"] = over_core(window_held["own"])
        done(window_held["own"])

    def delta_terms():
        windows = ordered(window_held["own"], window_held["other"])
        chunks = range(2)
        deltas = window_deltas(
            n_dp,
            units,
            me,
            block_kind,
            block_ff,
            block_d,
            block_owner[:, 0],
            list(windows),
            [piece for k in chunks for piece in owns[k][0]],
            [piece for k in chunks for piece in owns[k][1]],
        )
        done(deltas)
        deltas = deltas.reshape((2,) * bits + (CAP, BLOCK, BLOCK))
        cut = BLOCK // parts
        ready["delta"] = [deltas[..., q * cut : (q + 1) * cut, :] for q in range(parts)]

    swap("own")
    forward("own")
    send("own", 0)
    for mask in masks["near"][1::2]:
        relay(held, mask)
    swap("near")
    forward("near")
    send("near", 0)
    take("own", 0)
    for mask in masks[1][::2]:
        relay(held, mask)
    take("near", 0)
    merge()
    send(0, 1)
    swap(1)
    forward(1)
    send(1, 0)
    window_rows(0)
    hops = iter(range(1, n_z))
    for s in range(2, stages - 1):
        take(0, s - 1)
        send(0, s)
        window_rows(next(hops))
        take(1, s - 2)
        send(1, s - 1)
    for mask in hops:
        window_rows(mask)
    take(1, stages - 3)
    take(0, stages - 2)
    part_again()
    send(1, stages - 2)
    delta_terms()
    send("delta", 0)
    take(1, stages - 2)
    send(1, stages - 1)
    take("delta", 0)
    send("near", stages - 1)
    finish(1)
    send("own", stages - 1)
    send_home(1)
    finish("near")
    total = collect(masks[1][:1])
    *flying["own"], total = lax.optimization_barrier((*flying["own"], total))
    finish("own")
    send_home("near")
    for s in range(1, bits):
        if s > 1:
            take("delta", s - 1)
        send("delta", s)
    send_home("own")

    total = total + terms[0] + collect(masks[1][1:]) + collect(masks["near"])
    total = total.astype(bf16)
    pieces = [total[0]] + [over_dp(total[mask], mask) for mask in range(1, n_dp)]
    done(total)
    take("delta", bits - 1)
    deltas = jnp.concatenate(ready["delta"], axis=1)
    grad_tokens = place_slices(me, pieces)
    return (grad_tokens, deltas)


def solution(mesh):
    placed = (
        P(("groups", "dp", "tensor"), None),
        P(("groups", "dp", "tensor"), None),
        P("dp", "tensor"),
        P("dp", "tensor"),
        P("tensor", "dp"),
        P("tensor"),
        P("tensor"),
        P("tensor"),
        P("tensor", None),
    )
    return jax.shard_map(
        body,
        mesh=mesh,
        in_specs=placed,
        out_specs=(P(("groups", "dp", "tensor"), None), P(("groups", "dp", "tensor"), None, None)),
        check_vma=False,
    )
```

```python
import functools

import jax
import jax.numpy as jnp
import numpy as np
from jax import lax
from jax.experimental import pallas as pl
from jax.experimental.pallas import tpu as pltpu
from jax.sharding import PartitionSpec as P

BLOCK = 128
CAP = 5
CONTRACT_LAST = (((1,), (1,)), ((), ()))
SMALL = pl.CostEstimate(flops=1, bytes_accessed=1, transcendentals=0)


def xor_perm(size, mask):
    return [(i, i ^ mask) for i in range(size)]


def z_perm(n_tensor, mask):
    return [(rank, rank ^ 2 * mask) for rank in range(n_tensor)]


def chunk_masks(n_z):
    low, high = tuple(range(n_z // 2)), tuple(range(n_z // 2, n_z))
    return {"own": low[:1], "near": low[1:], 0: low, 1: high, "rest": low[1:] + high}


def delta_kernel(n_dp, n_pieces, me_ref, kind_ref, ff_ref, col_ref, owner_ref, *refs):
    window_refs, refs = refs[:2], refs[2:]
    hidden_refs, grad_refs, refs = refs[:n_pieces], refs[n_pieces : 2 * n_pieces], refs[2 * n_pieces :]
    out_ref, grads_ref, tokens_ref, hidden_ref, gate_ref, up_ref, used_ref = refs
    me = me_ref[0]
    out_ref[...] = jnp.zeros_like(out_ref)
    for owner in range(n_dp):
        used_ref[owner] = 0

    start = 0
    _, chips, rows, _ = window_refs[0].shape
    for chip in range(chips):
        for window_ref in window_refs:
            grads_ref[start : start + rows] = window_ref[0, chip]
            tokens_ref[start : start + rows] = window_ref[1, chip]
            start += rows
    start, column = 0, 0
    for hidden_piece, grad_piece in zip(hidden_refs, grad_refs):
        rows, units = hidden_piece.shape
        place = (slice(start, start + rows), slice(column, column + units))
        hidden_ref[place] = hidden_piece[...]
        gate_ref[place] = grad_piece[0]
        up_ref[place] = grad_piece[1]
        column += units
        if column == hidden_ref.shape[1]:
            start, column = start + rows, 0

    def step(entry, carry):
        owner = owner_ref[entry]
        slot = used_ref[owner]
        used_ref[owner] = slot + 1
        kind = kind_ref[entry]
        units = pl.ds(pl.multiple_of(ff_ref[entry] * BLOCK, BLOCK), BLOCK)
        columns = pl.ds(pl.multiple_of(col_ref[entry] * BLOCK, BLOCK), BLOCK)
        left = jnp.where(kind == 2, hidden_ref[:, units], tokens_ref[:, columns])
        right = jnp.where(
            kind == 0,
            gate_ref[:, units],
            jnp.where(kind == 1, up_ref[:, units], grads_ref[:, columns]),
        )
        out_ref[(owner ^ me) * CAP + slot] = lax.dot_general(
            left, right, (((0,), (0,)), ((), ())), preferred_element_type=jnp.float32
        )
        return carry

    lax.fori_loop(0, kind_ref.shape[0], step, 0)


def window_deltas(n_dp, units, me, kind, ff, col, owner, windows, hiddens, grads):
    _, chips, rows, features = windows[0].shape
    total = 2 * chips * rows
    if rows % 16:
        joined = jnp.stack(windows, axis=2).reshape(2, 1, total, features)
        windows = [joined[:, :, : total // 2], joined[:, :, total // 2 :]]
        across = units // hiddens[0].shape[1]
        groups = range(0, len(hiddens), across)
        hiddens = [
            jnp.concatenate([jnp.concatenate(hiddens[i : i + across], axis=1) for i in groups])
        ]
        grads = [
            jnp.concatenate([jnp.concatenate(grads[i : i + across], axis=2) for i in groups], axis=1)
        ]
    smem, vmem = pl.BlockSpec(memory_space=pltpu.SMEM), pl.BlockSpec(memory_space=pltpu.VMEM)
    bf16 = jnp.bfloat16
    return pl.pallas_call(
        functools.partial(delta_kernel, n_dp, len(hiddens)),
        out_shape=jax.ShapeDtypeStruct((n_dp * CAP, BLOCK, BLOCK), jnp.float32),
        in_specs=[smem] * 5 + [vmem] * (2 + 2 * len(hiddens)),
        out_specs=vmem,
        scratch_shapes=[
            pltpu.VMEM((total, features), bf16),
            pltpu.VMEM((total, features), bf16),
            pltpu.VMEM((total, units), bf16),
            pltpu.VMEM((total, units), bf16),
            pltpu.VMEM((total, units), bf16),
            pltpu.SMEM((n_dp,), jnp.int32),
        ],
        compiler_params=pltpu.CompilerParams(vmem_limit_bytes=24 << 20),
        cost_estimate=SMALL,
    )(me.reshape(1), kind, ff, col, owner, *windows, *hiddens, *grads)


def load_kernel(*refs):
    n = (len(refs) - 1) // 2
    copies = [
        pltpu.make_async_copy(source, target, refs[-1].at[i])
        for i, (source, target) in enumerate(zip(refs[:n], refs[n : 2 * n]))
    ]
    for copy in copies:
        copy.start()
    for copy in copies:
        copy.wait()


def in_vmem(*weights):
    return pl.pallas_call(
        load_kernel,
        out_shape=[pltpu.VMEM(w.shape, w.dtype) for w in weights],
        in_specs=[pl.BlockSpec(memory_space=pl.ANY)] * len(weights),
        out_specs=[pl.BlockSpec(memory_space=pltpu.VMEM)] * len(weights),
        scratch_shapes=[pltpu.SemaphoreType.DMA((len(weights),))],
        compiler_params=pltpu.CompilerParams(vmem_limit_bytes=1 << 20),
        cost_estimate=SMALL,
    )(*[pltpu.with_memory_space_constraint(w, pltpu.HBM) for w in weights])


def forward_kernel(bits, own_ref, other_ref, gate_ref, up_ref, down_ref, *refs):
    out_refs, chunk_ref = refs[:-1], refs[-1]
    f32 = jnp.float32
    chips, _, windows, rows, _ = own_ref.shape
    start = 0
    for window in range(windows):
        for chip in range(chips):
            for ref in (own_ref, other_ref):
                chunk_ref[:, start : start + rows] = ref[chip, :, window]
                start += rows
    count = start // windows
    grads, tokens = chunk_ref[0], chunk_ref[1]
    part = out_refs[0].shape[3]
    block = min(part, 512)
    for q, bit in enumerate(bits):
        for column in range(0, part, block):
            units = slice(q * part + column, q * part + column + block)
            products = (
                jnp.dot(tokens, gate_ref[:, units], preferred_element_type=f32),
                jnp.dot(tokens, up_ref[:, units], preferred_element_type=f32),
                lax.dot_general(
                    grads, down_ref[units, :], CONTRACT_LAST, preferred_element_type=f32
                ),
            )
            for i, product in enumerate(products):
                product = product.astype(chunk_ref.dtype)
                places = [0, 0]
                for window in range(windows):
                    sent = window >> bit & 1
                    out_refs[2 * q + sent][i, places[sent], :, column : column + block] = product[
                        window * count : (window + 1) * count
                    ]
                    places[sent] += 1


def forward_partials(bits, own, other, gate_weight, up_weight, down_weight):
    chips, _, windows, rows, width = own.shape
    count = 2 * chips * rows
    part = gate_weight.shape[1] // len(bits)
    vmem = pl.BlockSpec(memory_space=pltpu.VMEM)
    outs = pl.pallas_call(
        functools.partial(forward_kernel, bits),
        out_shape=[jax.ShapeDtypeStruct((3, windows // 2, count, part), own.dtype)] * 2 * len(bits),
        in_specs=[vmem] * 5,
        out_specs=[vmem] * 2 * len(bits),
        scratch_shapes=[pltpu.VMEM((2, windows * count, width), own.dtype)],
        compiler_params=pltpu.CompilerParams(vmem_limit_bytes=16 << 20),
        cost_estimate=SMALL if chips > 1 else pl.CostEstimate(
            flops=1*6 * windows * count * width * gate_weight.shape[1],
            bytes_accessed=3 * width * gate_weight.shape[1],
            transcendentals=0,
        ),
    )(own, other, gate_weight, up_weight, down_weight)
    return outs[::2], outs[1::2]


def backward_kernel(places, *refs):
    f32 = jnp.float32
    n = len(places)
    piece_refs, (gate_ref, up_ref, out_ref, grads_ref) = refs[:n], refs[n:]
    for piece_ref, (starts, column) in zip(piece_refs, places):
        _, _, rows, columns = piece_ref.shape
        for index, start in enumerate(starts):
            place = (slice(None), slice(start, start + rows), slice(column, column + columns))
            grads_ref[place] = piece_ref[index]
    width = out_ref.shape[1]
    block = min(width, 256)
    for column in range(0, width, block):
        cut = slice(column, column + block)
        first = lax.dot_general(
            grads_ref[0], gate_ref[cut, :], CONTRACT_LAST, preferred_element_type=f32
        )
        second = lax.dot_general(
            grads_ref[1], up_ref[cut, :], CONTRACT_LAST, preferred_element_type=f32
        )
        out_ref[:, cut] = first + second


def backward_partials(pieces, places, gate_weight, up_weight):
    width, units = gate_weight.shape
    total = max(start for starts, _ in places for start in starts) + pieces[0].shape[2]
    vmem = pl.BlockSpec(memory_space=pltpu.VMEM)
    return pl.pallas_call(
        functools.partial(backward_kernel, places),
        out_shape=jax.ShapeDtypeStruct((total, width), jnp.float32),
        in_specs=[vmem] * (len(pieces) + 2),
        out_specs=vmem,
        scratch_shapes=[pltpu.VMEM((2, total, units), jnp.bfloat16)],
        compiler_params=pltpu.CompilerParams(vmem_limit_bytes=16 << 20),
        cost_estimate=SMALL,
    )(*pieces, gate_weight, up_weight)


def place_kernel(me_ref, *refs):
    piece_refs, out_ref = refs[:-1], refs[-1]
    width = piece_refs[0].shape[1]
    for mask, piece_ref in enumerate(piece_refs):
        start = pl.multiple_of((me_ref[0] ^ mask) * width, BLOCK)
        out_ref[:, pl.ds(start, width)] = piece_ref[...]


def place_slices(me, pieces):
    smem, vmem = pl.BlockSpec(memory_space=pltpu.SMEM), pl.BlockSpec(memory_space=pltpu.VMEM)
    rows, width = pieces[0].shape
    return pl.pallas_call(
        place_kernel,
        out_shape=jax.ShapeDtypeStruct((rows, width * len(pieces)), pieces[0].dtype),
        in_specs=[smem] + [vmem] * len(pieces),
        out_specs=vmem,
        compiler_params=pltpu.CompilerParams(vmem_limit_bytes=4 << 20),
        cost_estimate=SMALL,
    )(me.reshape(1), *pieces)


def body(
    tokens,
    grad_out,
    gate_weight,
    up_weight,
    down_weight,
    block_kind,
    block_ff,
    block_d,
    block_owner,
):
    n_dp, n_tensor = lax.axis_size("dp"), lax.axis_size("tensor")
    n_z = n_tensor // 2
    bits = n_dp.bit_length() - 1
    rows, features = tokens.shape
    width, units = gate_weight.shape
    me = lax.axis_index("dp")
    bf16, f32 = jnp.bfloat16, jnp.float32
    parts = min(bits, 2)
    part = units // parts
    orders = [[(q + s) % bits for s in range(bits)] for q in range(parts)]
    masks = chunk_masks(n_z)
    stages = 2 * bits

    chain = []

    def ordered(*values):
        if not chain:
            return values
        return lax.optimization_barrier(values + tuple(chain))[: len(values)]

    def done(*results):
        chain[:] = results

    def over_dp(value, mask):
        return lax.ppermute(value, "dp", xor_perm(n_dp, mask))

    def over_core(value):
        return lax.ppermute(value, "tensor", xor_perm(n_tensor, 1))

    def over_z(value, mask):
        return lax.ppermute(value, "tensor", z_perm(n_tensor, mask))

    held, window_held, shards, other = {}, {}, {}, {}
    ready, flying, local, owns, out_flying, terms = {}, {}, {}, {}, {}, {}

    def hop(held, mask):
        low = mask & -mask
        held[mask] = over_z(held[mask ^ low], low)

    def relay(held, mask):
        (held[mask],) = ordered(held[mask])
        low = mask & -mask if mask else n_z
        for step in range(low.bit_length() - 1):
            hop(held, mask | 1 << step)

    def swap(k):
        got = ordered(*[held[mask] for mask in masks[k]])
        shards[k] = jnp.stack(got)
        other[k] = over_core(shards[k])
        done(shards[k])

    pieces = []
    for mask in range(n_dp):
        start = (me ^ mask) * width
        piece = jnp.stack(
            [lax.dynamic_slice_in_dim(x, start, width, axis=1) for x in (grad_out, tokens)]
        )
        pieces.append(over_dp(piece, mask) if mask else piece)
    if rows % 16 == 0:
        gate_weight, up_weight, down_weight = in_vmem(gate_weight, up_weight, down_weight)
        done(gate_weight, up_weight, down_weight)
    held[0] = jnp.stack(ordered(*pieces), axis=1)
    for step in range(n_z.bit_length() - 1):
        hop(held, 1 << step)

    def forward(k):
        own, others = ordered(shards[k], other[k])
        weights = (gate_weight, up_weight, down_weight)
        if rows % 16 == 0:
            first = [order[0] for order in orders]
            keep, fly = forward_partials(first, own, others, *weights)
            shape = (3,) + (2,) * (bits - 1) + (-1, part)
            local[k] = [x.reshape(shape) for x in keep]
            ready[k] = [x.reshape(shape) for x in fly]
            done(*local[k], *ready[k])
            return
        chunk = jnp.stack([own, others], axis=3).transpose(1, 2, 0, 3, 4, 5)
        chunk = chunk.reshape(2, -1, width)
        gate = jnp.dot(chunk[1], gate_weight, preferred_element_type=f32).astype(bf16)
        upward = jnp.dot(chunk[1], up_weight, preferred_element_type=f32).astype(bf16)
        hidden_grad = lax.dot_general(
            chunk[0], down_weight, CONTRACT_LAST, preferred_element_type=f32
        ).astype(bf16)
        sums = jnp.stack([gate, upward, hidden_grad])
        values = []
        for q in range(parts):
            value = sums[:, :, q * part : (q + 1) * part]
            values.append(value.reshape((3,) + (2,) * bits + (-1, part)))
        ready[k] = values
        done(*values)

    def add_halves(keep, fly):
        got = ordered(*fly)
        return [x.astype(f32) + y.astype(f32) for x, y in zip(keep, got)]

    def gradients(sums):
        hiddens, values = [], []
        for g, u, h in sums:
            sig = jax.nn.sigmoid(g)
            silu = g * sig
            hiddens.append((silu * u).astype(bf16))
            gate_grad = (h * u * sig * (1.0 + g * (1.0 - sig))).astype(bf16)
            up_grad = (h * silu).astype(bf16)
            values.append(jnp.stack([gate_grad, up_grad]))
        return hiddens, values

    def join(values, got, s):
        joined = []
        for value, more, order in zip(values, got, orders):
            order = order[::-1]
            axis = sum(1 for bit in order[:s] if bit > order[s])
            joined.append(jnp.stack([value, more], axis=axis))
        return joined

    def send(k, s):
        values = ordered(*ready[k])
        if s >= bits:
            local[k] = values
            flying[k] = [
                over_dp(value, 1 << order[::-1][s - bits]) for value, order in zip(values, orders)
            ]
            return
        if k != "delta" and s == 0 and rows % 16 == 0:
            flying[k] = [over_dp(x, 1 << order[s]) for x, order in zip(values, orders)]
            return
        local[k], fly = [], []
        for value, order in zip(values, orders):
            axis = (k != "delta") + sorted(order[s:], reverse=True).index(order[s])
            local[k].append(lax.index_in_dim(value, 0, axis, keepdims=False))
            fly.append(lax.index_in_dim(value, 1, axis, keepdims=False).astype(bf16))
        flying[k] = [over_dp(x, 1 << order[s]) for x, order in zip(fly, orders)]

    def take(k, s):
        if s < bits:
            values = add_halves(local[k], flying[k])
            if k == "delta":
                ready[k] = values
                done(*values)
                return
        else:
            values = join(local[k], ordered(*flying[k]), s - bits)
        if s == bits - 1:
            hiddens, values = gradients(values)
            owns[k] = (hiddens, values)
            done(*hiddens, *values)
        else:
            done(*values)
        ready[k] = values

    def merge():
        ready[0] = [
            jnp.concatenate(values, axis=-2) for values in zip(ready["own"], ready["near"])
        ]
        done(*ready[0])

    def part_again():
        count = 2 * rows
        ready["own"] = [x[..., :count, :] for x in ready[0]]
        ready["rest"] = [
            jnp.concatenate([x[..., count:, :], y], axis=-2) for x, y in zip(ready[0], ready[1])
        ]
        done(*ready["rest"])

    def finish(k):
        got = ordered(*flying[k])
        if rows % 16 == 0:
            count = 2 * len(masks[k]) * rows
            pieces, places = [], []
            for q in range(parts):
                order = orders[q][::-1]
                known = sorted(order[:-1], reverse=True)
                windows = [
                    sum(bit << at for bit, at in zip(index, known))
                    for index in np.ndindex((2,) * (bits - 1))
                ]
                for here, piece in enumerate((local[k][q], got[q])):
                    pieces.append(piece.reshape(-1, 2, count, part))
                    starts = [(window | here << order[-1]) * count for window in windows]
                    places.append((tuple(starts), q * part))
            out = backward_partials(pieces, tuple(places), gate_weight, up_weight)
        else:
            gathered = []
            for value in join(local[k], got, bits - 1):
                value = value.reshape((n_dp, 2, -1, part))
                gathered.append(jnp.swapaxes(value, 0, 1).reshape(2, -1, part))
            gathered = jnp.concatenate(gathered, axis=2)
            out = sum(
                lax.dot_general(x, w, CONTRACT_LAST, preferred_element_type=f32)
                for x, w in zip(gathered, (gate_weight, up_weight))
            )
        out = out.reshape(n_dp, len(masks[k]), 2, rows, width)
        send = out[:, :, 1].astype(bf16)
        out_flying[k] = (out[:, :, 0], over_core(send))
        done(send)

    def send_home(k):
        own, got = out_flying[k]
        (got,) = ordered(got)
        out = own + got.astype(f32)
        for place, mask in enumerate(masks[k]):
            term = out[:, place]
            if mask:
                term = term.astype(bf16)
                terms[mask] = over_z(term, mask)
            else:
                terms[mask] = term
            done(term)

    def collect(sources):
        total = 0.0
        for term in ordered(*[terms[mask] for mask in sources]):
            total = total + term.astype(f32)
        done(total)
        return total

    def window_rows(mask):
        if mask == 0:
            window_held[0] = jnp.stack(ordered(grad_out, tokens))
        else:
            places = list(window_held)
            values = ordered(*[window_held[place] for place in places])
            window_held.update(zip(places, values))
        if mask + 1 < n_z:
            hop(window_held, mask + 1)
            return
        rows_there = [window_held[mask] for k in range(2) for mask in masks[k]]
        window_held["own"] = jnp.stack(rows_there, axis=1)
        window_held["other"] = over_core(window_held["own"])
        done(window_held["own"])

    def delta_terms():
        windows = ordered(window_held["own"], window_held["other"])
        chunks = range(2)
        deltas = window_deltas(
            n_dp,
            units,
            me,
            block_kind,
            block_ff,
            block_d,
            block_owner[:, 0],
            list(windows),
            [piece for k in chunks for piece in owns[k][0]],
            [piece for k in chunks for piece in owns[k][1]],
        )
        done(deltas)
        deltas = deltas.reshape((2,) * bits + (CAP, BLOCK, BLOCK))
        cut = BLOCK // parts
        ready["delta"] = [deltas[..., q * cut : (q + 1) * cut, :] for q in range(parts)]

    swap("own")
    forward("own")
    send("own", 0)
    for mask in masks["near"][1::2]:
        relay(held, mask)
    swap("near")
    for mask in masks[1][::2]:
        relay(held, mask)
    forward("near")
    send("near", 0)
    take("own", 0)
    swap(1)
    take("near", 0)
    merge()
    send(0, 1)
    forward(1)
    send(1, 0)
    window_rows(0)
    hops = iter(range(1, n_z))
    for s in range(2, stages - 1):
        take(0, s - 1)
        send(0, s)
        window_rows(next(hops))
        take(1, s - 2)
        send(1, s - 1)
    for mask in hops:
        window_rows(mask)
    take(1, stages - 3)
    take(0, stages - 2)
    send(1, stages - 2)
    delta_terms()
    send("delta", 0)
    take(1, stages - 2)
    part_again()
    send("rest", stages - 1)
    take("delta", 0)
    send("own", stages - 1)
    finish("rest")
    send_home("rest")
    total = collect(masks["rest"][:1])
    *flying["own"], total = lax.optimization_barrier((*flying["own"], total))
    finish("own")
    for s in range(1, bits):
        if s > 1:
            take("delta", s - 1)
        send("delta", s)
    send_home("own")

    total = total + terms[0] + collect(masks["rest"][1:])
    total = total.astype(bf16)
    pieces = [total[0]] + [over_dp(total[mask], mask) for mask in range(1, n_dp)]
    done(total)
    take("delta", bits - 1)
    deltas = jnp.concatenate(ready["delta"], axis=1)
    grad_tokens = place_slices(me, pieces)
    return (grad_tokens, deltas)


def solution(mesh):
    placed = (
        P(("groups", "dp", "tensor"), None),
        P(("groups", "dp", "tensor"), None),
        P("dp", "tensor"),
        P("dp", "tensor"),
        P("tensor", "dp"),
        P("tensor"),
        P("tensor"),
        P("tensor"),
        P("tensor", None),
    )
    return jax.shard_map(
        body,
        mesh=mesh,
        in_specs=placed,
        out_specs=(P(("groups", "dp", "tensor"), None), P(("groups", "dp", "tensor"), None, None)),
        check_vma=False,
    )
```

```python
import functools

import jax
import jax.numpy as jnp
import numpy as np
from jax import lax
from jax.experimental import pallas as pl
from jax.experimental.pallas import tpu as pltpu
from jax.sharding import PartitionSpec as P

BLOCK = 128
CAP = 5
CONTRACT_LAST = (((1,), (1,)), ((), ()))
SMALL = pl.CostEstimate(flops=1, bytes_accessed=1, transcendentals=0)


def xor_perm(size, mask):
    return [(i, i ^ mask) for i in range(size)]


def z_perm(n_tensor, mask):
    return [(rank, rank ^ 2 * mask) for rank in range(n_tensor)]


def chunk_masks(n_z):
    low, high = tuple(range(n_z // 2)), tuple(range(n_z // 2, n_z))
    return {"own": low[:1], "near": low[1:], 0: low, 1: high, "rest": low[1:] + high}


def delta_kernel(n_dp, n_pieces, me_ref, kind_ref, ff_ref, col_ref, owner_ref, *refs):
    window_refs, refs = refs[:2], refs[2:]
    hidden_refs, grad_refs, refs = refs[:n_pieces], refs[n_pieces : 2 * n_pieces], refs[2 * n_pieces :]
    out_ref, grads_ref, tokens_ref, hidden_ref, gate_ref, up_ref, used_ref = refs
    me = me_ref[0]
    out_ref[...] = jnp.zeros_like(out_ref)
    for owner in range(n_dp):
        used_ref[owner] = 0

    start = 0
    _, chips, rows, _ = window_refs[0].shape
    for chip in range(chips):
        for window_ref in window_refs:
            grads_ref[start : start + rows] = window_ref[0, chip]
            tokens_ref[start : start + rows] = window_ref[1, chip]
            start += rows
    start, column = 0, 0
    for hidden_piece, grad_piece in zip(hidden_refs, grad_refs):
        rows, units = hidden_piece.shape
        place = (slice(start, start + rows), slice(column, column + units))
        hidden_ref[place] = hidden_piece[...]
        gate_ref[place] = grad_piece[0]
        up_ref[place] = grad_piece[1]
        column += units
        if column == hidden_ref.shape[1]:
            start, column = start + rows, 0

    def step(entry, carry):
        owner = owner_ref[entry]
        slot = used_ref[owner]
        used_ref[owner] = slot + 1
        kind = kind_ref[entry]
        units = pl.ds(pl.multiple_of(ff_ref[entry] * BLOCK, BLOCK), BLOCK)
        columns = pl.ds(pl.multiple_of(col_ref[entry] * BLOCK, BLOCK), BLOCK)
        left = jnp.where(kind == 2, hidden_ref[:, units], tokens_ref[:, columns])
        right = jnp.where(
            kind == 0,
            gate_ref[:, units],
            jnp.where(kind == 1, up_ref[:, units], grads_ref[:, columns]),
        )
        out_ref[(owner ^ me) * CAP + slot] = lax.dot_general(
            left, right, (((0,), (0,)), ((), ())), preferred_element_type=jnp.float32
        )
        return carry

    lax.fori_loop(0, kind_ref.shape[0], step, 0)


def window_deltas(n_dp, units, me, kind, ff, col, owner, windows, hiddens, grads):
    _, chips, rows, features = windows[0].shape
    total = 2 * chips * rows
    if rows % 16:
        joined = jnp.stack(windows, axis=2).reshape(2, 1, total, features)
        windows = [joined[:, :, : total // 2], joined[:, :, total // 2 :]]
        across = units // hiddens[0].shape[1]
        groups = range(0, len(hiddens), across)
        hiddens = [
            jnp.concatenate([jnp.concatenate(hiddens[i : i + across], axis=1) for i in groups])
        ]
        grads = [
            jnp.concatenate([jnp.concatenate(grads[i : i + across], axis=2) for i in groups], axis=1)
        ]
    smem, vmem = pl.BlockSpec(memory_space=pltpu.SMEM), pl.BlockSpec(memory_space=pltpu.VMEM)
    bf16 = jnp.bfloat16
    return pl.pallas_call(
        functools.partial(delta_kernel, n_dp, len(hiddens)),
        out_shape=jax.ShapeDtypeStruct((n_dp * CAP, BLOCK, BLOCK), jnp.float32),
        in_specs=[smem] * 5 + [vmem] * (2 + 2 * len(hiddens)),
        out_specs=vmem,
        scratch_shapes=[
            pltpu.VMEM((total, features), bf16),
            pltpu.VMEM((total, features), bf16),
            pltpu.VMEM((total, units), bf16),
            pltpu.VMEM((total, units), bf16),
            pltpu.VMEM((total, units), bf16),
            pltpu.SMEM((n_dp,), jnp.int32),
        ],
        compiler_params=pltpu.CompilerParams(vmem_limit_bytes=24 << 20),
        cost_estimate=SMALL,
    )(me.reshape(1), kind, ff, col, owner, *windows, *hiddens, *grads)


def load_kernel(*refs):
    n = (len(refs) - 1) // 2
    copies = [
        pltpu.make_async_copy(source, target, refs[-1].at[i])
        for i, (source, target) in enumerate(zip(refs[:n], refs[n : 2 * n]))
    ]
    for copy in copies:
        copy.start()
    for copy in copies:
        copy.wait()


def in_vmem(*weights):
    return pl.pallas_call(
        load_kernel,
        out_shape=[pltpu.VMEM(w.shape, w.dtype) for w in weights],
        in_specs=[pl.BlockSpec(memory_space=pl.ANY)] * len(weights),
        out_specs=[pl.BlockSpec(memory_space=pltpu.VMEM)] * len(weights),
        scratch_shapes=[pltpu.SemaphoreType.DMA((len(weights),))],
        compiler_params=pltpu.CompilerParams(vmem_limit_bytes=1 << 20),
        cost_estimate=SMALL,
    )(*[pltpu.with_memory_space_constraint(w, pltpu.HBM) for w in weights])


def forward_kernel(bits, own_ref, other_ref, gate_ref, up_ref, down_ref, *refs):
    out_refs, chunk_ref = refs[:-1], refs[-1]
    f32 = jnp.float32
    chips, _, windows, rows, _ = own_ref.shape
    start = 0
    for window in range(windows):
        for chip in range(chips):
            for ref in (own_ref, other_ref):
                chunk_ref[:, start : start + rows] = ref[chip, :, window]
                start += rows
    count = start // windows
    grads, tokens = chunk_ref[0], chunk_ref[1]
    part = out_refs[0].shape[3]
    block = min(part, 512)
    for q, bit in enumerate(bits):
        for column in range(0, part, block):
            units = slice(q * part + column, q * part + column + block)
            products = (
                jnp.dot(tokens, gate_ref[:, units], preferred_element_type=f32),
                jnp.dot(tokens, up_ref[:, units], preferred_element_type=f32),
                lax.dot_general(
                    grads, down_ref[units, :], CONTRACT_LAST, preferred_element_type=f32
                ),
            )
            for i, product in enumerate(products):
                product = product.astype(chunk_ref.dtype)
                places = [0, 0]
                for window in range(windows):
                    sent = window >> bit & 1
                    out_refs[2 * q + sent][i, places[sent], :, column : column + block] = product[
                        window * count : (window + 1) * count
                    ]
                    places[sent] += 1


def forward_partials(bits, own, other, gate_weight, up_weight, down_weight):
    chips, _, windows, rows, width = own.shape
    count = 2 * chips * rows
    part = gate_weight.shape[1] // len(bits)
    vmem = pl.BlockSpec(memory_space=pltpu.VMEM)
    outs = pl.pallas_call(
        functools.partial(forward_kernel, bits),
        out_shape=[jax.ShapeDtypeStruct((3, windows // 2, count, part), own.dtype)] * 2 * len(bits),
        in_specs=[vmem] * 5,
        out_specs=[vmem] * 2 * len(bits),
        scratch_shapes=[pltpu.VMEM((2, windows * count, width), own.dtype)],
        compiler_params=pltpu.CompilerParams(vmem_limit_bytes=16 << 20),
        cost_estimate=SMALL,
    )(own, other, gate_weight, up_weight, down_weight)
    return outs[::2], outs[1::2]


def backward_kernel(places, *refs):
    f32 = jnp.float32
    n = len(places)
    piece_refs, (gate_ref, up_ref, out_ref, grads_ref) = refs[:n], refs[n:]
    for piece_ref, (starts, column) in zip(piece_refs, places):
        _, _, rows, columns = piece_ref.shape
        for index, start in enumerate(starts):
            place = (slice(None), slice(start, start + rows), slice(column, column + columns))
            grads_ref[place] = piece_ref[index]
    width = out_ref.shape[1]
    block = min(width, 256)
    for column in range(0, width, block):
        cut = slice(column, column + block)
        first = lax.dot_general(
            grads_ref[0], gate_ref[cut, :], CONTRACT_LAST, preferred_element_type=f32
        )
        second = lax.dot_general(
            grads_ref[1], up_ref[cut, :], CONTRACT_LAST, preferred_element_type=f32
        )
        out_ref[:, cut] = first + second


def backward_partials(pieces, places, gate_weight, up_weight):
    width, units = gate_weight.shape
    total = max(start for starts, _ in places for start in starts) + pieces[0].shape[2]
    vmem = pl.BlockSpec(memory_space=pltpu.VMEM)
    return pl.pallas_call(
        functools.partial(backward_kernel, places),
        out_shape=jax.ShapeDtypeStruct((total, width), jnp.float32),
        in_specs=[vmem] * (len(pieces) + 2),
        out_specs=vmem,
        scratch_shapes=[pltpu.VMEM((2, total, units), jnp.bfloat16)],
        compiler_params=pltpu.CompilerParams(vmem_limit_bytes=16 << 20),
        cost_estimate=SMALL,
    )(*pieces, gate_weight, up_weight)


def place_kernel(me_ref, *refs):
    piece_refs, out_ref = refs[:-1], refs[-1]
    width = piece_refs[0].shape[1]
    for mask, piece_ref in enumerate(piece_refs):
        start = pl.multiple_of((me_ref[0] ^ mask) * width, BLOCK)
        out_ref[:, pl.ds(start, width)] = piece_ref[...]


def place_slices(me, pieces):
    smem, vmem = pl.BlockSpec(memory_space=pltpu.SMEM), pl.BlockSpec(memory_space=pltpu.VMEM)
    rows, width = pieces[0].shape
    return pl.pallas_call(
        place_kernel,
        out_shape=jax.ShapeDtypeStruct((rows, width * len(pieces)), pieces[0].dtype),
        in_specs=[smem] + [vmem] * len(pieces),
        out_specs=vmem,
        compiler_params=pltpu.CompilerParams(vmem_limit_bytes=4 << 20),
        cost_estimate=SMALL,
    )(me.reshape(1), *pieces)


def body(
    tokens,
    grad_out,
    gate_weight,
    up_weight,
    down_weight,
    block_kind,
    block_ff,
    block_d,
    block_owner,
):
    n_dp, n_tensor = lax.axis_size("dp"), lax.axis_size("tensor")
    n_z = n_tensor // 2
    bits = n_dp.bit_length() - 1
    rows, features = tokens.shape
    width, units = gate_weight.shape
    me = lax.axis_index("dp")
    bf16, f32 = jnp.bfloat16, jnp.float32
    parts = min(bits, 2)
    part = units // parts
    orders = [[(q + s) % bits for s in range(bits)] for q in range(parts)]
    masks = chunk_masks(n_z)
    stages = 2 * bits

    chain = []

    def ordered(*values):
        if not chain:
            return values
        return lax.optimization_barrier(values + tuple(chain))[: len(values)]

    def done(*results):
        chain[:] = results

    def over_dp(value, mask):
        return lax.ppermute(value, "dp", xor_perm(n_dp, mask))

    def over_core(value):
        return lax.ppermute(value, "tensor", xor_perm(n_tensor, 1))

    def over_z(value, mask):
        return lax.ppermute(value, "tensor", z_perm(n_tensor, mask))

    held, window_held, shards, other = {}, {}, {}, {}
    ready, flying, local, owns, out_flying, terms = {}, {}, {}, {}, {}, {}

    def hop(held, mask):
        low = mask & -mask
        held[mask] = over_z(held[mask ^ low], low)

    def relay(held, mask):
        (held[mask],) = ordered(held[mask])
        low = mask & -mask if mask else n_z
        for step in range(low.bit_length() - 1):
            hop(held, mask | 1 << step)
        chain.append(held[mask])

    def swap(k):
        got = ordered(*[held[mask] for mask in masks[k]])
        shards[k] = jnp.stack(got)
        other[k] = over_core(shards[k])
        done(shards[k])

    pieces = []
    for mask in range(n_dp):
        start = (me ^ mask) * width
        piece = jnp.stack(
            [lax.dynamic_slice_in_dim(x, start, width, axis=1) for x in (grad_out, tokens)]
        )
        pieces.append(over_dp(piece, mask) if mask else piece)
    if rows % 16 == 0:
        gate_weight, up_weight, down_weight = in_vmem(gate_weight, up_weight, down_weight)
        done(gate_weight, up_weight, down_weight)
    held[0] = jnp.stack(ordered(*pieces), axis=1)
    for step in range(n_z.bit_length() - 1):
        hop(held, 1 << step)

    def forward(k):
        own, others = ordered(shards[k], other[k])
        weights = (gate_weight, up_weight, down_weight)
        if rows % 16 == 0:
            first = [order[0] for order in orders]
            keep, fly = forward_partials(first, own, others, *weights)
            shape = (3,) + (2,) * (bits - 1) + (-1, part)
            local[k] = [x.reshape(shape) for x in keep]
            ready[k] = [x.reshape(shape) for x in fly]
            done(*local[k], *ready[k])
            return
        chunk = jnp.stack([own, others], axis=3).transpose(1, 2, 0, 3, 4, 5)
        chunk = chunk.reshape(2, -1, width)
        gate = jnp.dot(chunk[1], gate_weight, preferred_element_type=f32).astype(bf16)
        upward = jnp.dot(chunk[1], up_weight, preferred_element_type=f32).astype(bf16)
        hidden_grad = lax.dot_general(
            chunk[0], down_weight, CONTRACT_LAST, preferred_element_type=f32
        ).astype(bf16)
        sums = jnp.stack([gate, upward, hidden_grad])
        values = []
        for q in range(parts):
            value = sums[:, :, q * part : (q + 1) * part]
            values.append(value.reshape((3,) + (2,) * bits + (-1, part)))
        ready[k] = values
        done(*values)

    def add_halves(keep, fly):
        got = ordered(*fly)
        return [x.astype(f32) + y.astype(f32) for x, y in zip(keep, got)]

    def gradients(sums):
        hiddens, values = [], []
        for g, u, h in sums:
            sig = jax.nn.sigmoid(g)
            silu = g * sig
            hiddens.append((silu * u).astype(bf16))
            gate_grad = (h * u * sig * (1.0 + g * (1.0 - sig))).astype(bf16)
            up_grad = (h * silu).astype(bf16)
            values.append(jnp.stack([gate_grad, up_grad]))
        return hiddens, values

    def join(values, got, s):
        joined = []
        for value, more, order in zip(values, got, orders):
            order = order[::-1]
            axis = sum(1 for bit in order[:s] if bit > order[s])
            joined.append(jnp.stack([value, more], axis=axis))
        return joined

    def send(k, s):
        values = ordered(*ready[k])
        if s >= bits:
            local[k] = values
            flying[k] = [
                over_dp(value, 1 << order[::-1][s - bits]) for value, order in zip(values, orders)
            ]
            return
        if k != "delta" and s == 0 and rows % 16 == 0:
            flying[k] = [over_dp(x, 1 << order[s]) for x, order in zip(values, orders)]
            return
        local[k], fly = [], []
        for value, order in zip(values, orders):
            axis = (k != "delta") + sorted(order[s:], reverse=True).index(order[s])
            local[k].append(lax.index_in_dim(value, 0, axis, keepdims=False))
            fly.append(lax.index_in_dim(value, 1, axis, keepdims=False).astype(bf16))
        flying[k] = [over_dp(x, 1 << order[s]) for x, order in zip(fly, orders)]

    def take(k, s):
        if s < bits:
            values = add_halves(local[k], flying[k])
            if k == "delta":
                ready[k] = values
                done(*values)
                return
        else:
            values = join(local[k], ordered(*flying[k]), s - bits)
        if s == bits - 1:
            hiddens, values = gradients(values)
            owns[k] = (hiddens, values)
            done(*hiddens, *values)
        else:
            done(*values)
        ready[k] = values

    def merge():
        ready[0] = [
            jnp.concatenate(values, axis=-2) for values in zip(ready["own"], ready["near"])
        ]
        done(*ready[0])

    def part_again():
        count = 2 * rows
        ready["own"] = [x[..., :count, :] for x in ready[0]]
        ready["rest"] = [
            jnp.concatenate([x[..., count:, :], y], axis=-2) for x, y in zip(ready[0], ready[1])
        ]
        done(*ready["rest"])

    def finish(k):
        got = ordered(*flying[k])
        if rows % 16 == 0:
            count = 2 * len(masks[k]) * rows
            pieces, places = [], []
            for q in range(parts):
                order = orders[q][::-1]
                known = sorted(order[:-1], reverse=True)
                windows = [
                    sum(bit << at for bit, at in zip(index, known))
                    for index in np.ndindex((2,) * (bits - 1))
                ]
                for here, piece in enumerate((local[k][q], got[q])):
                    pieces.append(piece.reshape(-1, 2, count, part))
                    starts = [(window | here << order[-1]) * count for window in windows]
                    places.append((tuple(starts), q * part))
            out = backward_partials(pieces, tuple(places), gate_weight, up_weight)
        else:
            gathered = []
            for value in join(local[k], got, bits - 1):
                value = value.reshape((n_dp, 2, -1, part))
                gathered.append(jnp.swapaxes(value, 0, 1).reshape(2, -1, part))
            gathered = jnp.concatenate(gathered, axis=2)
            out = sum(
                lax.dot_general(x, w, CONTRACT_LAST, preferred_element_type=f32)
                for x, w in zip(gathered, (gate_weight, up_weight))
            )
        out = out.reshape(n_dp, len(masks[k]), 2, rows, width)
        send = out[:, :, 1].astype(bf16)
        out_flying[k] = (out[:, :, 0], over_core(send))
        done(send)

    def send_home(k):
        own, got = out_flying[k]
        (got,) = ordered(got)
        out = own + got.astype(f32)
        for place, mask in enumerate(masks[k]):
            term = out[:, place]
            if mask:
                term = term.astype(bf16)
                terms[mask] = over_z(term, mask)
            else:
                terms[mask] = term
            done(term)

    def collect(sources):
        total = 0.0
        for term in ordered(*[terms[mask] for mask in sources]):
            total = total + term.astype(f32)
        done(total)
        return total

    def window_rows(mask):
        if mask == 0:
            window_held[0] = jnp.stack(ordered(grad_out, tokens))
        else:
            places = list(window_held)
            values = ordered(*[window_held[place] for place in places])
            window_held.update(zip(places, values))
        if mask + 1 < n_z:
            hop(window_held, mask + 1)
            return
        rows_there = [window_held[mask] for k in range(2) for mask in masks[k]]
        window_held["own"] = jnp.stack(rows_there, axis=1)
        window_held["other"] = over_core(window_held["own"])
        done(window_held["own"])

    def delta_terms():
        windows = ordered(window_held["own"], window_held["other"])
        chunks = range(2)
        deltas = window_deltas(
            n_dp,
            units,
            me,
            block_kind,
            block_ff,
            block_d,
            block_owner[:, 0],
            list(windows),
            [piece for k in chunks for piece in owns[k][0]],
            [piece for k in chunks for piece in owns[k][1]],
        )
        done(deltas)
        deltas = deltas.reshape((2,) * bits + (CAP, BLOCK, BLOCK))
        cut = BLOCK // parts
        ready["delta"] = [deltas[..., q * cut : (q + 1) * cut, :] for q in range(parts)]

    swap("own")
    forward("own")
    send("own", 0)
    for mask in masks["near"][1::2]:
        relay(held, mask)
    swap("near")
    forward("near")
    send("near", 0)
    take("own", 0)
    for mask in masks[1][::2]:
        relay(held, mask)
    take("near", 0)
    merge()
    for s in range(1, stages - 1):
        send(0, s)
        if s == stages - 2:
            swap(1)
            forward(1)
            send(1, 0)
        take(0, s)
    window_rows(0)
    hops = iter(range(1, n_z))
    for s in range(1, stages - 2):
        window_rows(next(hops))
        take(1, s - 1)
        send(1, s)
    for mask in hops:
        window_rows(mask)
    take(1, stages - 3)
    send(1, stages - 2)
    delta_terms()
    send("delta", 0)
    take(1, stages - 2)
    part_again()
    send("rest", stages - 1)
    take("delta", 0)
    send("own", stages - 1)
    finish("rest")
    send_home("rest")
    total = collect(masks["rest"][:1])
    *flying["own"], total = lax.optimization_barrier((*flying["own"], total))
    finish("own")
    for s in range(1, bits):
        if s > 1:
            take("delta", s - 1)
        send("delta", s)
    send_home("own")

    total = total + terms[0] + collect(masks["rest"][1:])
    total = total.astype(bf16)
    pieces = [total[0]] + [over_dp(total[mask], mask) for mask in range(1, n_dp)]
    done(total)
    take("delta", bits - 1)
    deltas = jnp.concatenate(ready["delta"], axis=1)
    grad_tokens = place_slices(me, pieces)
    return (grad_tokens, deltas)


def solution(mesh):
    placed = (
        P(("groups", "dp", "tensor"), None),
        P(("groups", "dp", "tensor"), None),
        P("dp", "tensor"),
        P("dp", "tensor"),
        P("tensor", "dp"),
        P("tensor"),
        P("tensor"),
        P("tensor"),
        P("tensor", None),
    )
    return jax.shard_map(
        body,
        mesh=mesh,
        in_specs=placed,
        out_specs=(P(("groups", "dp", "tensor"), None), P(("groups", "dp", "tensor"), None, None)),
        check_vma=False,
    )
```

```python
import functools

import jax
import jax.numpy as jnp
import numpy as np
from jax import lax
from jax.experimental import pallas as pl
from jax.experimental.pallas import tpu as pltpu
from jax.sharding import PartitionSpec as P

BLOCK = 128
CAP = 5
CONTRACT_LAST = (((1,), (1,)), ((), ()))
SMALL = pl.CostEstimate(flops=1, bytes_accessed=1, transcendentals=0)


def xor_perm(size, mask):
    return [(i, i ^ mask) for i in range(size)]


def z_perm(n_tensor, mask):
    return [(rank, rank ^ 2 * mask) for rank in range(n_tensor)]


def chunk_masks(n_z):
    low, high = tuple(range(n_z // 2)), tuple(range(n_z // 2, n_z))
    return {"own": low[:1], "near": low[1:], 0: low, 1: high, "rest": low[1:] + high}


def delta_kernel(n_dp, n_pieces, me_ref, kind_ref, ff_ref, col_ref, owner_ref, *refs):
    window_refs, refs = refs[:2], refs[2:]
    hidden_refs, grad_refs, refs = refs[:n_pieces], refs[n_pieces : 2 * n_pieces], refs[2 * n_pieces :]
    out_ref, grads_ref, tokens_ref, hidden_ref, gate_ref, up_ref, used_ref = refs
    me = me_ref[0]
    out_ref[...] = jnp.zeros_like(out_ref)
    for owner in range(n_dp):
        used_ref[owner] = 0

    start = 0
    _, chips, rows, _ = window_refs[0].shape
    for chip in range(chips):
        for window_ref in window_refs:
            grads_ref[start : start + rows] = window_ref[0, chip]
            tokens_ref[start : start + rows] = window_ref[1, chip]
            start += rows
    start, column = 0, 0
    for hidden_piece, grad_piece in zip(hidden_refs, grad_refs):
        rows, units = hidden_piece.shape
        place = (slice(start, start + rows), slice(column, column + units))
        hidden_ref[place] = hidden_piece[...]
        gate_ref[place] = grad_piece[0]
        up_ref[place] = grad_piece[1]
        column += units
        if column == hidden_ref.shape[1]:
            start, column = start + rows, 0

    def step(entry, carry):
        owner = owner_ref[entry]
        slot = used_ref[owner]
        used_ref[owner] = slot + 1
        kind = kind_ref[entry]
        units = pl.ds(pl.multiple_of(ff_ref[entry] * BLOCK, BLOCK), BLOCK)
        columns = pl.ds(pl.multiple_of(col_ref[entry] * BLOCK, BLOCK), BLOCK)
        left = jnp.where(kind == 2, hidden_ref[:, units], tokens_ref[:, columns])
        right = jnp.where(
            kind == 0,
            gate_ref[:, units],
            jnp.where(kind == 1, up_ref[:, units], grads_ref[:, columns]),
        )
        out_ref[(owner ^ me) * CAP + slot] = lax.dot_general(
            left, right, (((0,), (0,)), ((), ())), preferred_element_type=jnp.float32
        )
        return carry

    lax.fori_loop(0, kind_ref.shape[0], step, 0)


def window_deltas(n_dp, units, me, kind, ff, col, owner, windows, hiddens, grads):
    _, chips, rows, features = windows[0].shape
    total = 2 * chips * rows
    if rows % 16:
        joined = jnp.stack(windows, axis=2).reshape(2, 1, total, features)
        windows = [joined[:, :, : total // 2], joined[:, :, total // 2 :]]
        across = units // hiddens[0].shape[1]
        groups = range(0, len(hiddens), across)
        hiddens = [
            jnp.concatenate([jnp.concatenate(hiddens[i : i + across], axis=1) for i in groups])
        ]
        grads = [
            jnp.concatenate([jnp.concatenate(grads[i : i + across], axis=2) for i in groups], axis=1)
        ]
    smem, vmem = pl.BlockSpec(memory_space=pltpu.SMEM), pl.BlockSpec(memory_space=pltpu.VMEM)
    bf16 = jnp.bfloat16
    return pl.pallas_call(
        functools.partial(delta_kernel, n_dp, len(hiddens)),
        out_shape=jax.ShapeDtypeStruct((n_dp * CAP, BLOCK, BLOCK), jnp.float32),
        in_specs=[smem] * 5 + [vmem] * (2 + 2 * len(hiddens)),
        out_specs=vmem,
        scratch_shapes=[
            pltpu.VMEM((total, features), bf16),
            pltpu.VMEM((total, features), bf16),
            pltpu.VMEM((total, units), bf16),
            pltpu.VMEM((total, units), bf16),
            pltpu.VMEM((total, units), bf16),
            pltpu.SMEM((n_dp,), jnp.int32),
        ],
        compiler_params=pltpu.CompilerParams(vmem_limit_bytes=24 << 20),
        cost_estimate=SMALL,
    )(me.reshape(1), kind, ff, col, owner, *windows, *hiddens, *grads)


def load_kernel(*refs):
    n = (len(refs) - 1) // 2
    copies = [
        pltpu.make_async_copy(source, target, refs[-1].at[i])
        for i, (source, target) in enumerate(zip(refs[:n], refs[n : 2 * n]))
    ]
    for copy in copies:
        copy.start()
    for copy in copies:
        copy.wait()


def in_vmem(*weights):
    return pl.pallas_call(
        load_kernel,
        out_shape=[pltpu.VMEM(w.shape, w.dtype) for w in weights],
        in_specs=[pl.BlockSpec(memory_space=pl.ANY)] * len(weights),
        out_specs=[pl.BlockSpec(memory_space=pltpu.VMEM)] * len(weights),
        scratch_shapes=[pltpu.SemaphoreType.DMA((len(weights),))],
        compiler_params=pltpu.CompilerParams(vmem_limit_bytes=1 << 20),
        cost_estimate=SMALL,
    )(*[pltpu.with_memory_space_constraint(w, pltpu.HBM) for w in weights])


def forward_kernel(bits, own_ref, other_ref, gate_ref, up_ref, down_ref, *refs):
    out_refs, chunk_ref = refs[:-1], refs[-1]
    f32 = jnp.float32
    chips, _, windows, rows, _ = own_ref.shape
    start = 0
    for window in range(windows):
        for chip in range(chips):
            for ref in (own_ref, other_ref):
                chunk_ref[:, start : start + rows] = ref[chip, :, window]
                start += rows
    count = start // windows
    grads, tokens = chunk_ref[0], chunk_ref[1]
    part = out_refs[0].shape[3]
    block = min(part, 512)
    for q, bit in enumerate(bits):
        for column in range(0, part, block):
            units = slice(q * part + column, q * part + column + block)
            products = (
                jnp.dot(tokens, gate_ref[:, units], preferred_element_type=f32),
                jnp.dot(tokens, up_ref[:, units], preferred_element_type=f32),
                lax.dot_general(
                    grads, down_ref[units, :], CONTRACT_LAST, preferred_element_type=f32
                ),
            )
            for i, product in enumerate(products):
                product = product.astype(chunk_ref.dtype)
                places = [0, 0]
                for window in range(windows):
                    sent = window >> bit & 1
                    out_refs[2 * q + sent][i, places[sent], :, column : column + block] = product[
                        window * count : (window + 1) * count
                    ]
                    places[sent] += 1


def forward_partials(bits, own, other, gate_weight, up_weight, down_weight):
    chips, _, windows, rows, width = own.shape
    count = 2 * chips * rows
    part = gate_weight.shape[1] // len(bits)
    vmem = pl.BlockSpec(memory_space=pltpu.VMEM)
    outs = pl.pallas_call(
        functools.partial(forward_kernel, bits),
        out_shape=[jax.ShapeDtypeStruct((3, windows // 2, count, part), own.dtype)] * 2 * len(bits),
        in_specs=[vmem] * 5,
        out_specs=[vmem] * 2 * len(bits),
        scratch_shapes=[pltpu.VMEM((2, windows * count, width), own.dtype)],
        compiler_params=pltpu.CompilerParams(vmem_limit_bytes=16 << 20),
        cost_estimate=SMALL,
    )(own, other, gate_weight, up_weight, down_weight)
    return outs[::2], outs[1::2]


def backward_kernel(places, *refs):
    f32 = jnp.float32
    n = len(places)
    piece_refs, (gate_ref, up_ref, out_ref, grads_ref) = refs[:n], refs[n:]
    for piece_ref, (starts, column) in zip(piece_refs, places):
        _, _, rows, columns = piece_ref.shape
        for index, start in enumerate(starts):
            place = (slice(None), slice(start, start + rows), slice(column, column + columns))
            grads_ref[place] = piece_ref[index]
    width = out_ref.shape[1]
    block = min(width, 256)
    for column in range(0, width, block):
        cut = slice(column, column + block)
        first = lax.dot_general(
            grads_ref[0], gate_ref[cut, :], CONTRACT_LAST, preferred_element_type=f32
        )
        second = lax.dot_general(
            grads_ref[1], up_ref[cut, :], CONTRACT_LAST, preferred_element_type=f32
        )
        out_ref[:, cut] = first + second


def backward_partials(pieces, places, gate_weight, up_weight):
    width, units = gate_weight.shape
    total = max(start for starts, _ in places for start in starts) + pieces[0].shape[2]
    vmem = pl.BlockSpec(memory_space=pltpu.VMEM)
    return pl.pallas_call(
        functools.partial(backward_kernel, places),
        out_shape=jax.ShapeDtypeStruct((total, width), jnp.float32),
        in_specs=[vmem] * (len(pieces) + 2),
        out_specs=vmem,
        scratch_shapes=[pltpu.VMEM((2, total, units), jnp.bfloat16)],
        compiler_params=pltpu.CompilerParams(vmem_limit_bytes=16 << 20),
        cost_estimate=SMALL,
    )(*pieces, gate_weight, up_weight)


def backward_kernel(places, *refs):
    f32 = jnp.float32
    n = len(places)
    piece_refs, (gate_ref, up_ref, out_ref, grads_ref) = refs[:n], refs[n:]
    for piece_ref, (starts, column) in zip(piece_refs, places):
        _, _, rows, columns = piece_ref.shape
        for index, start in enumerate(starts):
            place = (slice(None), slice(start, start + rows), slice(column, column + columns))
            grads_ref[place] = piece_ref[index]
    width = out_ref.shape[1]
    block = min(width, 256)
    for column in range(0, width, block):
        cut = slice(column, column + block)
        first = lax.dot_general(
            grads_ref[0], gate_ref[cut, :], CONTRACT_LAST, preferred_element_type=f32
        )
        second = lax.dot_general(
            grads_ref[1], up_ref[cut, :], CONTRACT_LAST, preferred_element_type=f32
        )
        out_ref[:, cut] = first + second


def backward_partials(pieces, places, gate_weight, up_weight):
    width, units = gate_weight.shape
    total = max(start for starts, _ in places for start in starts) + pieces[0].shape[2]
    vmem = pl.BlockSpec(memory_space=pltpu.VMEM)
    return pl.pallas_call(
        functools.partial(backward_kernel, places),
        out_shape=jax.ShapeDtypeStruct((total, width), jnp.float32),
        in_specs=[vmem] * (len(pieces) + 2),
        out_specs=vmem,
        scratch_shapes=[pltpu.VMEM((2, total, units), jnp.bfloat16)],
        compiler_params=pltpu.CompilerParams(vmem_limit_bytes=16 << 20),
        cost_estimate=SMALL,
    )(*pieces, gate_weight, up_weight)


def place_kernel(me_ref, *refs):
    piece_refs, out_ref = refs[:-1], refs[-1]
    width = piece_refs[0].shape[1]
    for mask, piece_ref in enumerate(piece_refs):
        start = pl.multiple_of((me_ref[0] ^ mask) * width, BLOCK)
        out_ref[:, pl.ds(start, width)] = piece_ref[...]


def place_slices(me, pieces):
    smem, vmem = pl.BlockSpec(memory_space=pltpu.SMEM), pl.BlockSpec(memory_space=pltpu.VMEM)
    rows, width = pieces[0].shape
    return pl.pallas_call(
        place_kernel,
        out_shape=jax.ShapeDtypeStruct((rows, width * len(pieces)), pieces[0].dtype),
        in_specs=[smem] + [vmem] * len(pieces),
        out_specs=vmem,
        compiler_params=pltpu.CompilerParams(vmem_limit_bytes=4 << 20),
        cost_estimate=SMALL,
    )(me.reshape(1), *pieces)


def body(
    tokens,
    grad_out,
    gate_weight,
    up_weight,
    down_weight,
    block_kind,
    block_ff,
    block_d,
    block_owner,
):
    n_dp, n_tensor = lax.axis_size("dp"), lax.axis_size("tensor")
    n_z = n_tensor // 2
    bits = n_dp.bit_length() - 1
    rows, features = tokens.shape
    width, units = gate_weight.shape
    me = lax.axis_index("dp")
    bf16, f32 = jnp.bfloat16, jnp.float32
    parts = min(bits, 2)
    part = units // parts
    orders = [[(q + s) % bits for s in range(bits)] for q in range(parts)]
    masks = chunk_masks(n_z)
    stages = 2 * bits

    chain = []

    def ordered(*values):
        if not chain:
            return values
        return lax.optimization_barrier(values + tuple(chain))[: len(values)]

    def done(*results):
        chain[:] = results

    def over_dp(value, mask):
        return lax.ppermute(value, "dp", xor_perm(n_dp, mask))

    def over_core(value):
        return lax.ppermute(value, "tensor", xor_perm(n_tensor, 1))

    def over_z(value, mask):
        return lax.ppermute(value, "tensor", z_perm(n_tensor, mask))

    held, window_held, shards, other = {}, {}, {}, {}
    ready, flying, local, owns, out_flying, terms = {}, {}, {}, {}, {}, {}

    def hop(held, mask):
        low = mask & -mask
        held[mask] = over_z(held[mask ^ low], low)

    def relay(held, mask):
        (held[mask],) = ordered(held[mask])
        low = mask & -mask if mask else n_z
        for step in range(low.bit_length() - 1):
            hop(held, mask | 1 << step)
        chain.append(held[mask])

    def swap(k):
        got = ordered(*[held[mask] for mask in masks[k]])
        shards[k] = jnp.stack(got)
        other[k] = over_core(shards[k])
        done(shards[k])

    pieces = []
    for mask in range(n_dp):
        start = (me ^ mask) * width
        piece = jnp.stack(
            [lax.dynamic_slice_in_dim(x, start, width, axis=1) for x in (grad_out, tokens)]
        )
        pieces.append(over_dp(piece, mask) if mask else piece)
    if rows % 16 == 0:
        gate_weight, up_weight, down_weight = in_vmem(gate_weight, up_weight, down_weight)
        done(gate_weight, up_weight, down_weight)
    held[0] = jnp.stack(ordered(*pieces), axis=1)
    for step in range(n_z.bit_length() - 1):
        hop(held, 1 << step)

    def forward(k):
        own, others = ordered(shards[k], other[k])
        weights = (gate_weight, up_weight, down_weight)
        if rows % 16 == 0:
            first = [order[0] for order in orders]
            keep, fly = forward_partials(first, own, others, *weights)
            shape = (3,) + (2,) * (bits - 1) + (-1, part)
            local[k] = [x.reshape(shape) for x in keep]
            ready[k] = [x.reshape(shape) for x in fly]
            done(*local[k], *ready[k])
            return
        chunk = jnp.stack([own, others], axis=3).transpose(1, 2, 0, 3, 4, 5)
        chunk = chunk.reshape(2, -1, width)
        gate = jnp.dot(chunk[1], gate_weight, preferred_element_type=f32).astype(bf16)
        upward = jnp.dot(chunk[1], up_weight, preferred_element_type=f32).astype(bf16)
        hidden_grad = lax.dot_general(
            chunk[0], down_weight, CONTRACT_LAST, preferred_element_type=f32
        ).astype(bf16)
        sums = jnp.stack([gate, upward, hidden_grad])
        values = []
        for q in range(parts):
            value = sums[:, :, q * part : (q + 1) * part]
            values.append(value.reshape((3,) + (2,) * bits + (-1, part)))
        ready[k] = values
        done(*values)

    def add_halves(keep, fly):
        got = ordered(*fly)
        return [x.astype(f32) + y.astype(f32) for x, y in zip(keep, got)]

    def gradients(sums):
        hiddens, values = [], []
        for g, u, h in sums:
            sig = jax.nn.sigmoid(g)
            silu = g * sig
            hiddens.append((silu * u).astype(bf16))
            gate_grad = (h * u * sig * (1.0 + g * (1.0 - sig))).astype(bf16)
            up_grad = (h * silu).astype(bf16)
            values.append(jnp.stack([gate_grad, up_grad]))
        return hiddens, values

    def join(values, got, s):
        joined = []
        for value, more, order in zip(values, got, orders):
            order = order[::-1]
            axis = sum(1 for bit in order[:s] if bit > order[s])
            joined.append(jnp.stack([value, more], axis=axis))
        return joined

    def send(k, s):
        values = ordered(*ready[k])
        if s >= bits:
            local[k] = values
            flying[k] = [
                over_dp(value, 1 << order[::-1][s - bits]) for value, order in zip(values, orders)
            ]
            return
        if k != "delta" and s == 0 and rows % 16 == 0:
            flying[k] = [over_dp(x, 1 << order[s]) for x, order in zip(values, orders)]
            return
        local[k], fly = [], []
        for value, order in zip(values, orders):
            axis = (k != "delta") + sorted(order[s:], reverse=True).index(order[s])
            local[k].append(lax.index_in_dim(value, 0, axis, keepdims=False))
            fly.append(lax.index_in_dim(value, 1, axis, keepdims=False).astype(bf16))
        flying[k] = [over_dp(x, 1 << order[s]) for x, order in zip(fly, orders)]

    def take(k, s):
        if s < bits:
            values = add_halves(local[k], flying[k])
            if k == "delta":
                ready[k] = values
                done(*values)
                return
        else:
            values = join(local[k], ordered(*flying[k]), s - bits)
        if s == bits - 1:
            hiddens, values = gradients(values)
            owns[k] = (hiddens, values)
            done(*hiddens, *values)
        else:
            done(*values)
        ready[k] = values

    def merge():
        ready[0] = [
            jnp.concatenate(values, axis=-2) for values in zip(ready["own"], ready["near"])
        ]
        done(*ready[0])

    def part_again():
        count = 2 * rows
        ready["own"] = [x[..., :count, :] for x in ready[0]]
        ready["rest"] = [
            jnp.concatenate([x[..., count:, :], y], axis=-2) for x, y in zip(ready[0], ready[1])
        ]
        done(*ready["rest"])

    def finish(k):
        got = ordered(*flying[k])
        if rows % 16 == 0:
            count = 2 * len(masks[k]) * rows
            pieces, places = [], []
            for q in range(parts):
                order = orders[q][::-1]
                known = sorted(order[:-1], reverse=True)
                windows = [
                    sum(bit << at for bit, at in zip(index, known))
                    for index in np.ndindex((2,) * (bits - 1))
                ]
                for here, piece in enumerate((local[k][q], got[q])):
                    pieces.append(piece.reshape(-1, 2, count, part))
                    starts = [(window | here << order[-1]) * count for window in windows]
                    places.append((tuple(starts), q * part))
            out = backward_partials(pieces, tuple(places), gate_weight, up_weight)
        else:
            gathered = []
            for value in join(local[k], got, bits - 1):
                value = value.reshape((n_dp, 2, -1, part))
                gathered.append(jnp.swapaxes(value, 0, 1).reshape(2, -1, part))
            gathered = jnp.concatenate(gathered, axis=2)
            out = sum(
                lax.dot_general(x, w, CONTRACT_LAST, preferred_element_type=f32)
                for x, w in zip(gathered, (gate_weight, up_weight))
            )
        out = out.reshape(n_dp, len(masks[k]), 2, rows, width)
        send = out[:, :, 1].astype(bf16)
        out_flying[k] = (out[:, :, 0], over_core(send))
        done(send)

    def send_home(k):
        own, got = out_flying[k]
        (got,) = ordered(got)
        out = own + got.astype(f32)
        for place, mask in enumerate(masks[k]):
            term = out[:, place]
            if mask:
                term = term.astype(bf16)
                terms[mask] = over_z(term, mask)
            else:
                terms[mask] = term
            done(term)

    def collect(sources):
        total = 0.0
        for term in ordered(*[terms[mask] for mask in sources]):
            total = total + term.astype(f32)
        done(total)
        return total

    def window_rows(step):
        if step == 0:
            window_held[0] = jnp.stack(ordered(grad_out, tokens))
        else:
            places = list(window_held)
            window_held.update(zip(places, ordered(*[window_held[place] for place in places])))
            chain.append(window_held[places[-1]])
        if step + 1 < n_z:
            mask = sum(1 << i for i in range(n_z.bit_length() - 1) if (step + 1) * 2 << i & n_z)
            hop(window_held, mask)
            return
        rows_there = [window_held[mask] for k in range(2) for mask in masks[k]]
        window_held["own"] = jnp.stack(rows_there, axis=1)
        window_held["other"] = over_core(window_held["own"])
        done(window_held["own"])

    def delta_terms():
        windows = ordered(window_held["own"], window_held["other"])
        chunks = range(2)
        deltas = window_deltas(
            n_dp,
            units,
            me,
            block_kind,
            block_ff,
            block_d,
            block_owner[:, 0],
            list(windows),
            [piece for k in chunks for piece in owns[k][0]],
            [piece for k in chunks for piece in owns[k][1]],
        )
        done(deltas)
        deltas = deltas.reshape((2,) * bits + (CAP, BLOCK, BLOCK))
        cut = BLOCK // parts
        ready["delta"] = [deltas[..., q * cut : (q + 1) * cut, :] for q in range(parts)]

    swap("own")
    forward("own")
    send("own", 0)
    for mask in masks["near"][1::2]:
        relay(held, mask)
    swap("near")
    forward("near")
    send("near", 0)
    take("own", 0)
    for mask in masks[1][::2]:
        relay(held, mask)
    take("near", 0)
    merge()
    for s in range(1, stages - 1):
        send(0, s)
        if s == stages - 2:
            swap(1)
            forward(1)
            send(1, 0)
        take(0, s)
    window_rows(0)
    window_rows(1)
    for s in range(1, stages - 2):
        take(1, s - 1)
        send(1, s)
    for step in range(2, n_z - 1):
        window_rows(step)
    take(1, stages - 3)
    send(1, stages - 2)
    window_rows(n_z - 1)
    take(1, stages - 2)
    part_again()
    send("rest", stages - 1)
    delta_terms()
    send("delta", 0)
    take("delta", 0)
    send("own", stages - 1)
    finish("rest")
    send_home("rest")
    total = collect(masks["rest"][:1])
    *flying["own"], total = lax.optimization_barrier((*flying["own"], total))
    finish("own")
    for s in range(1, bits):
        if s > 1:
            take("delta", s - 1)
        send("delta", s)
    send_home("own")

    total = total + terms[0] + collect(masks["rest"][1:])
    total = total.astype(bf16)
    slots = jnp.arange(n_dp, dtype=jnp.int32)
    pieces = lax.all_to_all(total.at[slots ^ me].get(mode="promise_in_bounds"), "dp", 0, 0)
    done(total)
    take("delta", bits - 1)
    deltas = jnp.concatenate(ready["delta"], axis=1)
    grad_tokens = jnp.swapaxes(pieces, 0, 1).reshape(rows, features)
    return (grad_tokens, deltas)


def solution(mesh):
    placed = (
        P(("groups", "dp", "tensor"), None),
        P(("groups", "dp", "tensor"), None),
        P("dp", "tensor"),
        P("dp", "tensor"),
        P("tensor", "dp"),
        P("tensor"),
        P("tensor"),
        P("tensor"),
        P("tensor", None),
    )
    return jax.shard_map(
        body,
        mesh=mesh,
        in_specs=placed,
        out_specs=(P(("groups", "dp", "tensor"), None), P(("groups", "dp", "tensor"), None, None)),
        check_vma=False,
    )
```

```python
import functools

import jax
import jax.numpy as jnp
import numpy as np
from jax import lax
from jax.experimental import pallas as pl
from jax.experimental.pallas import tpu as pltpu
from jax.sharding import PartitionSpec as P

BLOCK = 128
CAP = 5
CONTRACT_LAST = (((1,), (1,)), ((), ()))
SMALL = pl.CostEstimate(flops=1, bytes_accessed=1, transcendentals=0)


def xor_perm(size, mask):
    return [(i, i ^ mask) for i in range(size)]


def z_perm(n_tensor, mask):
    return [(rank, rank ^ 2 * mask) for rank in range(n_tensor)]


def chunk_masks(n_z):
    low, high = tuple(range(n_z // 2)), tuple(range(n_z // 2, n_z))
    return {"own": low[:1], "near": low[1:], 0: low, 1: high, "rest": low[1:] + high}


def delta_kernel(n_dp, n_pieces, me_ref, kind_ref, ff_ref, col_ref, owner_ref, *refs):
    window_refs, refs = refs[:2], refs[2:]
    hidden_refs, grad_refs, refs = refs[:n_pieces], refs[n_pieces : 2 * n_pieces], refs[2 * n_pieces :]
    out_ref, grads_ref, tokens_ref, hidden_ref, gate_ref, up_ref, used_ref = refs
    me = me_ref[0]
    out_ref[...] = jnp.zeros_like(out_ref)
    for owner in range(n_dp):
        used_ref[owner] = 0

    start = 0
    _, chips, rows, _ = window_refs[0].shape
    for chip in range(chips):
        for window_ref in window_refs:
            grads_ref[start : start + rows] = window_ref[0, chip]
            tokens_ref[start : start + rows] = window_ref[1, chip]
            start += rows
    start, column = 0, 0
    for hidden_piece, grad_piece in zip(hidden_refs, grad_refs):
        rows, units = hidden_piece.shape
        place = (slice(start, start + rows), slice(column, column + units))
        hidden_ref[place] = hidden_piece[...]
        gate_ref[place] = grad_piece[0]
        up_ref[place] = grad_piece[1]
        column += units
        if column == hidden_ref.shape[1]:
            start, column = start + rows, 0

    def step(entry, carry):
        owner = owner_ref[entry]
        slot = used_ref[owner]
        used_ref[owner] = slot + 1
        kind = kind_ref[entry]
        units = pl.ds(pl.multiple_of(ff_ref[entry] * BLOCK, BLOCK), BLOCK)
        columns = pl.ds(pl.multiple_of(col_ref[entry] * BLOCK, BLOCK), BLOCK)
        left = jnp.where(kind == 2, hidden_ref[:, units], tokens_ref[:, columns])
        right = jnp.where(
            kind == 0,
            gate_ref[:, units],
            jnp.where(kind == 1, up_ref[:, units], grads_ref[:, columns]),
        )
        out_ref[(owner ^ me) * CAP + slot] = lax.dot_general(
            left, right, (((0,), (0,)), ((), ())), preferred_element_type=jnp.float32
        )
        return carry

    lax.fori_loop(0, kind_ref.shape[0], step, 0)


def window_deltas(n_dp, units, me, kind, ff, col, owner, windows, hiddens, grads):
    _, chips, rows, features = windows[0].shape
    total = 2 * chips * rows
    if rows % 16:
        joined = jnp.stack(windows, axis=2).reshape(2, 1, total, features)
        windows = [joined[:, :, : total // 2], joined[:, :, total // 2 :]]
        across = units // hiddens[0].shape[1]
        groups = range(0, len(hiddens), across)
        hiddens = [
            jnp.concatenate([jnp.concatenate(hiddens[i : i + across], axis=1) for i in groups])
        ]
        grads = [
            jnp.concatenate([jnp.concatenate(grads[i : i + across], axis=2) for i in groups], axis=1)
        ]
    smem, vmem = pl.BlockSpec(memory_space=pltpu.SMEM), pl.BlockSpec(memory_space=pltpu.VMEM)
    bf16 = jnp.bfloat16
    return pl.pallas_call(
        functools.partial(delta_kernel, n_dp, len(hiddens)),
        out_shape=jax.ShapeDtypeStruct((n_dp * CAP, BLOCK, BLOCK), jnp.float32),
        in_specs=[smem] * 5 + [vmem] * (2 + 2 * len(hiddens)),
        out_specs=vmem,
        scratch_shapes=[
            pltpu.VMEM((total, features), bf16),
            pltpu.VMEM((total, features), bf16),
            pltpu.VMEM((total, units), bf16),
            pltpu.VMEM((total, units), bf16),
            pltpu.VMEM((total, units), bf16),
            pltpu.SMEM((n_dp,), jnp.int32),
        ],
        compiler_params=pltpu.CompilerParams(vmem_limit_bytes=24 << 20),
        cost_estimate=SMALL,
    )(me.reshape(1), kind, ff, col, owner, *windows, *hiddens, *grads)


def load_kernel(*refs):
    n = (len(refs) - 1) // 2
    copies = [
        pltpu.make_async_copy(source, target, refs[-1].at[i])
        for i, (source, target) in enumerate(zip(refs[:n], refs[n : 2 * n]))
    ]
    for copy in copies:
        copy.start()
    for copy in copies:
        copy.wait()


def in_vmem(*weights):
    return pl.pallas_call(
        load_kernel,
        out_shape=[pltpu.VMEM(w.shape, w.dtype) for w in weights],
        in_specs=[pl.BlockSpec(memory_space=pl.ANY)] * len(weights),
        out_specs=[pl.BlockSpec(memory_space=pltpu.VMEM)] * len(weights),
        scratch_shapes=[pltpu.SemaphoreType.DMA((len(weights),))],
        compiler_params=pltpu.CompilerParams(vmem_limit_bytes=1 << 20),
        cost_estimate=SMALL,
    )(*[pltpu.with_memory_space_constraint(w, pltpu.HBM) for w in weights])


def forward_kernel(bits, own_ref, other_ref, gate_ref, up_ref, down_ref, *refs):
    out_refs, chunk_ref = refs[:-1], refs[-1]
    f32 = jnp.float32
    chips, _, windows, rows, _ = own_ref.shape
    start = 0
    for window in range(windows):
        for chip in range(chips):
            for ref in (own_ref, other_ref):
                chunk_ref[:, start : start + rows] = ref[chip, :, window]
                start += rows
    count = start // windows
    grads, tokens = chunk_ref[0], chunk_ref[1]
    part = out_refs[0].shape[3]
    block = min(part, 512)
    for q, bit in enumerate(bits):
        for column in range(0, part, block):
            units = slice(q * part + column, q * part + column + block)
            products = (
                jnp.dot(tokens, gate_ref[:, units], preferred_element_type=f32),
                jnp.dot(tokens, up_ref[:, units], preferred_element_type=f32),
                lax.dot_general(
                    grads, down_ref[units, :], CONTRACT_LAST, preferred_element_type=f32
                ),
            )
            for i, product in enumerate(products):
                product = product.astype(chunk_ref.dtype)
                places = [0, 0]
                for window in range(windows):
                    sent = window >> bit & 1
                    out_refs[2 * q + sent][i, places[sent], :, column : column + block] = product[
                        window * count : (window + 1) * count
                    ]
                    places[sent] += 1


def forward_partials(bits, own, other, gate_weight, up_weight, down_weight):
    chips, _, windows, rows, width = own.shape
    count = 2 * chips * rows
    part = gate_weight.shape[1] // len(bits)
    vmem = pl.BlockSpec(memory_space=pltpu.VMEM)
    outs = pl.pallas_call(
        functools.partial(forward_kernel, bits),
        out_shape=[jax.ShapeDtypeStruct((3, windows // 2, count, part), own.dtype)] * 2 * len(bits),
        in_specs=[vmem] * 5,
        out_specs=[vmem] * 2 * len(bits),
        scratch_shapes=[pltpu.VMEM((2, windows * count, width), own.dtype)],
        compiler_params=pltpu.CompilerParams(vmem_limit_bytes=16 << 20),
        cost_estimate=SMALL,
    )(own, other, gate_weight, up_weight, down_weight)
    return outs[::2], outs[1::2]


def backward_kernel(places, *refs):
    f32 = jnp.float32
    n = len(places)
    piece_refs, (gate_ref, up_ref, out_ref, grads_ref) = refs[:n], refs[n:]
    for piece_ref, (starts, column) in zip(piece_refs, places):
        _, _, rows, columns = piece_ref.shape
        for index, start in enumerate(starts):
            place = (slice(None), slice(start, start + rows), slice(column, column + columns))
            grads_ref[place] = piece_ref[index]
    width = out_ref.shape[1]
    block = min(width, 256)
    for column in range(0, width, block):
        cut = slice(column, column + block)
        first = lax.dot_general(
            grads_ref[0], gate_ref[cut, :], CONTRACT_LAST, preferred_element_type=f32
        )
        second = lax.dot_general(
            grads_ref[1], up_ref[cut, :], CONTRACT_LAST, preferred_element_type=f32
        )
        out_ref[:, cut] = first + second


def backward_partials(pieces, places, gate_weight, up_weight):
    width, units = gate_weight.shape
    total = max(start for starts, _ in places for start in starts) + pieces[0].shape[2]
    vmem = pl.BlockSpec(memory_space=pltpu.VMEM)
    return pl.pallas_call(
        functools.partial(backward_kernel, places),
        out_shape=jax.ShapeDtypeStruct((total, width), jnp.float32),
        in_specs=[vmem] * (len(pieces) + 2),
        out_specs=vmem,
        scratch_shapes=[pltpu.VMEM((2, total, units), jnp.bfloat16)],
        compiler_params=pltpu.CompilerParams(vmem_limit_bytes=16 << 20),
        cost_estimate=SMALL,
    )(*pieces, gate_weight, up_weight)


def place_kernel(me_ref, *refs):
    piece_refs, out_ref = refs[:-1], refs[-1]
    width = piece_refs[0].shape[1]
    for mask, piece_ref in enumerate(piece_refs):
        start = pl.multiple_of((me_ref[0] ^ mask) * width, BLOCK)
        out_ref[:, pl.ds(start, width)] = piece_ref[...]


def place_slices(me, pieces):
    smem, vmem = pl.BlockSpec(memory_space=pltpu.SMEM), pl.BlockSpec(memory_space=pltpu.VMEM)
    rows, width = pieces[0].shape
    return pl.pallas_call(
        place_kernel,
        out_shape=jax.ShapeDtypeStruct((rows, width * len(pieces)), pieces[0].dtype),
        in_specs=[smem] + [vmem] * len(pieces),
        out_specs=vmem,
        compiler_params=pltpu.CompilerParams(vmem_limit_bytes=4 << 20),
        cost_estimate=SMALL,
    )(me.reshape(1), *pieces)


def body(
    tokens,
    grad_out,
    gate_weight,
    up_weight,
    down_weight,
    block_kind,
    block_ff,
    block_d,
    block_owner,
):
    n_dp, n_tensor = lax.axis_size("dp"), lax.axis_size("tensor")
    n_z = n_tensor // 2
    bits = n_dp.bit_length() - 1
    rows, features = tokens.shape
    width, units = gate_weight.shape
    me = lax.axis_index("dp")
    bf16, f32 = jnp.bfloat16, jnp.float32
    parts = min(bits, 2)
    part = units // parts
    orders = [[(q + s) % bits for s in range(bits)] for q in range(parts)]
    masks = chunk_masks(n_z)
    stages = 2 * bits

    chain = []

    def ordered(*values):
        if not chain:
            return values
        return lax.optimization_barrier(values + tuple(chain))[: len(values)]

    def done(*results):
        chain[:] = results

    def over_dp(value, mask):
        return lax.ppermute(value, "dp", xor_perm(n_dp, mask))

    def over_core(value):
        return lax.ppermute(value, "tensor", xor_perm(n_tensor, 1))

    def over_z(value, mask):
        return lax.ppermute(value, "tensor", z_perm(n_tensor, mask))

    held, window_held, shards, other = {}, {}, {}, {}
    ready, flying, local, owns, out_flying, terms = {}, {}, {}, {}, {}, {}

    def hop(held, mask):
        low = mask & -mask
        held[mask] = over_z(held[mask ^ low], low)

    def relay(held, mask):
        (held[mask],) = ordered(held[mask])
        low = mask & -mask if mask else n_z
        for step in range(low.bit_length() - 1):
            hop(held, mask | 1 << step)
        chain.append(held[mask])

    def swap(k):
        got = ordered(*[held[mask] for mask in masks[k]])
        shards[k] = jnp.stack(got)
        other[k] = over_core(shards[k])
        done(shards[k])

    pieces = []
    for mask in range(n_dp):
        start = (me ^ mask) * width
        piece = jnp.stack(
            [lax.dynamic_slice_in_dim(x, start, width, axis=1) for x in (grad_out, tokens)]
        )
        pieces.append(over_dp(piece, mask) if mask else piece)
    if rows % 16 == 0:
        gate_weight, up_weight, down_weight = in_vmem(gate_weight, up_weight, down_weight)
        done(gate_weight, up_weight, down_weight)
    held[0] = jnp.stack(ordered(*pieces), axis=1)
    for step in range(n_z.bit_length() - 1):
        hop(held, 1 << step)

    def forward(k):
        own, others = ordered(shards[k], other[k])
        weights = (gate_weight, up_weight, down_weight)
        if rows % 16 == 0:
            first = [order[0] for order in orders]
            keep, fly = forward_partials(first, own, others, *weights)
            shape = (3,) + (2,) * (bits - 1) + (-1, part)
            local[k] = [x.reshape(shape) for x in keep]
            ready[k] = [x.reshape(shape) for x in fly]
            done(*local[k], *ready[k])
            return
        chunk = jnp.stack([own, others], axis=3).transpose(1, 2, 0, 3, 4, 5)
        chunk = chunk.reshape(2, -1, width)
        gate = jnp.dot(chunk[1], gate_weight, preferred_element_type=f32).astype(bf16)
        upward = jnp.dot(chunk[1], up_weight, preferred_element_type=f32).astype(bf16)
        hidden_grad = lax.dot_general(
            chunk[0], down_weight, CONTRACT_LAST, preferred_element_type=f32
        ).astype(bf16)
        sums = jnp.stack([gate, upward, hidden_grad])
        values = []
        for q in range(parts):
            value = sums[:, :, q * part : (q + 1) * part]
            values.append(value.reshape((3,) + (2,) * bits + (-1, part)))
        ready[k] = values
        done(*values)

    def add_halves(keep, fly):
        got = ordered(*fly)
        return [x.astype(f32) + y.astype(f32) for x, y in zip(keep, got)]

    def gradients(sums):
        hiddens, values = [], []
        for g, u, h in sums:
            sig = jax.nn.sigmoid(g)
            silu = g * sig
            hiddens.append((silu * u).astype(bf16))
            gate_grad = (h * u * sig * (1.0 + g * (1.0 - sig))).astype(bf16)
            up_grad = (h * silu).astype(bf16)
            values.append(jnp.stack([gate_grad, up_grad]))
        return hiddens, values

    def join(values, got, s):
        joined = []
        for value, more, order in zip(values, got, orders):
            order = order[::-1]
            axis = sum(1 for bit in order[:s] if bit > order[s])
            joined.append(jnp.stack([value, more], axis=axis))
        return joined

    def send(k, s):
        values = ordered(*ready[k])
        if s >= bits:
            local[k] = values
            flying[k] = [
                over_dp(value, 1 << order[::-1][s - bits]) for value, order in zip(values, orders)
            ]
            return
        if k != "delta" and s == 0 and rows % 16 == 0:
            flying[k] = [over_dp(x, 1 << order[s]) for x, order in zip(values, orders)]
            return
        local[k], fly = [], []
        for value, order in zip(values, orders):
            axis = (k != "delta") + sorted(order[s:], reverse=True).index(order[s])
            local[k].append(lax.index_in_dim(value, 0, axis, keepdims=False))
            fly.append(lax.index_in_dim(value, 1, axis, keepdims=False).astype(bf16))
        flying[k] = [over_dp(x, 1 << order[s]) for x, order in zip(fly, orders)]

    def take(k, s):
        if s < bits:
            values = add_halves(local[k], flying[k])
            if k == "delta":
                ready[k] = values
                done(*values)
                return
        else:
            values = join(local[k], ordered(*flying[k]), s - bits)
        if s == bits - 1:
            hiddens, values = gradients(values)
            owns[k] = (hiddens, values)
            done(*hiddens, *values)
        else:
            done(*values)
        ready[k] = values

    def merge():
        ready[0] = [
            jnp.concatenate(values, axis=-2) for values in zip(ready["own"], ready["near"])
        ]
        done(*ready[0])

    def part_again():
        count = 2 * rows
        ready["own"] = [x[..., :count, :] for x in ready[0]]
        ready["rest"] = [
            jnp.concatenate([x[..., count:, :], y], axis=-2) for x, y in zip(ready[0], ready[1])
        ]
        done(*ready["rest"])

    def finish(k):
        got = ordered(*flying[k])
        if rows % 16 == 0:
            count = 2 * len(masks[k]) * rows
            pieces, places = [], []
            for q in range(parts):
                order = orders[q][::-1]
                known = sorted(order[:-1], reverse=True)
                windows = [
                    sum(bit << at for bit, at in zip(index, known))
                    for index in np.ndindex((2,) * (bits - 1))
                ]
                for here, piece in enumerate((local[k][q], got[q])):
                    pieces.append(piece.reshape(-1, 2, count, part))
                    starts = [(window | here << order[-1]) * count for window in windows]
                    places.append((tuple(starts), q * part))
            out = backward_partials(pieces, tuple(places), gate_weight, up_weight)
        else:
            gathered = []
            for value in join(local[k], got, bits - 1):
                value = value.reshape((n_dp, 2, -1, part))
                gathered.append(jnp.swapaxes(value, 0, 1).reshape(2, -1, part))
            gathered = jnp.concatenate(gathered, axis=2)
            out = sum(
                lax.dot_general(x, w, CONTRACT_LAST, preferred_element_type=f32)
                for x, w in zip(gathered, (gate_weight, up_weight))
            )
        out = out.reshape(n_dp, len(masks[k]), 2, rows, width)
        send = out[:, :, 1].astype(bf16)
        out_flying[k] = (out[:, :, 0], over_core(send))
        done(send)

    def send_home(k):
        own, got = out_flying[k]
        (got,) = ordered(got)
        out = own + got.astype(f32)
        for place, mask in enumerate(masks[k]):
            term = out[:, place]
            if mask:
                term = term.astype(bf16)
                terms[mask] = over_z(term, mask)
            else:
                terms[mask] = term
            done(term)

    def collect(sources):
        total = 0.0
        for term in ordered(*[terms[mask] for mask in sources]):
            total = total + term.astype(f32)
        done(total)
        return total

    def window_rows(step):
        if step == 0:
            window_held[0] = jnp.stack(ordered(grad_out, tokens))
        else:
            places = list(window_held)
            window_held.update(zip(places, ordered(*[window_held[place] for place in places])))
            chain.append(window_held[places[-1]])
        if step < levels:
            for mask in range(n_z):
                if mask.bit_count() == step + 1:
                    hop(window_held, mask)
            return
        rows_there = [window_held[mask] for k in range(2) for mask in masks[k]]
        window_held["own"] = jnp.stack(rows_there, axis=1)
        window_held["other"] = over_core(window_held["own"])
        done(window_held["own"])

    def delta_terms():
        windows = ordered(window_held["own"], window_held["other"])
        chunks = range(2)
        deltas = window_deltas(
            n_dp,
            units,
            me,
            block_kind,
            block_ff,
            block_d,
            block_owner[:, 0],
            list(windows),
            [piece for k in chunks for piece in owns[k][0]],
            [piece for k in chunks for piece in owns[k][1]],
        )
        done(deltas)
        deltas = deltas.reshape((2,) * bits + (CAP, BLOCK, BLOCK))
        cut = BLOCK // parts
        ready["delta"] = [deltas[..., q * cut : (q + 1) * cut, :] for q in range(parts)]

    swap("own")
    forward("own")
    send("own", 0)
    for mask in masks["near"][1::2]:
        relay(held, mask)
    swap("near")
    forward("near")
    send("near", 0)
    take("own", 0)
    for mask in masks[1][::2]:
        relay(held, mask)
    take("near", 0)
    merge()
    for s in range(1, stages - 1):
        send(0, s)
        if s == stages - 2:
            swap(1)
            forward(1)
            send(1, 0)
        take(0, s)
    levels = n_z.bit_length() - 1
    window_rows(0)
    window_rows(1)
    for s in range(1, stages - 2):
        take(1, s - 1)
        send(1, s)
    for step in range(2, levels + 1):
        window_rows(step)
    take(1, stages - 3)
    send(1, stages - 2)
    delta_terms()
    send("delta", 0)
    take(1, stages - 2)
    part_again()
    send("rest", stages - 1)
    take("delta", 0)
    send("own", stages - 1)
    finish("rest")
    send_home("rest")
    total = collect(masks["rest"][:1])
    *flying["own"], total = lax.optimization_barrier((*flying["own"], total))
    finish("own")
    for s in range(1, bits):
        if s > 1:
            take("delta", s - 1)
        send("delta", s)
    send_home("own")

    total = total + terms[0] + collect(masks["rest"][1:])
    total = total.astype(bf16)
    pieces = [total[0]] + [over_dp(total[mask], mask) for mask in range(1, n_dp)]
    done(total)
    take("delta", bits - 1)
    deltas = jnp.concatenate(ready["delta"], axis=1)
    grad_tokens = place_slices(me, pieces)
    return (grad_tokens, deltas)


def solution(mesh):
    placed = (
        P(("groups", "dp", "tensor"), None),
        P(("groups", "dp", "tensor"), None),
        P("dp", "tensor"),
        P("dp", "tensor"),
        P("tensor", "dp"),
        P("tensor"),
        P("tensor"),
        P("tensor"),
        P("tensor", None),
    )
    return jax.shard_map(
        body,
        mesh=mesh,
        in_specs=placed,
        out_specs=(P(("groups", "dp", "tensor"), None), P(("groups", "dp", "tensor"), None, None)),
        check_vma=False,
    )
```

```python
import functools

import jax
import jax.numpy as jnp
import numpy as np
from jax import lax
from jax.experimental import pallas as pl
from jax.experimental.pallas import tpu as pltpu
from jax.sharding import PartitionSpec as P

BLOCK = 128
CAP = 5
CONTRACT_LAST = (((1,), (1,)), ((), ()))
SMALL = pl.CostEstimate(flops=1, bytes_accessed=1, transcendentals=0)


def xor_perm(size, mask):
    return [(i, i ^ mask) for i in range(size)]


def z_perm(n_tensor, mask):
    return [(rank, rank ^ 2 * mask) for rank in range(n_tensor)]


def chunk_masks(n_z):
    low, high = tuple(range(n_z // 2)), tuple(range(n_z // 2, n_z))
    return {"own": low[:1], "near": low[1:], 0: low, 1: high, "rest": high + low[1:]}


def delta_kernel(n_dp, n_pieces, me_ref, kind_ref, ff_ref, col_ref, owner_ref, *refs):
    window_refs, refs = refs[:2], refs[2:]
    hidden_refs, grad_refs, refs = refs[:n_pieces], refs[n_pieces : 2 * n_pieces], refs[2 * n_pieces :]
    out_ref, grads_ref, tokens_ref, hidden_ref, gate_ref, up_ref, used_ref = refs
    me = me_ref[0]
    out_ref[...] = jnp.zeros_like(out_ref)
    for owner in range(n_dp):
        used_ref[owner] = 0

    start = 0
    _, chips, rows, _ = window_refs[0].shape
    for chip in range(chips):
        for window_ref in window_refs:
            grads_ref[start : start + rows] = window_ref[0, chip]
            tokens_ref[start : start + rows] = window_ref[1, chip]
            start += rows
    start, column = 0, 0
    for hidden_piece, grad_piece in zip(hidden_refs, grad_refs):
        rows, units = hidden_piece.shape
        place = (slice(start, start + rows), slice(column, column + units))
        hidden_ref[place] = hidden_piece[...]
        gate_ref[place] = grad_piece[0]
        up_ref[place] = grad_piece[1]
        column += units
        if column == hidden_ref.shape[1]:
            start, column = start + rows, 0

    def step(entry, carry):
        owner = owner_ref[entry]
        slot = used_ref[owner]
        used_ref[owner] = slot + 1
        kind = kind_ref[entry]
        units = pl.ds(pl.multiple_of(ff_ref[entry] * BLOCK, BLOCK), BLOCK)
        columns = pl.ds(pl.multiple_of(col_ref[entry] * BLOCK, BLOCK), BLOCK)
        left = jnp.where(kind == 2, hidden_ref[:, units], tokens_ref[:, columns])
        right = jnp.where(
            kind == 0,
            gate_ref[:, units],
            jnp.where(kind == 1, up_ref[:, units], grads_ref[:, columns]),
        )
        out_ref[(owner ^ me) * CAP + slot] = lax.dot_general(
            left, right, (((0,), (0,)), ((), ())), preferred_element_type=jnp.float32
        )
        return carry

    lax.fori_loop(0, kind_ref.shape[0], step, 0)


def window_deltas(n_dp, units, me, kind, ff, col, owner, windows, hiddens, grads):
    _, chips, rows, features = windows[0].shape
    total = 2 * chips * rows
    if rows % 16:
        joined = jnp.stack(windows, axis=2).reshape(2, 1, total, features)
        windows = [joined[:, :, : total // 2], joined[:, :, total // 2 :]]
        across = units // hiddens[0].shape[1]
        groups = range(0, len(hiddens), across)
        hiddens = [
            jnp.concatenate([jnp.concatenate(hiddens[i : i + across], axis=1) for i in groups])
        ]
        grads = [
            jnp.concatenate([jnp.concatenate(grads[i : i + across], axis=2) for i in groups], axis=1)
        ]
    smem, vmem = pl.BlockSpec(memory_space=pltpu.SMEM), pl.BlockSpec(memory_space=pltpu.VMEM)
    bf16 = jnp.bfloat16
    return pl.pallas_call(
        functools.partial(delta_kernel, n_dp, len(hiddens)),
        out_shape=jax.ShapeDtypeStruct((n_dp * CAP, BLOCK, BLOCK), jnp.float32),
        in_specs=[smem] * 5 + [vmem] * (2 + 2 * len(hiddens)),
        out_specs=vmem,
        scratch_shapes=[
            pltpu.VMEM((total, features), bf16),
            pltpu.VMEM((total, features), bf16),
            pltpu.VMEM((total, units), bf16),
            pltpu.VMEM((total, units), bf16),
            pltpu.VMEM((total, units), bf16),
            pltpu.SMEM((n_dp,), jnp.int32),
        ],
        compiler_params=pltpu.CompilerParams(vmem_limit_bytes=24 << 20),
        cost_estimate=SMALL,
    )(me.reshape(1), kind, ff, col, owner, *windows, *hiddens, *grads)


def load_kernel(*refs):
    n = (len(refs) - 1) // 2
    copies = [
        pltpu.make_async_copy(source, target, refs[-1].at[i])
        for i, (source, target) in enumerate(zip(refs[:n], refs[n : 2 * n]))
    ]
    for copy in copies:
        copy.start()
    for copy in copies:
        copy.wait()


def in_vmem(*weights):
    return pl.pallas_call(
        load_kernel,
        out_shape=[pltpu.VMEM(w.shape, w.dtype) for w in weights],
        in_specs=[pl.BlockSpec(memory_space=pl.ANY)] * len(weights),
        out_specs=[pl.BlockSpec(memory_space=pltpu.VMEM)] * len(weights),
        scratch_shapes=[pltpu.SemaphoreType.DMA((len(weights),))],
        compiler_params=pltpu.CompilerParams(vmem_limit_bytes=1 << 20),
        cost_estimate=SMALL,
    )(*[pltpu.with_memory_space_constraint(w, pltpu.HBM) for w in weights])


def forward_kernel(bits, load, own_ref, other_ref, gate_ref, up_ref, down_ref, *refs):
    if load:
        *out_refs, held_ref, chunk_ref, sem = refs
        copy = pltpu.make_async_copy(down_ref, held_ref, sem)
        copy.start()
        down_ref = held_ref
    else:
        *out_refs, chunk_ref = refs
    f32 = jnp.float32
    chips, _, windows, rows, _ = own_ref.shape
    start = 0
    for window in range(windows):
        for chip in range(chips):
            for ref in (own_ref, other_ref):
                chunk_ref[:, start : start + rows] = ref[chip, :, window]
                start += rows
    count = start // windows
    grads, tokens = chunk_ref[0], chunk_ref[1]
    part = out_refs[0].shape[3]
    block = min(part, 512)
    for i in range(3):
        if load and i == 2:
            copy.wait()
        for q, bit in enumerate(bits):
            for column in range(0, part, block):
                units = slice(q * part + column, q * part + column + block)
                if i < 2:
                    weight = (gate_ref, up_ref)[i][:, units]
                    product = jnp.dot(tokens, weight, preferred_element_type=f32)
                else:
                    product = lax.dot_general(
                        grads, down_ref[units, :], CONTRACT_LAST, preferred_element_type=f32
                    )
                product = product.astype(chunk_ref.dtype)
                places = [0, 0]
                for window in range(windows):
                    sent = window >> bit & 1
                    out_refs[2 * q + sent][i, places[sent], :, column : column + block] = product[
                        window * count : (window + 1) * count
                    ]
                    places[sent] += 1


def forward_partials(bits, load, own, other, gate_weight, up_weight, down_weight):
    chips, _, windows, rows, width = own.shape
    count = 2 * chips * rows
    part = gate_weight.shape[1] // len(bits)
    vmem = pl.BlockSpec(memory_space=pltpu.VMEM)
    shape = jax.ShapeDtypeStruct((3, windows // 2, count, part), own.dtype)
    n = 2 * len(bits)
    loaded = [pltpu.VMEM(down_weight.shape, down_weight.dtype)] * load
    if load:
        down_weight = pltpu.with_memory_space_constraint(down_weight, pltpu.HBM)
    outs = pl.pallas_call(
        functools.partial(forward_kernel, bits, load),
        out_shape=[shape] * n + loaded,
        in_specs=[vmem] * 4 + [pl.BlockSpec(memory_space=pl.ANY) if load else vmem],
        out_specs=[vmem] * (n + len(loaded)),
        scratch_shapes=[pltpu.VMEM((2, windows * count, width), own.dtype)]
        + [pltpu.SemaphoreType.DMA(())] * load,
        compiler_params=pltpu.CompilerParams(vmem_limit_bytes=16 << 20),
        cost_estimate=SMALL,
    )(own, other, gate_weight, up_weight, down_weight)
    return outs[:n:2], outs[1:n:2], outs[n:]


def backward_kernel(places, *refs):
    f32 = jnp.float32
    n = len(places)
    piece_refs, (gate_ref, up_ref, out_ref, grads_ref) = refs[:n], refs[n:]
    for piece_ref, (starts, column) in zip(piece_refs, places):
        _, _, rows, columns = piece_ref.shape
        for index, start in enumerate(starts):
            place = (slice(None), slice(start, start + rows), slice(column, column + columns))
            grads_ref[place] = piece_ref[index]
    width = out_ref.shape[1]
    block = min(width, 256)
    for column in range(0, width, block):
        cut = slice(column, column + block)
        first = lax.dot_general(
            grads_ref[0], gate_ref[cut, :], CONTRACT_LAST, preferred_element_type=f32
        )
        second = lax.dot_general(
            grads_ref[1], up_ref[cut, :], CONTRACT_LAST, preferred_element_type=f32
        )
        out_ref[:, cut] = first + second


def backward_partials(pieces, places, gate_weight, up_weight):
    width, units = gate_weight.shape
    total = max(start for starts, _ in places for start in starts) + pieces[0].shape[2]
    vmem = pl.BlockSpec(memory_space=pltpu.VMEM)
    return pl.pallas_call(
        functools.partial(backward_kernel, places),
        out_shape=jax.ShapeDtypeStruct((total, width), jnp.float32),
        in_specs=[vmem] * (len(pieces) + 2),
        out_specs=vmem,
        scratch_shapes=[pltpu.VMEM((2, total, units), jnp.bfloat16)],
        compiler_params=pltpu.CompilerParams(vmem_limit_bytes=16 << 20),
        cost_estimate=SMALL,
    )(*pieces, gate_weight, up_weight)


def place_kernel(me_ref, *refs):
    piece_refs, out_ref = refs[:-1], refs[-1]
    width = piece_refs[0].shape[1]
    for mask, piece_ref in enumerate(piece_refs):
        start = pl.multiple_of((me_ref[0] ^ mask) * width, BLOCK)
        out_ref[:, pl.ds(start, width)] = piece_ref[...]


def place_slices(me, pieces):
    smem, vmem = pl.BlockSpec(memory_space=pltpu.SMEM), pl.BlockSpec(memory_space=pltpu.VMEM)
    rows, width = pieces[0].shape
    return pl.pallas_call(
        place_kernel,
        out_shape=jax.ShapeDtypeStruct((rows, width * len(pieces)), pieces[0].dtype),
        in_specs=[smem] + [vmem] * len(pieces),
        out_specs=vmem,
        compiler_params=pltpu.CompilerParams(vmem_limit_bytes=4 << 20),
        cost_estimate=SMALL,
    )(me.reshape(1), *pieces)


def body(
    tokens,
    grad_out,
    gate_weight,
    up_weight,
    down_weight,
    block_kind,
    block_ff,
    block_d,
    block_owner,
):
    n_dp, n_tensor = lax.axis_size("dp"), lax.axis_size("tensor")
    n_z = n_tensor // 2
    bits = n_dp.bit_length() - 1
    rows, features = tokens.shape
    width, units = gate_weight.shape
    me = lax.axis_index("dp")
    bf16, f32 = jnp.bfloat16, jnp.float32
    parts = min(bits, 2)
    part = units // parts
    orders = [[(q + s) % bits for s in range(bits)] for q in range(parts)]
    masks = chunk_masks(n_z)
    stages = 2 * bits

    chain = []

    def ordered(*values):
        if not chain:
            return values
        return lax.optimization_barrier(values + tuple(chain))[: len(values)]

    def done(*results):
        chain[:] = results

    def over_dp(value, mask):
        return lax.ppermute(value, "dp", xor_perm(n_dp, mask))

    def over_core(value):
        return lax.ppermute(value, "tensor", xor_perm(n_tensor, 1))

    def over_z(value, mask):
        return lax.ppermute(value, "tensor", z_perm(n_tensor, mask))

    held, window_held, shards, other = {}, {}, {}, {}
    down_held = [down_weight]
    ready, flying, local, owns, out_flying, terms = {}, {}, {}, {}, {}, {}

    def hop(held, mask):
        low = mask & -mask
        held[mask] = over_z(held[mask ^ low], low)

    def relay(held, mask):
        (held[mask],) = ordered(held[mask])
        low = mask & -mask if mask else n_z
        for step in range(low.bit_length() - 1):
            hop(held, mask | 1 << step)
        chain.append(held[mask])

    def swap(k):
        got = ordered(*[held[mask] for mask in masks[k]])
        shards[k] = jnp.stack(got)
        other[k] = over_core(shards[k])
        done(shards[k])

    pieces = []
    for mask in range(n_dp):
        start = (me ^ mask) * width
        piece = jnp.stack(
            [lax.dynamic_slice_in_dim(x, start, width, axis=1) for x in (grad_out, tokens)]
        )
        pieces.append(over_dp(piece, mask) if mask else piece)
    if rows % 16 == 0:
        gate_weight, up_weight = in_vmem(gate_weight, up_weight)
        done(gate_weight, up_weight)
    held[0] = jnp.stack(ordered(*pieces), axis=1)
    for step in range(n_z.bit_length() - 1):
        hop(held, 1 << step)

    def forward(k):
        own, others = ordered(shards[k], other[k])
        weights = (gate_weight, up_weight, *down_held[-1:])
        if rows % 16 == 0:
            first = [order[0] for order in orders]
            keep, fly, loaded = forward_partials(first, k == "own", own, others, *weights)
            shape = (3,) + (2,) * (bits - 1) + (-1, part)
            local[k] = [x.reshape(shape) for x in keep]
            ready[k] = [x.reshape(shape) for x in fly]
            done(*local[k], *ready[k])
            down_held.extend(loaded)
            return
        chunk = jnp.stack([own, others], axis=3).transpose(1, 2, 0, 3, 4, 5)
        chunk = chunk.reshape(2, -1, width)
        gate = jnp.dot(chunk[1], gate_weight, preferred_element_type=f32).astype(bf16)
        upward = jnp.dot(chunk[1], up_weight, preferred_element_type=f32).astype(bf16)
        hidden_grad = lax.dot_general(
            chunk[0], down_weight, CONTRACT_LAST, preferred_element_type=f32
        ).astype(bf16)
        sums = jnp.stack([gate, upward, hidden_grad])
        values = []
        for q in range(parts):
            value = sums[:, :, q * part : (q + 1) * part]
            values.append(value.reshape((3,) + (2,) * bits + (-1, part)))
        ready[k] = values
        done(*values)

    def add_halves(keep, fly):
        got = ordered(*fly)
        return [x.astype(f32) + y.astype(f32) for x, y in zip(keep, got)]

    def gradients(sums):
        hiddens, values = [], []
        for g, u, h in sums:
            sig = jax.nn.sigmoid(g)
            silu = g * sig
            hiddens.append((silu * u).astype(bf16))
            gate_grad = (h * u * sig * (1.0 + g * (1.0 - sig))).astype(bf16)
            up_grad = (h * silu).astype(bf16)
            values.append(jnp.stack([gate_grad, up_grad]))
        return hiddens, values

    def join(values, got, s):
        joined = []
        for value, more, order in zip(values, got, orders):
            order = order[::-1]
            axis = sum(1 for bit in order[:s] if bit > order[s])
            joined.append(jnp.stack([value, more], axis=axis))
        return joined

    def send(k, s):
        values = ordered(*ready[k])
        if s >= bits:
            local[k] = values
            flying[k] = [
                over_dp(value, 1 << order[::-1][s - bits]) for value, order in zip(values, orders)
            ]
            return
        if k != "delta" and s == 0 and rows % 16 == 0:
            flying[k] = [over_dp(x, 1 << order[s]) for x, order in zip(values, orders)]
            return
        local[k], fly = [], []
        for value, order in zip(values, orders):
            axis = (k != "delta") + sorted(order[s:], reverse=True).index(order[s])
            local[k].append(lax.index_in_dim(value, 0, axis, keepdims=False))
            fly.append(lax.index_in_dim(value, 1, axis, keepdims=False).astype(bf16))
        flying[k] = [over_dp(x, 1 << order[s]) for x, order in zip(fly, orders)]

    def take(k, s):
        if s < bits:
            values = add_halves(local[k], flying[k])
            if k == "delta":
                ready[k] = values
                done(*values)
                return
        else:
            values = join(local[k], ordered(*flying[k]), s - bits)
        if s == bits - 1:
            hiddens, values = gradients(values)
            owns[k] = (hiddens, values)
            done(*hiddens, *values)
        else:
            done(*values)
        ready[k] = values

    def merge():
        ready[0] = [
            jnp.concatenate(values, axis=-2) for values in zip(ready["own"], ready["near"])
        ]
        done(*ready[0])

    def part_again():
        count = 2 * rows
        ready["own"] = [x[..., :count, :] for x in ready[0]]
        ready["rest"] = [
            jnp.concatenate([y, x[..., count:, :]], axis=-2) for x, y in zip(ready[0], ready[1])
        ]
        done(*ready["rest"])

    def finish(k):
        got = ordered(*flying[k])
        if rows % 16 == 0:
            count = 2 * len(masks[k]) * rows
            pieces, places = [], []
            for q in range(parts):
                order = orders[q][::-1]
                known = sorted(order[:-1], reverse=True)
                windows = [
                    sum(bit << at for bit, at in zip(index, known))
                    for index in np.ndindex((2,) * (bits - 1))
                ]
                for here, piece in enumerate((local[k][q], got[q])):
                    pieces.append(piece.reshape(-1, 2, count, part))
                    starts = [(window | here << order[-1]) * count for window in windows]
                    places.append((tuple(starts), q * part))
            out = backward_partials(pieces, tuple(places), gate_weight, up_weight)
        else:
            gathered = []
            for value in join(local[k], got, bits - 1):
                value = value.reshape((n_dp, 2, -1, part))
                gathered.append(jnp.swapaxes(value, 0, 1).reshape(2, -1, part))
            gathered = jnp.concatenate(gathered, axis=2)
            out = sum(
                lax.dot_general(x, w, CONTRACT_LAST, preferred_element_type=f32)
                for x, w in zip(gathered, (gate_weight, up_weight))
            )
        out = out.reshape(n_dp, len(masks[k]), 2, rows, width)
        send = out[:, :, 1].astype(bf16)
        out_flying[k] = (out[:, :, 0], over_core(send))
        done(send)

    def send_home(k):
        own, got = out_flying[k]
        (got,) = ordered(got)
        out = own + got.astype(f32)
        for place, mask in enumerate(masks[k]):
            term = out[:, place]
            if mask:
                term = term.astype(bf16)
                terms[mask] = over_z(term, mask)
            else:
                terms[mask] = term
            done(term)

    def collect(sources):
        total = 0.0
        for term in ordered(*[terms[mask] for mask in sources]):
            total = total + term.astype(f32)
        done(total)
        return total

    def window_rows(step):
        if step == 0:
            window_held[0] = jnp.stack(ordered(grad_out, tokens))
        else:
            places = list(window_held)
            window_held.update(zip(places, ordered(*[window_held[place] for place in places])))
            chain.append(window_held[places[-1]])
        if step < levels:
            for mask in range(n_z):
                if mask.bit_count() == step + 1:
                    hop(window_held, mask)
            return
        rows_there = [window_held[mask] for k in range(2) for mask in masks[k]]
        window_held["own"] = jnp.stack(rows_there, axis=1)
        window_held["other"] = over_core(window_held["own"])
        done(window_held["own"])

    def delta_terms():
        windows = ordered(window_held["own"], window_held["other"])
        chunks = range(2)
        deltas = window_deltas(
            n_dp,
            units,
            me,
            block_kind,
            block_ff,
            block_d,
            block_owner[:, 0],
            list(windows),
            [piece for k in chunks for piece in owns[k][0]],
            [piece for k in chunks for piece in owns[k][1]],
        )
        done(deltas)
        deltas = deltas.reshape((2,) * bits + (CAP, BLOCK, BLOCK))
        cut = BLOCK // parts
        ready["delta"] = [deltas[..., q * cut : (q + 1) * cut, :] for q in range(parts)]

    levels = n_z.bit_length() - 1
    swap("own")
    forward("own")
    send("own", 0)
    for mask in masks["near"][1::2]:
        relay(held, mask)
    swap("near")
    forward("near")
    send("near", 0)
    take("own", 0)
    for mask in masks[1][::2]:
        relay(held, mask)
    take("near", 0)
    merge()
    for s in range(1, stages - 1):
        send(0, s)
        if s == stages - 2:
            swap(1)
            forward(1)
            send(1, 0)
            window_rows(0)
        take(0, s)
    window_rows(1)
    for s in range(1, stages - 2):
        take(1, s - 1)
        send(1, s)
    for step in range(2, levels + 1):
        window_rows(step)
    take(1, stages - 3)
    send(1, stages - 2)
    delta_terms()
    send("delta", 0)
    take(1, stages - 2)
    part_again()
    send("rest", stages - 1)
    take("delta", 0)
    send("own", stages - 1)
    finish("rest")
    send_home("rest")
    total = collect(masks["rest"][-1:])
    *flying["own"], total = lax.optimization_barrier((*flying["own"], total))
    finish("own")
    for s in range(1, bits):
        if s > 1:
            take("delta", s - 1)
        send("delta", s)
    send_home("own")

    total = total + terms[0] + collect(masks["rest"][:-1])
    total = total.astype(bf16)
    pieces = [total[0]] + [over_dp(total[mask], mask) for mask in range(1, n_dp)]
    done(total)
    take("delta", bits - 1)
    deltas = jnp.concatenate(ready["delta"], axis=1)
    grad_tokens = place_slices(me, pieces)
    return (grad_tokens, deltas)


def solution(mesh):
    placed = (
        P(("groups", "dp", "tensor"), None),
        P(("groups", "dp", "tensor"), None),
        P("dp", "tensor"),
        P("dp", "tensor"),
        P("tensor", "dp"),
        P("tensor"),
        P("tensor"),
        P("tensor"),
        P("tensor", None),
    )
    return jax.shard_map(
        body,
        mesh=mesh,
        in_specs=placed,
        out_specs=(P(("groups", "dp", "tensor"), None), P(("groups", "dp", "tensor"), None, None)),
        check_vma=False,
    )
```

```python
import functools

import jax
import jax.numpy as jnp
import numpy as np
from jax import lax
from jax.experimental import pallas as pl
from jax.experimental.pallas import tpu as pltpu
from jax.sharding import PartitionSpec as P

BLOCK = 128
CAP = 5
CONTRACT_LAST = (((1,), (1,)), ((), ()))
SMALL = pl.CostEstimate(flops=1, bytes_accessed=1, transcendentals=0)


def xor_perm(size, mask):
    return [(i, i ^ mask) for i in range(size)]


def z_perm(n_tensor, mask):
    return [(rank, rank ^ 2 * mask) for rank in range(n_tensor)]


def chunk_masks(n_z):
    low, high = tuple(range(n_z // 2)), tuple(range(n_z // 2, n_z))
    return {"own": low[:1], "near": low[1:], 0: low, 1: high, "rest": low[1:] + high}


def delta_kernel(n_dp, n_pieces, me_ref, kind_ref, ff_ref, col_ref, owner_ref, *refs):
    window_refs, refs = refs[:2], refs[2:]
    hidden_refs, grad_refs, refs = refs[:n_pieces], refs[n_pieces : 2 * n_pieces], refs[2 * n_pieces :]
    out_ref, grads_ref, tokens_ref, hidden_ref, gate_ref, up_ref, used_ref = refs
    me = me_ref[0]
    out_ref[...] = jnp.zeros_like(out_ref)
    for owner in range(n_dp):
        used_ref[owner] = 0

    start = 0
    _, chips, rows, _ = window_refs[0].shape
    for chip in range(chips):
        for window_ref in window_refs:
            grads_ref[start : start + rows] = window_ref[0, chip]
            tokens_ref[start : start + rows] = window_ref[1, chip]
            start += rows
    start, column = 0, 0
    for hidden_piece, grad_piece in zip(hidden_refs, grad_refs):
        rows, units = hidden_piece.shape
        place = (slice(start, start + rows), slice(column, column + units))
        hidden_ref[place] = hidden_piece[...]
        gate_ref[place] = grad_piece[0]
        up_ref[place] = grad_piece[1]
        column += units
        if column == hidden_ref.shape[1]:
            start, column = start + rows, 0

    def step(entry, carry):
        owner = owner_ref[entry]
        slot = used_ref[owner]
        used_ref[owner] = slot + 1
        kind = kind_ref[entry]
        units = pl.ds(pl.multiple_of(ff_ref[entry] * BLOCK, BLOCK), BLOCK)
        columns = pl.ds(pl.multiple_of(col_ref[entry] * BLOCK, BLOCK), BLOCK)
        left = jnp.where(kind == 2, hidden_ref[:, units], tokens_ref[:, columns])
        right = jnp.where(
            kind == 0,
            gate_ref[:, units],
            jnp.where(kind == 1, up_ref[:, units], grads_ref[:, columns]),
        )
        out_ref[(owner ^ me) * CAP + slot] = lax.dot_general(
            left, right, (((0,), (0,)), ((), ())), preferred_element_type=jnp.float32
        )
        return carry

    lax.fori_loop(0, kind_ref.shape[0], step, 0)


def window_deltas(n_dp, units, me, kind, ff, col, owner, windows, hiddens, grads):
    _, chips, rows, features = windows[0].shape
    total = 2 * chips * rows
    if rows % 16:
        joined = jnp.stack(windows, axis=2).reshape(2, 1, total, features)
        windows = [joined[:, :, : total // 2], joined[:, :, total // 2 :]]
        across = units // hiddens[0].shape[1]
        groups = range(0, len(hiddens), across)
        hiddens = [
            jnp.concatenate([jnp.concatenate(hiddens[i : i + across], axis=1) for i in groups])
        ]
        grads = [
            jnp.concatenate([jnp.concatenate(grads[i : i + across], axis=2) for i in groups], axis=1)
        ]
    smem, vmem = pl.BlockSpec(memory_space=pltpu.SMEM), pl.BlockSpec(memory_space=pltpu.VMEM)
    bf16 = jnp.bfloat16
    return pl.pallas_call(
        functools.partial(delta_kernel, n_dp, len(hiddens)),
        out_shape=jax.ShapeDtypeStruct((n_dp * CAP, BLOCK, BLOCK), jnp.float32),
        in_specs=[smem] * 5 + [vmem] * (2 + 2 * len(hiddens)),
        out_specs=vmem,
        scratch_shapes=[
            pltpu.VMEM((total, features), bf16),
            pltpu.VMEM((total, features), bf16),
            pltpu.VMEM((total, units), bf16),
            pltpu.VMEM((total, units), bf16),
            pltpu.VMEM((total, units), bf16),
            pltpu.SMEM((n_dp,), jnp.int32),
        ],
        compiler_params=pltpu.CompilerParams(vmem_limit_bytes=24 << 20),
        cost_estimate=SMALL,
    )(me.reshape(1), kind, ff, col, owner, *windows, *hiddens, *grads)


def load_kernel(*refs):
    n = (len(refs) - 1) // 2
    copies = [
        pltpu.make_async_copy(source, target, refs[-1].at[i])
        for i, (source, target) in enumerate(zip(refs[:n], refs[n : 2 * n]))
    ]
    for copy in copies:
        copy.start()
    for copy in copies:
        copy.wait()


def in_vmem(*weights):
    return pl.pallas_call(
        load_kernel,
        out_shape=[pltpu.VMEM(w.shape, w.dtype) for w in weights],
        in_specs=[pl.BlockSpec(memory_space=pl.ANY)] * len(weights),
        out_specs=[pl.BlockSpec(memory_space=pltpu.VMEM)] * len(weights),
        scratch_shapes=[pltpu.SemaphoreType.DMA((len(weights),))],
        compiler_params=pltpu.CompilerParams(vmem_limit_bytes=1 << 20),
        cost_estimate=SMALL,
    )(*[pltpu.with_memory_space_constraint(w, pltpu.HBM) for w in weights])


def forward_kernel(bits, load, own_ref, other_ref, gate_ref, up_ref, down_ref, *refs):
    if load:
        *out_refs, held_ref, chunk_ref, sem = refs
        copy = pltpu.make_async_copy(down_ref, held_ref, sem)
        copy.start()
        down_ref = held_ref
    else:
        *out_refs, chunk_ref = refs
    f32 = jnp.float32
    chips, _, windows, rows, _ = own_ref.shape
    start = 0
    for window in range(windows):
        for chip in range(chips):
            for ref in (own_ref, other_ref):
                chunk_ref[:, start : start + rows] = ref[chip, :, window]
                start += rows
    count = start // windows
    grads, tokens = chunk_ref[0], chunk_ref[1]
    part = out_refs[0].shape[3]
    block = min(part, 512)
    for i in range(3):
        if load and i == 2:
            copy.wait()
        for q, bit in enumerate(bits):
            for column in range(0, part, block):
                units = slice(q * part + column, q * part + column + block)
                if i < 2:
                    weight = (gate_ref, up_ref)[i][:, units]
                    product = jnp.dot(tokens, weight, preferred_element_type=f32)
                else:
                    product = lax.dot_general(
                        grads, down_ref[units, :], CONTRACT_LAST, preferred_element_type=f32
                    )
                product = product.astype(chunk_ref.dtype)
                places = [0, 0]
                for window in range(windows):
                    sent = window >> bit & 1
                    out_refs[2 * q + sent][i, places[sent], :, column : column + block] = product[
                        window * count : (window + 1) * count
                    ]
                    places[sent] += 1


def forward_partials(bits, load, own, other, gate_weight, up_weight, down_weight):
    chips, _, windows, rows, width = own.shape
    count = 2 * chips * rows
    part = gate_weight.shape[1] // len(bits)
    vmem = pl.BlockSpec(memory_space=pltpu.VMEM)
    shape = jax.ShapeDtypeStruct((3, windows // 2, count, part), own.dtype)
    n = 2 * len(bits)
    loaded = [pltpu.VMEM(down_weight.shape, down_weight.dtype)] * load
    if load:
        down_weight = pltpu.with_memory_space_constraint(down_weight, pltpu.HBM)
    outs = pl.pallas_call(
        functools.partial(forward_kernel, bits, load),
        out_shape=[shape] * n + loaded,
        in_specs=[vmem] * 4 + [pl.BlockSpec(memory_space=pl.ANY) if load else vmem],
        out_specs=[vmem] * (n + len(loaded)),
        scratch_shapes=[pltpu.VMEM((2, windows * count, width), own.dtype)]
        + [pltpu.SemaphoreType.DMA(())] * load,
        compiler_params=pltpu.CompilerParams(vmem_limit_bytes=16 << 20),
        cost_estimate=SMALL,
    )(own, other, gate_weight, up_weight, down_weight)
    return outs[:n:2], outs[1:n:2], outs[n:]


def backward_kernel(places, *refs):
    f32 = jnp.float32
    n = len(places)
    piece_refs, (gate_ref, up_ref, out_ref, grads_ref) = refs[:n], refs[n:]
    for piece_ref, (starts, column) in zip(piece_refs, places):
        _, _, rows, columns = piece_ref.shape
        for index, start in enumerate(starts):
            place = (slice(None), slice(start, start + rows), slice(column, column + columns))
            grads_ref[place] = piece_ref[index]
    width = out_ref.shape[1]
    block = min(width, 256)
    for column in range(0, width, block):
        cut = slice(column, column + block)
        first = lax.dot_general(
            grads_ref[0], gate_ref[cut, :], CONTRACT_LAST, preferred_element_type=f32
        )
        second = lax.dot_general(
            grads_ref[1], up_ref[cut, :], CONTRACT_LAST, preferred_element_type=f32
        )
        out_ref[:, cut] = first + second


def backward_partials(pieces, places, gate_weight, up_weight):
    width, units = gate_weight.shape
    total = max(start for starts, _ in places for start in starts) + pieces[0].shape[2]
    vmem = pl.BlockSpec(memory_space=pltpu.VMEM)
    return pl.pallas_call(
        functools.partial(backward_kernel, places),
        out_shape=jax.ShapeDtypeStruct((total, width), jnp.float32),
        in_specs=[vmem] * (len(pieces) + 2),
        out_specs=vmem,
        scratch_shapes=[pltpu.VMEM((2, total, units), jnp.bfloat16)],
        compiler_params=pltpu.CompilerParams(vmem_limit_bytes=16 << 20),
        cost_estimate=SMALL,
    )(*pieces, gate_weight, up_weight)


def place_kernel(me_ref, *refs):
    piece_refs, out_ref = refs[:-1], refs[-1]
    width = piece_refs[0].shape[1]
    for mask, piece_ref in enumerate(piece_refs):
        start = pl.multiple_of((me_ref[0] ^ mask) * width, BLOCK)
        out_ref[:, pl.ds(start, width)] = piece_ref[...]


def place_slices(me, pieces):
    smem, vmem = pl.BlockSpec(memory_space=pltpu.SMEM), pl.BlockSpec(memory_space=pltpu.VMEM)
    rows, width = pieces[0].shape
    return pl.pallas_call(
        place_kernel,
        out_shape=jax.ShapeDtypeStruct((rows, width * len(pieces)), pieces[0].dtype),
        in_specs=[smem] + [vmem] * len(pieces),
        out_specs=vmem,
        compiler_params=pltpu.CompilerParams(vmem_limit_bytes=4 << 20),
        cost_estimate=SMALL,
    )(me.reshape(1), *pieces)


def body(
    tokens,
    grad_out,
    gate_weight,
    up_weight,
    down_weight,
    block_kind,
    block_ff,
    block_d,
    block_owner,
):
    n_dp, n_tensor = lax.axis_size("dp"), lax.axis_size("tensor")
    n_z = n_tensor // 2
    bits = n_dp.bit_length() - 1
    rows, features = tokens.shape
    width, units = gate_weight.shape
    me = lax.axis_index("dp")
    bf16, f32 = jnp.bfloat16, jnp.float32
    parts = min(bits, 2)
    part = units // parts
    orders = [[(q + s) % bits for s in range(bits)] for q in range(parts)]
    masks = chunk_masks(n_z)
    stages = 2 * bits

    chain = []

    def ordered(*values):
        if not chain:
            return values
        return lax.optimization_barrier(values + tuple(chain))[: len(values)]

    def done(*results):
        chain[:] = results

    def over_dp(value, mask):
        return lax.ppermute(value, "dp", xor_perm(n_dp, mask))

    def over_core(value):
        return lax.ppermute(value, "tensor", xor_perm(n_tensor, 1))

    def over_z(value, mask):
        return lax.ppermute(value, "tensor", z_perm(n_tensor, mask))

    held, window_held, shards, other = {}, {}, {}, {}
    down_held = [down_weight]
    ready, flying, local, owns, out_flying, terms = {}, {}, {}, {}, {}, {}

    def hop(held, mask):
        low = mask & -mask
        held[mask] = over_z(held[mask ^ low], low)

    def relay(held, mask):
        (held[mask],) = ordered(held[mask])
        low = mask & -mask if mask else n_z
        for step in range(low.bit_length() - 1):
            hop(held, mask | 1 << step)
        chain.append(held[mask])

    def swap(k):
        got = ordered(*[held[mask] for mask in masks[k]])
        shards[k] = jnp.stack(got)
        other[k] = over_core(shards[k])
        done(shards[k])

    pieces = []
    for mask in range(n_dp):
        start = (me ^ mask) * width
        piece = jnp.stack(
            [lax.dynamic_slice_in_dim(x, start, width, axis=1) for x in (grad_out, tokens)]
        )
        pieces.append(over_dp(piece, mask) if mask else piece)
    if rows % 16 == 0:
        gate_weight, up_weight = in_vmem(gate_weight, up_weight)
        done(gate_weight, up_weight)
    held[0] = jnp.stack(ordered(*pieces), axis=1)
    for step in range(n_z.bit_length() - 1):
        hop(held, 1 << step)

    def forward(k):
        own, others = ordered(shards[k], other[k])
        weights = (gate_weight, up_weight, *down_held[-1:])
        if rows % 16 == 0:
            first = [order[0] for order in orders]
            keep, fly, loaded = forward_partials(first, k == "own", own, others, *weights)
            shape = (3,) + (2,) * (bits - 1) + (-1, part)
            local[k] = [x.reshape(shape) for x in keep]
            ready[k] = [x.reshape(shape) for x in fly]
            done(*local[k], *ready[k])
            down_held.extend(loaded)
            return
        chunk = jnp.stack([own, others], axis=3).transpose(1, 2, 0, 3, 4, 5)
        chunk = chunk.reshape(2, -1, width)
        gate = jnp.dot(chunk[1], gate_weight, preferred_element_type=f32).astype(bf16)
        upward = jnp.dot(chunk[1], up_weight, preferred_element_type=f32).astype(bf16)
        hidden_grad = lax.dot_general(
            chunk[0], down_weight, CONTRACT_LAST, preferred_element_type=f32
        ).astype(bf16)
        sums = jnp.stack([gate, upward, hidden_grad])
        values = []
        for q in range(parts):
            value = sums[:, :, q * part : (q + 1) * part]
            values.append(value.reshape((3,) + (2,) * bits + (-1, part)))
        ready[k] = values
        done(*values)

    def add_halves(keep, fly):
        got = ordered(*fly)
        return [x.astype(f32) + y.astype(f32) for x, y in zip(keep, got)]

    def gradients(sums):
        hiddens, values = [], []
        for g, u, h in sums:
            sig = jax.nn.sigmoid(g)
            silu = g * sig
            hiddens.append((silu * u).astype(bf16))
            gate_grad = (h * u * sig * (1.0 + g * (1.0 - sig))).astype(bf16)
            up_grad = (h * silu).astype(bf16)
            values.append(jnp.stack([gate_grad, up_grad]))
        return hiddens, values

    def join(values, got, s):
        joined = []
        for value, more, order in zip(values, got, orders):
            order = order[::-1]
            axis = sum(1 for bit in order[:s] if bit > order[s])
            joined.append(jnp.stack([value, more], axis=axis))
        return joined

    def send(k, s):
        values = ordered(*ready[k])
        if s >= bits:
            local[k] = values
            flying[k] = [
                over_dp(value, 1 << order[::-1][s - bits]) for value, order in zip(values, orders)
            ]
            return
        if k != "delta" and s == 0 and rows % 16 == 0:
            flying[k] = [over_dp(x, 1 << order[s]) for x, order in zip(values, orders)]
            return
        local[k], fly = [], []
        for value, order in zip(values, orders):
            axis = (k != "delta") + sorted(order[s:], reverse=True).index(order[s])
            local[k].append(lax.index_in_dim(value, 0, axis, keepdims=False))
            fly.append(lax.index_in_dim(value, 1, axis, keepdims=False).astype(bf16))
        flying[k] = [over_dp(x, 1 << order[s]) for x, order in zip(fly, orders)]

    def take(k, s):
        if s < bits:
            values = add_halves(local[k], flying[k])
            if k == "delta":
                ready[k] = values
                done(*values)
                return
        else:
            values = join(local[k], ordered(*flying[k]), s - bits)
        if s == bits - 1:
            hiddens, values = gradients(values)
            owns[k] = (hiddens, values)
            done(*hiddens, *values)
        else:
            done(*values)
        ready[k] = values

    def merge():
        ready[0] = [
            jnp.concatenate(values, axis=-2) for values in zip(ready["own"], ready["near"])
        ]
        done(*ready[0])

    def part_again():
        count = 2 * rows
        ready["own"] = [x[..., :count, :] for x in ready[0]]
        ready["rest"] = [
            jnp.concatenate([x[..., count:, :], y], axis=-2) for x, y in zip(ready[0], ready[1])
        ]
        done(*ready["rest"])

    def finish(k):
        got = ordered(*flying[k])
        if rows % 16 == 0:
            count = 2 * len(masks[k]) * rows
            pieces, places = [], []
            for q in range(parts):
                order = orders[q][::-1]
                known = sorted(order[:-1], reverse=True)
                windows = [
                    sum(bit << at for bit, at in zip(index, known))
                    for index in np.ndindex((2,) * (bits - 1))
                ]
                for here, piece in enumerate((local[k][q], got[q])):
                    pieces.append(piece.reshape(-1, 2, count, part))
                    starts = [(window | here << order[-1]) * count for window in windows]
                    places.append((tuple(starts), q * part))
            out = backward_partials(pieces, tuple(places), gate_weight, up_weight)
        else:
            gathered = []
            for value in join(local[k], got, bits - 1):
                value = value.reshape((n_dp, 2, -1, part))
                gathered.append(jnp.swapaxes(value, 0, 1).reshape(2, -1, part))
            gathered = jnp.concatenate(gathered, axis=2)
            out = sum(
                lax.dot_general(x, w, CONTRACT_LAST, preferred_element_type=f32)
                for x, w in zip(gathered, (gate_weight, up_weight))
            )
        out = out.reshape(n_dp, len(masks[k]), 2, rows, width)
        send = out[:, :, 1].astype(bf16)
        out_flying[k] = (out[:, :, 0], over_core(send))
        done(send)

    def send_home(k):
        own, got = out_flying[k]
        (got,) = ordered(got)
        out = own + got.astype(f32)
        for place, mask in enumerate(masks[k]):
            term = out[:, place]
            if mask:
                term = term.astype(bf16)
                terms[mask] = over_z(term, mask)
            else:
                terms[mask] = term
            done(term)

    def collect(sources):
        total = 0.0
        for term in ordered(*[terms[mask] for mask in sources]):
            total = total + term.astype(f32)
        done(total)
        return total

    def window_rows(step):
        if step == 0:
            window_held[0] = jnp.stack(ordered(grad_out, tokens))
        else:
            places = list(window_held)
            window_held.update(zip(places, ordered(*[window_held[place] for place in places])))
            chain.append(window_held[places[-1]])
        if step < levels:
            for mask in range(n_z):
                if mask.bit_count() == step + 1:
                    hop(window_held, mask)
            return
        rows_there = [window_held[mask] for k in range(2) for mask in masks[k]]
        window_held["own"] = jnp.stack(rows_there, axis=1)
        window_held["other"] = over_core(window_held["own"])
        done(window_held["own"])

    def delta_terms():
        windows = ordered(window_held["own"], window_held["other"])
        chunks = range(2)
        deltas = window_deltas(
            n_dp,
            units,
            me,
            block_kind,
            block_ff,
            block_d,
            block_owner[:, 0],
            list(windows),
            [piece for k in chunks for piece in owns[k][0]],
            [piece for k in chunks for piece in owns[k][1]],
        )
        done(deltas)
        deltas = deltas.reshape((2,) * bits + (CAP, BLOCK, BLOCK))
        cut = BLOCK // parts
        ready["delta"] = [deltas[..., q * cut : (q + 1) * cut, :] for q in range(parts)]

    swap("own")
    forward("own")
    send("own", 0)
    for mask in masks["near"][1::2]:
        relay(held, mask)
    swap("near")
    forward("near")
    send("near", 0)
    take("own", 0)
    for mask in masks[1][::2]:
        relay(held, mask)
    take("near", 0)
    merge()
    for s in range(1, stages - 1):
        send(0, s)
        if s == stages - 2:
            swap(1)
            forward(1)
            send(1, 0)
        take(0, s)
    levels = n_z.bit_length() - 1
    window_rows(0)
    window_rows(1)
    for s in range(1, stages - 2):
        take(1, s - 1)
        send(1, s)
    for step in range(2, levels + 1):
        window_rows(step)
    take(1, stages - 3)
    send(1, stages - 2)
    delta_terms()
    send("delta", 0)
    take(1, stages - 2)
    part_again()
    send("rest", stages - 1)
    take("delta", 0)
    send("own", stages - 1)
    finish("rest")
    send_home("rest")
    total = collect(masks["rest"][:1])
    *flying["own"], total = lax.optimization_barrier((*flying["own"], total))
    finish("own")
    for s in range(1, bits):
        if s > 1:
            take("delta", s - 1)
        send("delta", s)
    send_home("own")

    total = total + terms[0] + collect(masks["rest"][1:])
    total = total.astype(bf16)
    pieces = [total[0]] + [over_dp(total[mask], mask) for mask in range(1, n_dp)]
    done(total)
    take("delta", bits - 1)
    deltas = jnp.concatenate(ready["delta"], axis=1)
    grad_tokens = place_slices(me, pieces)
    return (grad_tokens, deltas)


def solution(mesh):
    placed = (
        P(("groups", "dp", "tensor"), None),
        P(("groups", "dp", "tensor"), None),
        P("dp", "tensor"),
        P("dp", "tensor"),
        P("tensor", "dp"),
        P("tensor"),
        P("tensor"),
        P("tensor"),
        P("tensor", None),
    )
    return jax.shard_map(
        body,
        mesh=mesh,
        in_specs=placed,
        out_specs=(P(("groups", "dp", "tensor"), None), P(("groups", "dp", "tensor"), None, None)),
        check_vma=False,
    )
```

```python
import functools

import jax
import jax.numpy as jnp
import numpy as np
from jax import lax
from jax.experimental import pallas as pl
from jax.experimental.pallas import tpu as pltpu
from jax.sharding import PartitionSpec as P

BLOCK = 128
CAP = 5
CONTRACT_LAST = (((1,), (1,)), ((), ()))
SMALL = pl.CostEstimate(flops=1, bytes_accessed=1, transcendentals=0)


def xor_perm(size, mask):
    return [(i, i ^ mask) for i in range(size)]


def z_perm(n_tensor, mask):
    return [(rank, rank ^ 2 * mask) for rank in range(n_tensor)]


def chunk_masks(n_z):
    low, high = tuple(range(n_z // 2)), tuple(range(n_z // 2, n_z))
    return {"own": low[:1], "near": low[1:], 0: low, 1: high, "rest": low[1:] + high}


def delta_kernel(n_dp, n_pieces, me_ref, kind_ref, ff_ref, col_ref, owner_ref, *refs):
    window_refs, refs = refs[:2], refs[2:]
    hidden_refs, grad_refs, refs = refs[:n_pieces], refs[n_pieces : 2 * n_pieces], refs[2 * n_pieces :]
    out_ref, grads_ref, tokens_ref, hidden_ref, gate_ref, up_ref, used_ref = refs
    me = me_ref[0]
    out_ref[...] = jnp.zeros_like(out_ref)
    for owner in range(n_dp):
        used_ref[owner] = 0

    start = 0
    _, chips, rows, _ = window_refs[0].shape
    for chip in range(chips):
        for window_ref in window_refs:
            grads_ref[start : start + rows] = window_ref[0, chip]
            tokens_ref[start : start + rows] = window_ref[1, chip]
            start += rows
    start, column = 0, 0
    for hidden_piece, grad_piece in zip(hidden_refs, grad_refs):
        rows, units = hidden_piece.shape
        place = (slice(start, start + rows), slice(column, column + units))
        hidden_ref[place] = hidden_piece[...]
        gate_ref[place] = grad_piece[0]
        up_ref[place] = grad_piece[1]
        column += units
        if column == hidden_ref.shape[1]:
            start, column = start + rows, 0

    def step(entry, carry):
        owner = owner_ref[entry]
        slot = used_ref[owner]
        used_ref[owner] = slot + 1
        kind = kind_ref[entry]
        units = pl.ds(pl.multiple_of(ff_ref[entry] * BLOCK, BLOCK), BLOCK)
        columns = pl.ds(pl.multiple_of(col_ref[entry] * BLOCK, BLOCK), BLOCK)
        left = jnp.where(kind == 2, hidden_ref[:, units], tokens_ref[:, columns])
        right = jnp.where(
            kind == 0,
            gate_ref[:, units],
            jnp.where(kind == 1, up_ref[:, units], grads_ref[:, columns]),
        )
        out_ref[(owner ^ me) * CAP + slot] = lax.dot_general(
            left, right, (((0,), (0,)), ((), ())), preferred_element_type=jnp.float32
        )
        return carry

    lax.fori_loop(0, kind_ref.shape[0], step, 0)


def window_deltas(n_dp, units, me, kind, ff, col, owner, windows, hiddens, grads):
    _, chips, rows, features = windows[0].shape
    total = 2 * chips * rows
    if rows % 16:
        joined = jnp.stack(windows, axis=2).reshape(2, 1, total, features)
        windows = [joined[:, :, : total // 2], joined[:, :, total // 2 :]]
        across = units // hiddens[0].shape[1]
        groups = range(0, len(hiddens), across)
        hiddens = [
            jnp.concatenate([jnp.concatenate(hiddens[i : i + across], axis=1) for i in groups])
        ]
        grads = [
            jnp.concatenate([jnp.concatenate(grads[i : i + across], axis=2) for i in groups], axis=1)
        ]
    smem, vmem = pl.BlockSpec(memory_space=pltpu.SMEM), pl.BlockSpec(memory_space=pltpu.VMEM)
    bf16 = jnp.bfloat16
    return pl.pallas_call(
        functools.partial(delta_kernel, n_dp, len(hiddens)),
        out_shape=jax.ShapeDtypeStruct((n_dp * CAP, BLOCK, BLOCK), jnp.float32),
        in_specs=[smem] * 5 + [vmem] * (2 + 2 * len(hiddens)),
        out_specs=vmem,
        scratch_shapes=[
            pltpu.VMEM((total, features), bf16),
            pltpu.VMEM((total, features), bf16),
            pltpu.VMEM((total, units), bf16),
            pltpu.VMEM((total, units), bf16),
            pltpu.VMEM((total, units), bf16),
            pltpu.SMEM((n_dp,), jnp.int32),
        ],
        compiler_params=pltpu.CompilerParams(vmem_limit_bytes=24 << 20),
        cost_estimate=SMALL,
    )(me.reshape(1), kind, ff, col, owner, *windows, *hiddens, *grads)


def load_kernel(*refs):
    n = (len(refs) - 1) // 2
    copies = []
    for i, (source, target) in enumerate(zip(refs[:n], refs[n : 2 * n])):
        rows = source.shape[0] // 4
        for j in range(4):
            cut = pl.ds(j * rows, rows)
            copies.append(pltpu.make_async_copy(source.at[cut], target.at[cut], refs[-1].at[i, j]))
    for copy in copies:
        copy.start()
    for copy in copies:
        copy.wait()


def in_vmem(*weights):
    return pl.pallas_call(
        load_kernel,
        out_shape=[pltpu.VMEM(w.shape, w.dtype) for w in weights],
        in_specs=[pl.BlockSpec(memory_space=pl.ANY)] * len(weights),
        out_specs=[pl.BlockSpec(memory_space=pltpu.VMEM)] * len(weights),
        scratch_shapes=[pltpu.SemaphoreType.DMA((len(weights), 4))],
        compiler_params=pltpu.CompilerParams(vmem_limit_bytes=1 << 20),
        cost_estimate=SMALL,
    )(*[pltpu.with_memory_space_constraint(w, pltpu.HBM) for w in weights])


def forward_kernel(bits, own_ref, other_ref, gate_ref, up_ref, down_ref, *refs):
    out_refs, chunk_ref = refs[:-1], refs[-1]
    f32 = jnp.float32
    chips, _, windows, rows, _ = own_ref.shape
    start = 0
    for window in range(windows):
        for chip in range(chips):
            for ref in (own_ref, other_ref):
                chunk_ref[:, start : start + rows] = ref[chip, :, window]
                start += rows
    count = start // windows
    grads, tokens = chunk_ref[0], chunk_ref[1]
    part = out_refs[0].shape[3]
    block = min(part, 512)
    for q, bit in enumerate(bits):
        for column in range(0, part, block):
            units = slice(q * part + column, q * part + column + block)
            products = (
                jnp.dot(tokens, gate_ref[:, units], preferred_element_type=f32),
                jnp.dot(tokens, up_ref[:, units], preferred_element_type=f32),
                lax.dot_general(
                    grads, down_ref[units, :], CONTRACT_LAST, preferred_element_type=f32
                ),
            )
            for i, product in enumerate(products):
                product = product.astype(chunk_ref.dtype)
                places = [0, 0]
                for window in range(windows):
                    sent = window >> bit & 1
                    out_refs[2 * q + sent][i, places[sent], :, column : column + block] = product[
                        window * count : (window + 1) * count
                    ]
                    places[sent] += 1


def forward_partials(bits, own, other, gate_weight, up_weight, down_weight):
    chips, _, windows, rows, width = own.shape
    count = 2 * chips * rows
    part = gate_weight.shape[1] // len(bits)
    vmem = pl.BlockSpec(memory_space=pltpu.VMEM)
    outs = pl.pallas_call(
        functools.partial(forward_kernel, bits),
        out_shape=[jax.ShapeDtypeStruct((3, windows // 2, count, part), own.dtype)] * 2 * len(bits),
        in_specs=[vmem] * 5,
        out_specs=[vmem] * 2 * len(bits),
        scratch_shapes=[pltpu.VMEM((2, windows * count, width), own.dtype)],
        compiler_params=pltpu.CompilerParams(vmem_limit_bytes=16 << 20),
        cost_estimate=SMALL,
    )(own, other, gate_weight, up_weight, down_weight)
    return outs[::2], outs[1::2]


def backward_kernel(places, *refs):
    f32 = jnp.float32
    n = len(places)
    piece_refs, (gate_ref, up_ref, out_ref, grads_ref) = refs[:n], refs[n:]
    for piece_ref, (starts, column) in zip(piece_refs, places):
        _, _, rows, columns = piece_ref.shape
        for index, start in enumerate(starts):
            place = (slice(None), slice(start, start + rows), slice(column, column + columns))
            grads_ref[place] = piece_ref[index]
    width = out_ref.shape[1]
    block = min(width, 256)
    for column in range(0, width, block):
        cut = slice(column, column + block)
        first = lax.dot_general(
            grads_ref[0], gate_ref[cut, :], CONTRACT_LAST, preferred_element_type=f32
        )
        second = lax.dot_general(
            grads_ref[1], up_ref[cut, :], CONTRACT_LAST, preferred_element_type=f32
        )
        out_ref[:, cut] = first + second


def backward_partials(pieces, places, gate_weight, up_weight):
    width, units = gate_weight.shape
    total = max(start for starts, _ in places for start in starts) + pieces[0].shape[2]
    vmem = pl.BlockSpec(memory_space=pltpu.VMEM)
    return pl.pallas_call(
        functools.partial(backward_kernel, places),
        out_shape=jax.ShapeDtypeStruct((total, width), jnp.float32),
        in_specs=[vmem] * (len(pieces) + 2),
        out_specs=vmem,
        scratch_shapes=[pltpu.VMEM((2, total, units), jnp.bfloat16)],
        compiler_params=pltpu.CompilerParams(vmem_limit_bytes=16 << 20),
        cost_estimate=SMALL,
    )(*pieces, gate_weight, up_weight)


def place_kernel(me_ref, *refs):
    piece_refs, out_ref = refs[:-1], refs[-1]
    width = piece_refs[0].shape[1]
    for mask, piece_ref in enumerate(piece_refs):
        start = pl.multiple_of((me_ref[0] ^ mask) * width, BLOCK)
        out_ref[:, pl.ds(start, width)] = piece_ref[...]


def place_slices(me, pieces):
    smem, vmem = pl.BlockSpec(memory_space=pltpu.SMEM), pl.BlockSpec(memory_space=pltpu.VMEM)
    rows, width = pieces[0].shape
    return pl.pallas_call(
        place_kernel,
        out_shape=jax.ShapeDtypeStruct((rows, width * len(pieces)), pieces[0].dtype),
        in_specs=[smem] + [vmem] * len(pieces),
        out_specs=vmem,
        compiler_params=pltpu.CompilerParams(vmem_limit_bytes=4 << 20),
        cost_estimate=SMALL,
    )(me.reshape(1), *pieces)


def body(
    tokens,
    grad_out,
    gate_weight,
    up_weight,
    down_weight,
    block_kind,
    block_ff,
    block_d,
    block_owner,
):
    n_dp, n_tensor = lax.axis_size("dp"), lax.axis_size("tensor")
    n_z = n_tensor // 2
    bits = n_dp.bit_length() - 1
    rows, features = tokens.shape
    width, units = gate_weight.shape
    me = lax.axis_index("dp")
    bf16, f32 = jnp.bfloat16, jnp.float32
    parts = min(bits, 2)
    part = units // parts
    orders = [[(q + s) % bits for s in range(bits)] for q in range(parts)]
    masks = chunk_masks(n_z)
    stages = 2 * bits

    chain = []

    def ordered(*values):
        if not chain:
            return values
        return lax.optimization_barrier(values + tuple(chain))[: len(values)]

    def done(*results):
        chain[:] = results

    def over_dp(value, mask):
        return lax.ppermute(value, "dp", xor_perm(n_dp, mask))

    def over_core(value):
        return lax.ppermute(value, "tensor", xor_perm(n_tensor, 1))

    def over_z(value, mask):
        return lax.ppermute(value, "tensor", z_perm(n_tensor, mask))

    held, window_held, shards, other = {}, {}, {}, {}
    ready, flying, local, owns, out_flying, terms = {}, {}, {}, {}, {}, {}

    def hop(held, mask):
        low = mask & -mask
        held[mask] = over_z(held[mask ^ low], low)

    def relay(held, mask):
        (held[mask],) = ordered(held[mask])
        low = mask & -mask if mask else n_z
        for step in range(low.bit_length() - 1):
            hop(held, mask | 1 << step)
        chain.append(held[mask])

    def swap(k):
        got = ordered(*[held[mask] for mask in masks[k]])
        shards[k] = jnp.stack(got)
        other[k] = over_core(shards[k])
        done(shards[k])

    pieces = []
    for mask in range(n_dp):
        start = (me ^ mask) * width
        piece = jnp.stack(
            [lax.dynamic_slice_in_dim(x, start, width, axis=1) for x in (grad_out, tokens)]
        )
        pieces.append(over_dp(piece, mask) if mask else piece)
    if rows % 16 == 0:
        gate_weight, up_weight, down_weight = in_vmem(gate_weight, up_weight, down_weight)
        done(gate_weight, up_weight, down_weight)
    held[0] = jnp.stack(ordered(*pieces), axis=1)
    for step in range(n_z.bit_length() - 1):
        hop(held, 1 << step)

    def forward(k):
        own, others = ordered(shards[k], other[k])
        weights = (gate_weight, up_weight, down_weight)
        if rows % 16 == 0:
            first = [order[0] for order in orders]
            keep, fly = forward_partials(first, own, others, *weights)
            shape = (3,) + (2,) * (bits - 1) + (-1, part)
            local[k] = [x.reshape(shape) for x in keep]
            ready[k] = [x.reshape(shape) for x in fly]
            done(*local[k], *ready[k])
            return
        chunk = jnp.stack([own, others], axis=3).transpose(1, 2, 0, 3, 4, 5)
        chunk = chunk.reshape(2, -1, width)
        gate = jnp.dot(chunk[1], gate_weight, preferred_element_type=f32).astype(bf16)
        upward = jnp.dot(chunk[1], up_weight, preferred_element_type=f32).astype(bf16)
        hidden_grad = lax.dot_general(
            chunk[0], down_weight, CONTRACT_LAST, preferred_element_type=f32
        ).astype(bf16)
        sums = jnp.stack([gate, upward, hidden_grad])
        values = []
        for q in range(parts):
            value = sums[:, :, q * part : (q + 1) * part]
            values.append(value.reshape((3,) + (2,) * bits + (-1, part)))
        ready[k] = values
        done(*values)

    def add_halves(keep, fly):
        got = ordered(*fly)
        return [x.astype(f32) + y.astype(f32) for x, y in zip(keep, got)]

    def gradients(sums):
        hiddens, values = [], []
        for g, u, h in sums:
            sig = jax.nn.sigmoid(g)
            silu = g * sig
            hiddens.append((silu * u).astype(bf16))
            gate_grad = (h * u * sig * (1.0 + g * (1.0 - sig))).astype(bf16)
            up_grad = (h * silu).astype(bf16)
            values.append(jnp.stack([gate_grad, up_grad]))
        return hiddens, values

    def join(values, got, s):
        joined = []
        for value, more, order in zip(values, got, orders):
            order = order[::-1]
            axis = sum(1 for bit in order[:s] if bit > order[s])
            joined.append(jnp.stack([value, more], axis=axis))
        return joined

    def send(k, s):
        values = ordered(*ready[k])
        if s >= bits:
            local[k] = values
            flying[k] = [
                over_dp(value, 1 << order[::-1][s - bits]) for value, order in zip(values, orders)
            ]
            return
        if k != "delta" and s == 0 and rows % 16 == 0:
            flying[k] = [over_dp(x, 1 << order[s]) for x, order in zip(values, orders)]
            return
        local[k], fly = [], []
        for value, order in zip(values, orders):
            axis = (k != "delta") + sorted(order[s:], reverse=True).index(order[s])
            local[k].append(lax.index_in_dim(value, 0, axis, keepdims=False))
            fly.append(lax.index_in_dim(value, 1, axis, keepdims=False).astype(bf16))
        flying[k] = [over_dp(x, 1 << order[s]) for x, order in zip(fly, orders)]

    def take(k, s):
        if s < bits:
            values = add_halves(local[k], flying[k])
            if k == "delta":
                ready[k] = values
                done(*values)
                return
        else:
            values = join(local[k], ordered(*flying[k]), s - bits)
        if s == bits - 1:
            hiddens, values = gradients(values)
            owns[k] = (hiddens, values)
            done(*hiddens, *values)
        else:
            done(*values)
        ready[k] = values

    def merge():
        ready[0] = [
            jnp.concatenate(values, axis=-2) for values in zip(ready["own"], ready["near"])
        ]
        done(*ready[0])

    def part_again():
        count = 2 * rows
        ready["own"] = [x[..., :count, :] for x in ready[0]]
        ready["rest"] = [
            jnp.concatenate([x[..., count:, :], y], axis=-2) for x, y in zip(ready[0], ready[1])
        ]
        done(*ready["rest"])

    def finish(k):
        got = ordered(*flying[k])
        if rows % 16 == 0:
            count = 2 * len(masks[k]) * rows
            pieces, places = [], []
            for q in range(parts):
                order = orders[q][::-1]
                known = sorted(order[:-1], reverse=True)
                windows = [
                    sum(bit << at for bit, at in zip(index, known))
                    for index in np.ndindex((2,) * (bits - 1))
                ]
                for here, piece in enumerate((local[k][q], got[q])):
                    pieces.append(piece.reshape(-1, 2, count, part))
                    starts = [(window | here << order[-1]) * count for window in windows]
                    places.append((tuple(starts), q * part))
            out = backward_partials(pieces, tuple(places), gate_weight, up_weight)
        else:
            gathered = []
            for value in join(local[k], got, bits - 1):
                value = value.reshape((n_dp, 2, -1, part))
                gathered.append(jnp.swapaxes(value, 0, 1).reshape(2, -1, part))
            gathered = jnp.concatenate(gathered, axis=2)
            out = sum(
                lax.dot_general(x, w, CONTRACT_LAST, preferred_element_type=f32)
                for x, w in zip(gathered, (gate_weight, up_weight))
            )
        out = out.reshape(n_dp, len(masks[k]), 2, rows, width)
        send = out[:, :, 1].astype(bf16)
        out_flying[k] = (out[:, :, 0], over_core(send))
        done(send)

    def send_home(k):
        own, got = out_flying[k]
        (got,) = ordered(got)
        out = own + got.astype(f32)
        for place, mask in enumerate(masks[k]):
            term = out[:, place]
            if mask:
                term = term.astype(bf16)
                terms[mask] = over_z(term, mask)
            else:
                terms[mask] = term
            done(term)

    def collect(sources):
        total = 0.0
        for term in ordered(*[terms[mask] for mask in sources]):
            total = total + term.astype(f32)
        done(total)
        return total

    def window_rows(step):
        if step == 0:
            window_held[0] = jnp.stack(ordered(grad_out, tokens))
        else:
            places = list(window_held)
            window_held.update(zip(places, ordered(*[window_held[place] for place in places])))
            chain.append(window_held[places[-1]])
        if step < levels:
            for mask in range(n_z):
                if mask.bit_count() == step + 1:
                    hop(window_held, mask)
            return
        rows_there = [window_held[mask] for k in range(2) for mask in masks[k]]
        window_held["own"] = jnp.stack(rows_there, axis=1)
        window_held["other"] = over_core(window_held["own"])
        done(window_held["own"])

    def delta_terms():
        windows = ordered(window_held["own"], window_held["other"])
        chunks = range(2)
        deltas = window_deltas(
            n_dp,
            units,
            me,
            block_kind,
            block_ff,
            block_d,
            block_owner[:, 0],
            list(windows),
            [piece for k in chunks for piece in owns[k][0]],
            [piece for k in chunks for piece in owns[k][1]],
        )
        done(deltas)
        deltas = deltas.reshape((2,) * bits + (CAP, BLOCK, BLOCK))
        cut = BLOCK // parts
        ready["delta"] = [deltas[..., q * cut : (q + 1) * cut, :] for q in range(parts)]

    swap("own")
    forward("own")
    send("own", 0)
    for mask in masks["near"][1::2]:
        relay(held, mask)
    swap("near")
    forward("near")
    send("near", 0)
    take("own", 0)
    for mask in masks[1][::2]:
        relay(held, mask)
    take("near", 0)
    merge()
    for s in range(1, stages - 1):
        send(0, s)
        if s == stages - 2:
            swap(1)
            forward(1)
            send(1, 0)
        take(0, s)
    levels = n_z.bit_length() - 1
    window_rows(0)
    window_rows(1)
    for s in range(1, stages - 2):
        take(1, s - 1)
        send(1, s)
    for step in range(2, levels + 1):
        window_rows(step)
    take(1, stages - 3)
    send(1, stages - 2)
    delta_terms()
    send("delta", 0)
    take(1, stages - 2)
    part_again()
    send("rest", stages - 1)
    take("delta", 0)
    send("own", stages - 1)
    finish("rest")
    send_home("rest")
    total = collect(masks["rest"][:1])
    *flying["own"], total = lax.optimization_barrier((*flying["own"], total))
    finish("own")
    for s in range(1, bits):
        if s > 1:
            take("delta", s - 1)
        send("delta", s)
    send_home("own")

    total = total + terms[0] + collect(masks["rest"][1:])
    total = total.astype(bf16)
    pieces = [total[0]] + [over_dp(total[mask], mask) for mask in range(1, n_dp)]
    done(total)
    take("delta", bits - 1)
    deltas = jnp.concatenate(ready["delta"], axis=1)
    grad_tokens = place_slices(me, pieces)
    return (grad_tokens, deltas)


def solution(mesh):
    placed = (
        P(("groups", "dp", "tensor"), None),
        P(("groups", "dp", "tensor"), None),
        P("dp", "tensor"),
        P("dp", "tensor"),
        P("tensor", "dp"),
        P("tensor"),
        P("tensor"),
        P("tensor"),
        P("tensor", None),
    )
    return jax.shard_map(
        body,
        mesh=mesh,
        in_specs=placed,
        out_specs=(P(("groups", "dp", "tensor"), None), P(("groups", "dp", "tensor"), None, None)),
        check_vma=False,
    )
```
